32 devices in a mesh: dp: 4 (over y, x), seq: 8 (over z, core).
Axes of the slice: x: 2, y: 2, z: 4, core: 2. Of those that a mesh axis runs over, the one named last changes fastest.
Arguments:
- tokens: bfloat16 [2, 8192, 768], P(None, ('dp', 'seq')), may hold values from -6 to 6
- cotangent: bfloat16 [2, 8192, 768], P(None, ('dp', 'seq')), may hold values from -6 to 6
- lengths: int32 [2, 4, 16], P(None, 'dp'), may hold values from 0 to 512, as said below
- ln_gain: bfloat16 [768], P('seq'), may hold values from 0.5 to 1.5
- ln_bias: bfloat16 [768], P('seq'), may hold values from -3 to 3
- w_value: bfloat16 [768, 3072], P('seq'), may hold values from -0.21875 to 0.21875
- w_filter: bfloat16 [768, 1536], P('seq'), may hold values from -0.21875 to 0.21875
- w_fore: bfloat16 [1536, 3072], P('seq'), may hold values from -0.15625 to 0.15625
- w_back: bfloat16 [1536, 3072], P('seq'), may hold values from -0.15625 to 0.15625
- w_out: bfloat16 [3072, 768], P('seq'), may hold values from -0.21875 to 0.21875
- ssm_coef: float32 [2, 1536, 64], P(None, 'seq'), may hold values from -1 to 1
- ssm_rate: float32 [2, 1536, 64], P(None, 'seq'), may hold values from 0.001 to 0.12
- ssm_freq: float32 [2, 1536, 64], P(None, 'seq'), may hold values from 0 to 0.3
Outputs:
- mixed: bfloat16 [2, 8192, 768], P(None, ('dp', 'seq'))
- grad_tokens: bfloat16 [2, 8192, 768], P(None, ('dp', 'seq'))
- grad_gain: float32 [768], P('seq')
- grad_bias: float32 [768], P('seq')
- grad_value: float32 [768, 3072], P('seq')
- grad_filter: float32 [768, 1536], P('seq')
- grad_fore: float32 [1536, 3072], P('seq')
- grad_back: float32 [1536, 3072], P('seq')
- grad_out: float32 [3072, 768], P('seq')
- grad_coef: float32 [2, 1536, 64], P(None, 'seq')
- grad_rate: float32 [2, 1536, 64], P(None, 'seq')
- grad_freq: float32 [2, 1536, 64], P(None, 'seq')
The draws below stay inside these ranges and needn't reach their ends.
Inputs may be any that keep to these rules, and one draw needn't show every extreme that they name: For each micro-batch m and stream g, lengths[m, g] lists the items of the stream's 2048 tokens in order, each of 128 or 512 tokens, followed by zeros; the items fill the stream exactly, and each stream has items of both lengths.
All inputs are finite; a program needn't handle non-finite values.
Results may differ from the reference program's by a relative error of at most 0.0087.
Values may be sent and summed in bfloat16 or wider, within the bound.
A program may use at most 368 MiB of HBM per device.

```python
import math
import jax
import jax.numpy as jnp
from jax import lax

D = 768
FFN = 3072
FH = 1536
NS = 64
LONG = 512
MICRO = 2
SHORT = 128
STREAM = 2048
TOTAL = 8192
UNITS = 16


def draw_lengths(key, part):
    key = jax.random.fold_in(key, 11)
    slot_count = STREAM // LONG - 1
    unit_count = STREAM // SHORT
    stream_count = MICRO * (TOTAL // STREAM)
    stream_keys = jax.random.split(key, stream_count)

    def one_stream(stream_key):
        first_key, second_key, third_key = jax.random.split(stream_key, 3)
        leading = jax.random.randint(first_key, (), 1, 4)
        big_slot = jax.random.randint(second_key, (slot_count,), 0, 2)
        forced = jax.random.randint(third_key, (), 0, slot_count)
        big_slot = jnp.where(jnp.arange(slot_count) == forced, 1, big_slot)
        places = jnp.arange(unit_count).astype(jnp.int32)
        inner = places - leading
        slot_of = jnp.clip(inner // 4, 0, slot_count - 1)
        within = (inner >= 0) & (inner < 4 * slot_count)
        is_big = within & (big_slot[slot_of] == 1)
        at_head = inner % 4 == 0
        item_sizes = jnp.where(is_big, jnp.where(at_head, LONG, 0), SHORT).astype(jnp.int32)
        order = jnp.argsort((item_sizes == 0).astype(jnp.int32), stable=True)
        return item_sizes[order].astype(jnp.int32)
    return jax.vmap(one_stream)(stream_keys).reshape(MICRO, TOTAL // STREAM, unit_count).astype(jnp.int32)


def block_scale(key, extent, cuts, least, top_value):
    level, own = 1.0, jax.random.fold_in(key, 6)
    for position, parts in cuts:
        draws = jnp.exp(jax.random.uniform(jax.random.fold_in(own, position), (parts,), jnp.float32, least / len(cuts), top_value / len(cuts)))
        level = level * jnp.repeat(draws, extent[position] // parts).reshape([-1 if axis == position else 1 for axis in range(len(extent))])
    return level


def scatter_about(own_key, extent, deviation, most, cuts=(), kind=jnp.bfloat16):
    array = deviation * jax.random.normal(own_key, extent, jnp.float32)
    if cuts:
        array = array * block_scale(own_key, extent, cuts, -0.22, 0.18)
    return jnp.clip(array, -most, most).astype(kind)


def setup_inputs(seed: int = 0) -> dict:
    seeds = jax.random.split(jax.random.key(seed), 14)
    tokens = scatter_about(seeds[0], (MICRO, TOTAL, D), 1.0, 6.0, ((1, 32),))
    cotangent = scatter_about(seeds[1], (MICRO, TOTAL, D), 1.0, 6.0, ((1, 32),))
    lengths = draw_lengths(jax.random.fold_in(seeds[13], 71), 0)
    ln_gain = jnp.clip(1.0 + 0.1 * jax.random.normal(seeds[3], (D,), jnp.float32), 0.5, 1.5).astype(jnp.bfloat16)
    ln_bias = scatter_about(seeds[4], (D,), 0.3, 3.0, ((0, 8),))
    w_value = scatter_about(seeds[5], (D, FFN), D ** -0.5, 0.21875, ((0, 8),))
    w_filter = scatter_about(seeds[6], (D, FH), D ** -0.5, 0.21875, ((0, 8),))
    w_fore = scatter_about(seeds[7], (FH, FFN), FH ** -0.5, 0.15625, ((0, 8),))
    w_back = scatter_about(seeds[8], (FH, FFN), FH ** -0.5, 0.15625, ((0, 8),))
    w_out = scatter_about(seeds[9], (FFN, D), (FFN // 4) ** -0.5, 0.21875, ((0, 8),))
    ssm_coef = scatter_about(seeds[10], (2, FH, NS), (NS // 2) ** -0.5, 1.0, ((1, 8),), jnp.float32)
    ssm_rate = jnp.clip(jnp.exp(math.log(0.12) - 4.787492 * jax.random.uniform(seeds[11], (2, FH, NS), jnp.float32) ** block_scale(seeds[11], (2, FH, NS), ((1, 8),), -0.2, 0.2)), 0.001, 0.12)
    ssm_freq = jnp.clip(0.3 * jax.random.uniform(seeds[12], (2, FH, NS), jnp.float32) ** block_scale(seeds[12], (2, FH, NS), ((1, 8),), -0.2, 0.2), 0.0, 0.3)
    return dict(tokens=tokens, cotangent=cotangent, lengths=lengths, ln_gain=ln_gain, ln_bias=ln_bias, w_value=w_value, w_filter=w_filter, w_fore=w_fore, w_back=w_back, w_out=w_out, ssm_coef=ssm_coef, ssm_rate=ssm_rate, ssm_freq=ssm_freq)


@jax.custom_vjp
def low(v):
    return lax.optimization_barrier(v.astype(jnp.bfloat16)).astype(jnp.float32)

@jax.custom_vjp
def low_back(v):
    return v

def low_keep(v):
    return (low(v), None)

def low_pass(kept, grad):
    return (grad,)

def back_keep(v):
    return (v, None)

def back_low(kept, grad):
    return (low(grad),)
low.defvjp(low_keep, low_pass)
low_back.defvjp(back_keep, back_low)
EPSILON = 1e-05
HIGHEST = lax.Precision.HIGHEST

def matmul(left_side, right_side):
    return jnp.dot(left_side, right_side, precision=HIGHEST, preferred_element_type=jnp.float32)

def layer_norm(token_rows, gain_vec, bias_vec):
    centre = lax.optimization_barrier(jnp.mean(token_rows, axis=-1, keepdims=True))
    shifted = token_rows - centre
    spread = lax.optimization_barrier(jnp.mean(shifted * shifted, axis=-1, keepdims=True))
    return shifted * lax.rsqrt(spread + EPSILON) * gain_vec + bias_vec

def make_kernels(ssm_coef, ssm_rate, ssm_freq):
    lag_steps = jnp.arange(LONG).astype(jnp.float32)

    def one_side(weights, decays, angular):
        wave_terms = jnp.sqrt(decays)[:, :, None] * jnp.exp(-decays[:, :, None] * lag_steps) * jnp.cos(angular[:, :, None] * lag_steps)
        return jnp.einsum('cn,cnl->cl', weights, wave_terms, precision=HIGHEST)
    per_side = jax.checkpoint(one_side)
    return jnp.stack([per_side(ssm_coef[0], ssm_rate[0], ssm_freq[0]), per_side(ssm_coef[1], ssm_rate[1], ssm_freq[1])])

def item_index(positions, item_starts, item_sizes):
    present = (item_starts[None, :] <= positions[:, None]) & (item_sizes[None, :] > 0)
    return lax.optimization_barrier(jnp.sum(present.astype(jnp.int32), axis=1)).astype(jnp.int32) - 1

def item_convolve(signal, kernels, item_starts, item_sizes):
    stream_len, channels = signal.shape
    padded = jnp.concatenate([signal, jnp.zeros((LONG, channels), jnp.float32)], 0)
    offsets = jnp.arange(LONG).astype(jnp.int32)
    places = jnp.minimum(item_starts[:, None] + offsets[None, :], stream_len + LONG - 1).astype(jnp.int32)
    inside = offsets[None, :] < item_sizes[:, None]
    pieces = jnp.where(inside[:, :, None], padded[places], 0.0)
    spectrum = jnp.fft.rfft(pieces, n=2 * LONG, axis=1)
    responses = jnp.fft.rfft(kernels, n=2 * LONG, axis=2)
    forward_items = jnp.fft.irfft(spectrum * jnp.transpose(responses[0])[None], n=2 * LONG, axis=1)[:, :LONG]
    backward_items = jnp.fft.irfft(spectrum * jnp.conj(jnp.transpose(responses[1]))[None], n=2 * LONG, axis=1)[:, :LONG]
    positions = jnp.arange(stream_len).astype(jnp.int32)
    owner_item = item_index(positions, item_starts, item_sizes)
    flat_index = (owner_item * LONG + positions - item_starts[owner_item]).astype(jnp.int32)
    return (forward_items.reshape(-1, channels)[flat_index], backward_items.reshape(-1, channels)[flat_index])

def block_forward(token_rows, gain_vec, bias_vec, w_value, w_filter, w_fore, w_back, w_out, kernels, item_starts, item_sizes):
    normed = layer_norm(token_rows, gain_vec, bias_vec)
    normed_low = low(normed)
    pre_value = low_back(matmul(normed_low, w_value))
    pre_filter = low_back(matmul(normed_low, w_filter))
    value_act = jax.nn.gelu(pre_value)
    filter_low = low(low_back(jax.nn.gelu(pre_filter)))
    fore_conv, back_conv = item_convolve(filter_low, kernels, item_starts, item_sizes)
    fore_low = low(low_back(fore_conv))
    back_low_val = low(low_back(back_conv))
    proj_fore = low_back(matmul(fore_low, w_fore))
    proj_back = low_back(matmul(back_low_val, w_back))
    hidden_low = low(proj_fore * proj_back * value_act)
    return token_rows + matmul(hidden_low, w_out)

def reference(tokens, cotangent, lengths, ln_gain, ln_bias, w_value, w_filter, w_fore, w_back, w_out, ssm_coef, ssm_rate, ssm_freq):
    params = tuple((member.astype(jnp.float32) for member in (ln_gain, ln_bias, w_value, w_filter, w_fore, w_back, w_out)))
    kernels, kernel_pull = jax.vjp(make_kernels, ssm_coef, ssm_rate, ssm_freq)
    groups = TOTAL // STREAM
    streams = tokens.astype(jnp.float32).reshape(MICRO * groups, STREAM, D)
    cot_streams = cotangent.astype(jnp.float32).reshape(MICRO * groups, STREAM, D)
    all_sizes = lengths.reshape(MICRO * groups, UNITS).astype(jnp.int32)

    def one_stream(running, inputs):
        token_rows, stream_cot, item_sizes = inputs
        item_starts = (jnp.cumsum(item_sizes) - item_sizes).astype(jnp.int32)

        def closed(rows_in, param_set, kernel_set):
            return block_forward(rows_in, param_set[0], param_set[1], param_set[2], param_set[3], param_set[4], param_set[5], param_set[6], kernel_set, item_starts, item_sizes)
        result, pull_back = jax.vjp(closed, token_rows, params, kernels)
        grad_rows, grad_params, grad_kernels = pull_back(stream_cot)
        running = jax.tree.map(jnp.add, running, (grad_params, grad_kernels))
        return (running, (result.astype(jnp.bfloat16), grad_rows.astype(jnp.bfloat16)))
    start_sums = jax.tree.map(jnp.zeros_like, (params, kernels))
    totals, outputs = lax.scan(one_stream, start_sums, (streams, cot_streams, all_sizes))
    grad_params, grad_kernels = totals
    grad_coef, grad_rate, grad_freq = kernel_pull(grad_kernels)
    mixed = outputs[0].reshape(MICRO, TOTAL, D)
    grad_tokens = outputs[1].reshape(MICRO, TOTAL, D)
    return (mixed, grad_tokens, grad_params[0], grad_params[1], grad_params[2], grad_params[3], grad_params[4], grad_params[5], grad_params[6], grad_coef, grad_rate, grad_freq)
```

```python
import functools

import numpy as np

import jax
import jax.numpy as jnp
from jax import lax
from jax.experimental import pallas as pl
from jax.experimental.pallas import tpu as pltpu
from jax.sharding import PartitionSpec as P

MESH = pl.DeviceIdType.MESH
LONG = 512
EPSILON = 1e-05
HIGHEST = lax.Precision.HIGHEST
LOW = jnp.bfloat16
F32 = jnp.float32


BLK = 128
REACH = 3


def wave_tables():
    k = np.arange(BLK)[:, None] + 0.5
    n = np.arange(-BLK, BLK)[None, :]
    angle = 2 * np.pi * k * n / (2 * BLK)
    return np.concatenate([np.cos(angle), -np.sin(angle)], 0).astype(np.float32)


def dot(a, b, ca, cb):
    return lax.dot_general(a, b, (((ca,), (cb,)), ((), ())), preferred_element_type=jnp.float32)


def kernel_spectra(wave_ref, kern_ref, spec_ref, tile):
    for side in range(2):
        rows = jnp.concatenate([kern_ref[a, b, side] for a in range(kern_ref.shape[0]) for b in range(kern_ref.shape[1])], 0)
        spec_ref[side, 0] = dot(wave_ref[:, BLK:], rows[:, :BLK], 1, 1)
        for d in range(1, REACH + 1):
            spec_ref[side, d] = dot(wave_ref[...], rows[:, (d - 1) * BLK:(d + 1) * BLK], 1, 1)


def block_of(parts, micro, at):
    for p in parts:
        n = p.shape[1] // BLK
        if at < n:
            return p[micro, at * BLK:(at + 1) * BLK]
        at -= n


def fore_kernel(mask_ref, wave_ref, kern_ref, *refs):
    parts = refs[:5]
    fore_ref, back_ref, spec_ref, x_ref, y_ref = refs[5:]
    tile = fore_ref.shape[-1]
    kernel_spectra(wave_ref, kern_ref, spec_ref, tile)
    fwd = wave_ref[:, BLK:]
    for micro in range(2):
        for b in range(8):
            x_ref[b] = dot(fwd, block_of(parts, micro, b), 1, 0)

        @pl.loop(0, BLK // 8)
        def _(r):
            re = pl.ds(pl.multiple_of(r * 8, 8), 8)
            im = pl.ds(pl.multiple_of(r * 8 + BLK, 8), 8)
            for lane in range(tile // 128):
                ln = slice(lane * 128, lane * 128 + 128)
                xr = [x_ref[b, re, ln] for b in range(8)]
                xi = [x_ref[b, im, ln] for b in range(8)]
                for side in range(2):
                    cr = [spec_ref[side, d, re, ln] for d in range(4)]
                    ci = [spec_ref[side, d, im, ln] for d in range(4)]
                    for own in range(2):
                        yr = yi = None
                        for d in range(4):
                            at = own + 3 + (d if side else -d)
                            pr = cr[d] * xr[at]
                            pi = cr[d] * xi[at]
                            qr = ci[d] * xi[at]
                            qi = ci[d] * xr[at]
                            if side:
                                tr, ti = pr + qr, pi - qi
                            else:
                                tr, ti = pr - qr, pi + qi
                            if d:
                                m = mask_ref[(micro * 2 + own) * 7 + 3 + (d if side else -d)]
                                tr, ti = tr * m, ti * m
                            yr = tr if yr is None else yr + tr
                            yi = ti if yi is None else yi + ti
                        y_ref[side, own, re, ln] = yr
                        y_ref[side, own, im, ln] = yi
        for own in range(2):
            for side, o in ((0, fore_ref), (1, back_ref)):
                y = dot(fwd, y_ref[side, own].astype(jnp.bfloat16), 0, 0)
                o[micro, own * BLK:(own + 1) * BLK] = (y * (1.0 / BLK)).astype(jnp.bfloat16)


def back_kernel(mask_ref, wave_ref, kern_ref, *refs):
    parts = refs[:5]
    fparts = refs[5:8]
    bparts = refs[8:11]
    gfil_ref, gk_ref, spec_ref, x_ref, f_ref, b_ref, y_ref, r_ref = refs[11:]
    tile = gfil_ref.shape[-1]
    kernel_spectra(wave_ref, kern_ref, spec_ref, tile)
    fwd = wave_ref[:, BLK:]
    for micro in range(2):
        for b in range(8):
            x_ref[b] = dot(fwd, block_of(parts, micro, b), 1, 0)
        for b in range(5):
            f_ref[b] = dot(fwd, block_of(fparts, micro, b), 1, 0)
            b_ref[b] = dot(fwd, block_of(bparts, micro, b), 1, 0)

        @pl.loop(0, BLK // 8)
        def _(r):
            re = pl.ds(pl.multiple_of(r * 8, 8), 8)
            im = pl.ds(pl.multiple_of(r * 8 + BLK, 8), 8)
            for lane in range(tile // 128):
                ln = slice(lane * 128, lane * 128 + 128)
                fr = [f_ref[b, re, ln] for b in range(5)]
                fi = [f_ref[b, im, ln] for b in range(5)]
                gr = [b_ref[b, re, ln] for b in range(5)]
                gi = [b_ref[b, im, ln] for b in range(5)]
                acc = [[None, None], [None, None]]
                for d in range(4):
                    for side in range(2):
                        cr = spec_ref[side, d, re, ln]
                        ci = spec_ref[side, d, im, ln]
                        for own in range(2):
                            if side == 0:
                                vr, vi = fr[own + d], fi[own + d]
                                tr, ti = cr * vr + ci * vi, cr * vi - ci * vr
                                e = d
                            else:
                                vr, vi = gr[own + 3 - d], gi[own + 3 - d]
                                tr, ti = cr * vr - ci * vi, cr * vi + ci * vr
                                e = -d
                            if d:
                                m = mask_ref[(micro * 2 + own) * 7 + 3 + e]
                                tr, ti = tr * m, ti * m
                            a = acc[own]
                            acc[own] = [tr if a[0] is None else a[0] + tr, ti if a[1] is None else a[1] + ti]
                for own in range(2):
                    y_ref[own, re, ln] = acc[own][0]
                    y_ref[own, im, ln] = acc[own][1]
                for side in range(2):
                    for d in range(4):
                        sr = si = None
                        for own in range(2):
                            e = d if side else -d
                            xr, xi = x_ref[own + 3 + e, re, ln], x_ref[own + 3 + e, im, ln]
                            if side == 0:
                                vr, vi = fr[own], fi[own]
                                tr, ti = vr * xr + vi * xi, vi * xr - vr * xi
                            else:
                                vr, vi = gr[own + 3], gi[own + 3]
                                tr, ti = vr * xr + vi * xi, vr * xi - vi * xr
                            if d:
                                m = mask_ref[(micro * 2 + own) * 7 + 3 + e]
                                tr, ti = tr * m, ti * m
                            sr = tr if sr is None else sr + tr
                            si = ti if si is None else si + ti
                        if micro:
                            sr = sr + r_ref[side, d, re, ln]
                            si = si + r_ref[side, d, im, ln]
                        r_ref[side, d, re, ln] = sr
                        r_ref[side, d, im, ln] = si
        for own in range(2):
            y = dot(fwd, y_ref[own].astype(jnp.bfloat16), 0, 0)
            gfil_ref[micro, own * BLK:(own + 1) * BLK] = (y * (1.0 / BLK)).astype(jnp.bfloat16)
    A, B = gk_ref.shape[:2]
    for side in range(2):
        rows = [dot(r_ref[side, d].astype(jnp.bfloat16), wave_ref[:, BLK:] if d == 0 else wave_ref[...], 0, 0) for d in range(4)]
        for d in range(4):
            seg = rows[d][:, -BLK:]
            if d < 3:
                seg = seg + rows[d + 1][:, :BLK]
            seg = (seg * (1.0 / BLK)).astype(jnp.bfloat16)
            w = tile // (A * B)
            for a in range(A):
                for b in range(B):
                    at = (a * B + b) * w
                    gk_ref[a, b, side, :, d * BLK:(d + 1) * BLK] = seg[at:at + w]


def _specs(parts, tile):
    return [pl.BlockSpec((2, p.shape[1], tile), lambda i: (0, 0, i)) for p in parts]


def conv_call(body, mask, wave, kern, parts, outs, scratch, step):
    channels = parts[0].shape[-1]
    steps = kern.shape[0] // step
    tile = channels // steps
    kspec = pl.BlockSpec((step,) + kern.shape[1:], lambda i: (i, 0, 0, 0, 0))
    out_specs = []
    for o in outs:
        if len(o.shape) == 3:
            out_specs.append(pl.BlockSpec((2, o.shape[1], tile), lambda i: (0, 0, i)))
        else:
            out_specs.append(kspec)
    return pl.pallas_call(
        body,
        grid=(steps,),
        out_shape=outs,
        in_specs=[pl.BlockSpec(memory_space=pltpu.SMEM), pl.BlockSpec(memory_space=pltpu.VMEM), kspec] + _specs(parts, tile),
        out_specs=out_specs,
        scratch_shapes=[pltpu.VMEM(sh + (tile,), jnp.float32) for sh in scratch],
        compiler_params=pltpu.CompilerParams(vmem_limit_bytes=56 * 2**20),
        cost_estimate=pl.CostEstimate(flops=10**10, bytes_accessed=3 * 10**7, transcendentals=0),
    )(mask, wave, kern, *parts)


def conv_forward(mask, wave, kern, parts, step):
    own = parts[2]
    sh = jax.ShapeDtypeStruct(own.shape, jnp.bfloat16)
    return conv_call(fore_kernel, mask, wave, kern, parts, [sh, sh], [(2, 4, 256), (8, 256), (2, 2, 256)], step)


def conv_backward(mask, wave, kern, parts, fparts, bparts, step):
    own = parts[2]
    return conv_call(back_kernel, mask, wave, kern, list(parts) + list(fparts) + list(bparts),
                     [jax.ShapeDtypeStruct(own.shape, jnp.bfloat16), jax.ShapeDtypeStruct(kern.shape, jnp.bfloat16)],
                     [(2, 4, 256), (8, 256), (5, 256), (5, 256), (2, 256), (2, 4, 256)], step)


AHEAD = 1
L2 = 2
L3 = 4

def place(n_z):
    dp = lax.axis_index("dp"); s = lax.axis_index("seq")
    return dp, s, s // 2, lax.rem(s, 2)

def cut(ref, geom, q, h=None):
    kind = geom
    R, C = ref.shape[-2:]
    if kind == "col":
        cols = pl.ds(pl.multiple_of(q * (C // 4), 128), C // 4)
        rows = slice(None) if h is None else pl.ds(h * (R // 2), R // 2)
        return ref.at[rows, cols]
    if kind == "row":
        n = R // 4
        if h is None:
            return ref.at[pl.ds(pl.multiple_of(q * n, 16), n)]
        return ref.at[pl.ds(pl.multiple_of(q * n + h * (n // 2), 16), n // 2)]

GEOM = {"filter": "col", "kern": "row", "value": "col", "fore": "col", "back": "col", "out": "row"}

def ag_kernel(names, *refs):
    n = len(names)
    src = refs[:n]; out = refs[n:2 * n]
    stage = refs[2 * n:3 * n]
    isem, lsem, zs, zr, xs, xr, ys, yr, fxs, fxr, fys, fyr, ss, sr, ss0, sr0 = refs[3 * n:]
    dp, s, z, c = place(4)
    core = (dp, s + 1 - 2 * c)
    xn = (dp + 1 - 2 * lax.rem(dp, 2), s)
    yn = (lax.rem(dp + 2, 4), s)
    q = dp; qx = xn[0]; qy = yn[0]; qd = lax.rem(qx + 2, 4)
    def zdev(k): return (dp, lax.rem(s + 2 * k, 8))
    bar = pltpu.get_barrier_semaphore()
    for d in [core, xn, yn] + [zdev(k) for k in (1, 2, 3)]:
        pl.semaphore_signal(bar, inc=1, device_id=d, device_id_type=MESH)
    pl.semaphore_wait(bar, 6)

    def rc(a_ref, b_ref, s1, s2, dev):
        return pltpu.make_async_remote_copy(src_ref=a_ref, dst_ref=b_ref, send_sem=s1, recv_sem=s2, device_id=dev, device_id_type=MESH)
    g = [GEOM[m] for m in names]
    sends = []
    locs = []
    lins = []
    zsend = {}
    for a in range(n):
        if names[a] == "kern":
            lc = pltpu.make_async_copy(stage[a], cut(out[a].at[s], g[a], q), lsem.at[a])
        else:
            lc = pltpu.make_async_copy(stage[a], out[a].at[s], lsem.at[a])
        locs.append(lc)
        li = pltpu.make_async_copy(src[a], stage[a], isem.at[a]); li.start(); lins.append(li)
        for k in (1, 2, 3):
            piece = src[a] if names[a] == "kern" else cut(src[a], g[a], q)
            cp = rc(piece, cut(out[a].at[s], g[a], q), zs.at[a, k - 1], zr.at[a, k - 1], zdev(k))
            zsend[a, k] = cp
    def zgo(a):
        if a >= n: return
        for k in (1, 3, 2): zsend[a, k].start()
    def sibgo(a):
        if names[a] != "kern":
            cp = rc(src[a], out[a].at[s], ss0.at[a], sr0.at[a], core)
            cp.start(); sends.append(cp)
    for a in range(AHEAD): zgo(a)
    for a in range(n):
        lins[a].wait(); locs[a].start()
    sibgo(0)
    units = []
    for a in range(n):
        if names[a] == "kern": units.append((a, 0))
        for k in (1, 3, 2): units.append((a, k))
    xc, yc, fx, fy, sb = {}, {}, {}, {}, {}
    def blk(a, k):
        return out[a].at[lax.rem(s + 8 - 2 * k, 8)]
    def st1(u):
        a, k = u
        if k == 0:
            locs[a].wait()
        else:
            zsend[a, k].wait_recv()
        b = cut(blk(a, k), g[a], q)
        xc[u] = rc(b, b, xs.at[a, k], xr.at[a, k], xn); xc[u].start()
        yc[u] = rc(b, b, ys.at[a, k], yr.at[a, k], yn); yc[u].start()
    def st2(u):
        a, k = u
        xc[u].wait_recv()
        b = cut(blk(a, k), g[a], qx, 0)
        fy[u] = rc(b, b, fys.at[a, k], fyr.at[a, k], yn); fy[u].start()
        yc[u].wait_recv()
        b = cut(blk(a, k), g[a], qy, 1)
        fx[u] = rc(b, b, fxs.at[a, k], fxr.at[a, k], xn); fx[u].start()
    def st3(u):
        a, k = u
        fx[u].wait_recv(); fy[u].wait_recv()
        b = blk(a, k)
        sb[u] = rc(b, b, ss.at[a, k], sr.at[a, k], core); sb[u].start()
    for t in range(len(units) + L3):
        if t < len(units):
            st1(units[t])
            if units[t][1] == 2:
                zgo(units[t][0] + AHEAD)
                if units[t][0] + 1 < n: sibgo(units[t][0] + 1)
        if 0 <= t - L2 < len(units): st2(units[t - L2])
        if 0 <= t - L3 < len(units): st3(units[t - L3])
    for u in units:
        a, k = u
        sb[u].wait_recv()
        for d in (xc, yc, fx, fy, sb): d[u].wait_send()
    for cp in zsend.values(): cp.wait_send()
    for cp in sends: cp.wait()
    for a in range(n):
        if names[a] != "kern": locs[a].wait()

def gather_weights(names, arrs):
    n = len(names)
    shapes = []
    for m, a in zip(names, arrs):
        R, C = a.shape
        if m == "kern": R = R * 4
        shapes.append(jax.ShapeDtypeStruct((8, R, C), a.dtype))
    D = pltpu.SemaphoreType.DMA
    outs = pl.pallas_call(
        functools.partial(ag_kernel, names),
        out_shape=shapes,
        in_specs=[pl.BlockSpec(memory_space=pl.ANY)] * n,
        out_specs=[pl.BlockSpec(memory_space=pl.ANY)] * n,
        scratch_shapes=[pltpu.VMEM(a.shape, a.dtype) for a in arrs] + [D((n,)), D((n,)), D((n, 3)), D((n, 3))] + [D((n, 4))] * 10 + [D((n,)), D((n,))],
        compiler_params=pltpu.CompilerParams(collective_id=0, has_side_effects=True),
    )(*arrs)
    return outs


SLOTS = 3
LB, LC, LD, LE = 1, 2, 3, 4

def add_into(dst, srcs):
    R = dst.shape[-2]
    @pl.loop(0, R // 16)
    def _(r):
        rows = pl.ds(pl.multiple_of(r * 16, 16), 16)
        t = dst[rows, :].astype(jnp.float32)
        for s_ in srcs:
            t = t + s_[rows, :].astype(jnp.float32)
        dst[rows, :] = t.astype(jnp.bfloat16)

def rs_kernel(names, *refs):
    n = len(names)
    G = refs[:n]; out = refs[n:2 * n]
    P = refs[2 * n:3 * n]; bx = refs[3 * n:4 * n]; by = refs[4 * n:5 * n]; bc = refs[5 * n:6 * n]
    stg = refs[6 * n]
    lsem, as_, ar, xs, xr, ys, yr, cs, cr, gxs, gxr, gys, gyr, hxs, hxr, hys, hyr, osem = refs[6 * n + 1:]
    dp, s, z, c = place(4)
    core = (dp, s + 1 - 2 * c)
    xn = (dp + 1 - 2 * lax.rem(dp, 2), s)
    yn = (lax.rem(dp + 2, 4), s)
    q = dp; qx = xn[0]; qy = yn[0]; qd = lax.rem(qx + 2, 4)
    def zdev(k): return (dp, lax.rem(s + 2 * k, 8))
    bar = pltpu.get_barrier_semaphore()
    for d in [core, xn, yn] + [zdev(k) for k in (1, 2, 3)]:
        pl.semaphore_signal(bar, inc=1, device_id=d, device_id_type=MESH)
    pl.semaphore_wait(bar, 6)
    def rc(a_ref, b_ref, s1, s2, dev):
        return pltpu.make_async_remote_copy(src_ref=a_ref, dst_ref=b_ref, send_sem=s1, recv_sem=s2, device_id=dev, device_id_type=MESH)
    g = [GEOM[m] for m in names]
    units = [(a, k) for a in range(n) for k in (1, 2, 3, 0)]
    pend = []
    A, X, Y, C, LCP = {}, {}, {}, {}, {}
    def so(k, other):
        base = lax.rem(s + 2 * k, 8)
        return base + 1 - 2 * c if other else base
    def stA(i):
        a, k = units[i]
        A[i] = rc(G[a].at[so(k, True)], P[a].at[k], as_.at[a, k], ar.at[a, k], core); A[i].start()
    def load(i):
        a, k = units[i]
        R, Cc = G[a].shape[-2:]
        LCP[i] = pltpu.make_async_copy(G[a].at[so(k, False)], stg.at[i % SLOTS, pl.ds(0, R), pl.ds(0, Cc)] if False else stg[a].at[i % SLOTS], lsem.at[i % SLOTS])
        LCP[i].start()
    def stB(i):
        a, k = units[i]
        A[i].wait_recv(); LCP[i].wait()
        p = P[a].at[k]
        add_into(p, [stg[a].at[i % SLOTS]])
        X[i, 1] = rc(cut(p, g[a], qd, 0), bx[a].at[k, 1], xs.at[a, k, 1], xr.at[a, k, 1], xn)
        X[i, 0] = rc(cut(p, g[a], qx, 0), bx[a].at[k, 0], xs.at[a, k, 0], xr.at[a, k, 0], xn)
        Y[i, 1] = rc(cut(p, g[a], qd, 1), by[a].at[k, 1], ys.at[a, k, 1], yr.at[a, k, 1], yn)
        Y[i, 0] = rc(cut(p, g[a], qy, 1), by[a].at[k, 0], ys.at[a, k, 0], yr.at[a, k, 0], yn)
        for j in (1, 0): X[i, j].start(); Y[i, j].start()
    def stC(i):
        a, k = units[i]
        p = P[a].at[k]
        X[i, 1].wait_recv()
        add_into(cut(p, g[a], qy, 0), [bx[a].at[k, 1]])
        Y[i, 2] = rc(cut(p, g[a], qy, 0), by[a].at[k, 2], ys.at[a, k, 2], yr.at[a, k, 2], yn); Y[i, 2].start()
        Y[i, 1].wait_recv()
        add_into(cut(p, g[a], qx, 1), [by[a].at[k, 1]])
        X[i, 2] = rc(cut(p, g[a], qx, 1), bx[a].at[k, 2], xs.at[a, k, 2], xr.at[a, k, 2], xn); X[i, 2].start()
    def stD(i):
        a, k = units[i]
        p = P[a].at[k]
        X[i, 0].wait_recv(); Y[i, 2].wait_recv()
        add_into(cut(p, g[a], q, 0), [bx[a].at[k, 0], by[a].at[k, 2]])
        Y[i, 0].wait_recv(); X[i, 2].wait_recv()
        add_into(cut(p, g[a], q, 1), [by[a].at[k, 0], bx[a].at[k, 2]])
        if k:
            C[i] = rc(cut(p, g[a], q), bc[a].at[k - 1], cs.at[a, k - 1], cr.at[a, k - 1], zdev(k)); C[i].start()
    ag = {}
    def stE(a):
        for k in (1, 2, 3): C[units.index((a, k))].wait_recv()
        p = cut(P[a].at[0], g[a], q)
        add_into(p, [bc[a].at[j] for j in range(3)])
        own = out[a] if names[a] == "kern" else cut(out[a], g[a], q)
        o = pltpu.make_async_copy(p, own, osem.at[a]); o.start()
        ag[a, "o"] = o
        if names[a] != "kern":
            ag[a, "x"] = rc(p, own, gxs.at[a], gxr.at[a], xn); ag[a, "x"].start()
            ag[a, "y"] = rc(p, own, gys.at[a], gyr.at[a], yn); ag[a, "y"].start()
    def stF(a):
        if names[a] == "kern": return
        ag[a, "x"].wait_recv()
        b = cut(out[a], g[a], qx, 0)
        ag[a, "fy"] = rc(b, b, hys.at[a], hyr.at[a], yn); ag[a, "fy"].start()
        ag[a, "y"].wait_recv()
        b = cut(out[a], g[a], qy, 1)
        ag[a, "fx"] = rc(b, b, hxs.at[a], hxr.at[a], xn); ag[a, "fx"].start()
    N = len(units)
    for i in range(min(AHEAD_A, N)): stA(i)
    for i in range(min(SLOTS - 1, N)): load(i)
    for t in range(N + LE + 5):
        if t < N:
            if t + AHEAD_A < N: stA(t + AHEAD_A)
            if t + SLOTS - 1 < N: load(t + SLOTS - 1)
            stB(t)
        if 0 <= t - LC < N: stC(t - LC)
        if 0 <= t - LD < N: stD(t - LD)
        j = t - LE
        if 0 <= j < N and j % 4 == 3: stE(j // 4)
        j = t - LE - 2
        if 0 <= j < N and j % 4 == 3: stF(j // 4)
    for a in range(n):
        if names[a] != "kern":
            for w in ("fx", "fy"): ag[a, w].wait()
            for w in ("x", "y"): ag[a, w].wait_send()
        ag[a, "o"].wait()
    for d in (A, X, Y, C):
        for v in d.values(): v.wait_send()
AHEAD_A = 3

def halfshape(m, R, C):
    return (R // 2, C // 4) if GEOM[m] == "col" else (R // 8, C)
def qshape(m, R, C):
    return (R, C // 4) if GEOM[m] == "col" else (R // 4, C)

def reduce_weights(names, arrs):
    n = len(names)
    D = pltpu.SemaphoreType.DMA
    V = lambda sh: pltpu.VMEM(sh, jnp.bfloat16)
    shp = [a.shape[1:] for a in arrs]
    outs = pl.pallas_call(
        functools.partial(rs_kernel, names),
        out_shape=[jax.ShapeDtypeStruct(qshape(m, *sh) if m == "kern" else sh, jnp.bfloat16) for m, sh in zip(names, shp)],
        in_specs=[pl.BlockSpec(memory_space=pl.ANY)] * n,
        out_specs=[pl.BlockSpec(memory_space=pl.ANY)] * n,
        scratch_shapes=[V((4,) + sh) for sh in shp]
        + [V((4, 3) + halfshape(m, *sh)) for m, sh in zip(names, shp)] * 2
        + [V((3,) + qshape(m, *sh)) for m, sh in zip(names, shp)]
        + [[V((SLOTS,) + sh) for sh in shp]]
        + [D((SLOTS,)), D((n, 4)), D((n, 4))] + [D((n, 4, 3))] * 4 + [D((n, 3))] * 2 + [D((n,))] * 9,
        compiler_params=pltpu.CompilerParams(collective_id=1, has_side_effects=True, vmem_limit_bytes=62 * 2**20),
    )(*arrs)
    return outs


STEP_A = 32


def mode_powers(rate, freq):
    coarse = (jnp.arange(LONG // STEP_A) * STEP_A).astype(F32)
    fine = jnp.arange(STEP_A).astype(F32)

    def powers(lags):
        size = jnp.exp(-rate[:, None, :] * lags[None, :, None])
        turn = freq[:, None, :] * lags[None, :, None]
        return size * jnp.cos(turn), size * jnp.sin(turn)

    return powers(coarse), powers(fine)


def make_kernels(coef, rate, freq):
    (ar, ai), (br, bi) = mode_powers(rate, freq)
    weight = (coef * jnp.sqrt(rate))[:, None, :]
    left = jnp.concatenate([weight * ar, -weight * ai], -1)
    right = jnp.concatenate([br, bi], -1)
    rows = jnp.einsum("ran,rbn->rab", left, right, precision=HIGHEST, preferred_element_type=F32)
    return rows.reshape(rows.shape[0], LONG)


def pull_kernels(grad, coef, rate, freq):
    (ar, ai), (br, bi) = mode_powers(rate, freq)
    rows = grad.reshape(grad.shape[0], LONG // STEP_A, STEP_A)
    lags = jnp.arange(LONG).astype(F32).reshape(LONG // STEP_A, STEP_A)
    both = jnp.concatenate([rows, rows * lags[None]], 1)
    fine = jnp.concatenate([br, bi], -1)
    inner = jnp.einsum("rab,rbn->ran", both, fine, precision=HIGHEST, preferred_element_type=F32)
    n = rate.shape[-1]
    a = LONG // STEP_A
    zero_r, zero_i = inner[:, :a, :n], inner[:, :a, n:]
    one_r, one_i = inner[:, a:, :n], inner[:, a:, n:]
    plain = jnp.sum(ar * zero_r - ai * zero_i, 1)
    lag_r = jnp.sum(ar * one_r - ai * one_i, 1)
    lag_i = jnp.sum(ar * one_i + ai * one_r, 1)
    root = jnp.sqrt(rate)
    return root * plain, coef * (plain / (2 * root) - root * lag_r), -coef * root * lag_i


def dot_plain(left_side, right_side):
    return jnp.dot(left_side, right_side, preferred_element_type=F32)


def dot_inner(left_side, right_side):
    return lax.dot_general(left_side, right_side, (((0,), (0,)), ((), ())), preferred_element_type=F32)


def dot_outer(left_side, right_side):
    return lax.dot_general(left_side, right_side, (((1,), (1,)), ((), ())), preferred_element_type=F32)


def layer_norm(rows, gain, bias):
    centre = jnp.mean(rows, axis=-1, keepdims=True)
    shifted = rows - centre
    spread = jnp.mean(shifted * shifted, axis=-1, keepdims=True)
    return shifted * lax.rsqrt(spread + EPSILON) * gain + bias


def shift(array, by, count):
    pairs = [(i, i + by) for i in range(count) if 0 <= i + by < count]
    return lax.ppermute(array, "seq", pairs)


def from_left(array, count):
    return [shift(array[:, BLK:], 2, count), shift(array, 1, count)]


def from_right(array, count):
    return [shift(array, -1, count), shift(array[:, :BLK], -2, count)]


def same_item(lengths, own_blocks, count):
    starts = jnp.cumsum(lengths, axis=1) - lengths
    total = own_blocks * count
    places = jnp.arange(total) * BLK
    present = (starts[:, None, :] <= places[None, :, None]) & (lengths[:, None, :] > 0)
    owner = jnp.sum(present.astype(jnp.int32), -1)
    first = lax.axis_index("seq") * own_blocks
    padded = jnp.pad(owner, ((0, 0), (REACH, REACH)), constant_values=-1)
    near = lax.dynamic_slice_in_dim(padded, first, own_blocks + 2 * REACH, 1)
    return jnp.stack(
        [
            jnp.stack([(near[:, o + REACH] == near[:, o + REACH + e]) for e in range(-REACH, REACH + 1)], -1)
            for o in range(own_blocks)
        ],
        1,
    ).astype(F32)


def shards(
    n_dp,
    n_seq,
    tokens,
    cotangent,
    lengths,
    ln_gain,
    ln_bias,
    w_value,
    w_filter,
    w_fore,
    w_back,
    w_out,
    ssm_coef,
    ssm_rate,
    ssm_freq,
):
    linked = n_dp == 4 and n_seq == 8
    micros, rows_each, width = tokens.shape
    rows = micros * rows_each
    channels = ssm_coef.shape[1]
    modes = ssm_coef.shape[2]
    parts = 4 if linked else 1
    some = channels // parts
    first = lax.axis_index("dp") * some if linked else 0

    def mine(array):
        return lax.dynamic_slice_in_dim(array, first, some, 1).reshape(2 * some, modes)

    coef, rate, freq = mine(ssm_coef), mine(ssm_rate), mine(ssm_freq)
    kernels = make_kernels(coef, rate, freq).astype(LOW)
    if linked:
        own = {"filter": w_filter, "kern": kernels, "value": w_value, "fore": w_fore, "back": w_back, "out": w_out}
        names = tuple(own)
        gathered = dict(zip(names, gather_weights(names, [own[m] for m in names])))
        kern = gathered["kern"].reshape(n_seq, parts, 2, some, LONG)
    else:
        own = {"filter": w_filter, "value": w_value, "fore": w_fore, "back": w_back, "out": w_out}
        gathered = {m: lax.all_gather(a, "seq", axis=0) for m, a in own.items()}
        kern = lax.all_gather(kernels.reshape(1, 2, some, LONG), "seq", axis=0)
    full = {m: a.reshape(-1, a.shape[-1]) for m, a in gathered.items() if m != "kern"}
    gain = lax.all_gather(ln_gain, "seq", axis=0, tiled=True).astype(F32)
    bias = lax.all_gather(ln_bias, "seq", axis=0, tiled=True).astype(F32)
    tile_step = max(1, 384 // channels)
    wave = jnp.asarray(wave_tables(), LOW)
    mask = same_item(lengths[:, 0], rows_each // BLK, n_seq).reshape(-1)

    token_rows = tokens.reshape(rows, width).astype(F32)
    normed, norm_pull = jax.vjp(layer_norm, token_rows, gain, bias)
    normed_low = normed.astype(LOW)
    pre_filter = dot_plain(normed_low, full["filter"])
    filter_act, filter_pull = jax.vjp(jax.nn.gelu, pre_filter)
    filter_low = filter_act.astype(LOW).reshape(micros, rows_each, -1)
    around = from_left(filter_low, n_seq) + [filter_low] + from_right(filter_low, n_seq)
    pre_value = dot_plain(normed_low, full["value"])
    value_act, value_pull = jax.vjp(jax.nn.gelu, pre_value)
    fore_low, back_low = [a.reshape(rows, -1) for a in conv_forward(mask, wave, kern, around, tile_step)]
    proj_fore = dot_plain(fore_low, full["fore"])
    proj_back = dot_plain(back_low, full["back"])
    hidden_low = (proj_fore * proj_back * value_act).astype(LOW)
    mixed = (token_rows + dot_plain(hidden_low, full["out"])).astype(LOW).reshape(tokens.shape)

    cot_rows = cotangent.reshape(rows, width)
    grad_hidden = dot_outer(cot_rows, full["out"])
    grad_proj_fore = (grad_hidden * proj_back * value_act).astype(LOW)
    grad_proj_back = (grad_hidden * proj_fore * value_act).astype(LOW)
    grad_pre_value = value_pull(grad_hidden * proj_fore * proj_back)[0].astype(LOW)
    grad_fore_low = dot_outer(grad_proj_fore, full["fore"]).astype(LOW).reshape(filter_low.shape)
    grad_back_low = dot_outer(grad_proj_back, full["back"]).astype(LOW).reshape(filter_low.shape)
    fore_around = [grad_fore_low] + from_right(grad_fore_low, n_seq)
    back_around = from_left(grad_back_low, n_seq) + [grad_back_low]
    grads = {}
    grads["out"] = dot_inner(hidden_low, cot_rows)
    grads["fore"] = dot_inner(fore_low, grad_proj_fore)
    grads["back"] = dot_inner(back_low, grad_proj_back)
    grads["value"] = dot_inner(normed_low, grad_pre_value)
    grad_filter_low, grad_kern = conv_backward(mask, wave, kern, around, fore_around, back_around, tile_step)
    grad_pre_filter = filter_pull(grad_filter_low.reshape(rows, -1).astype(F32))[0].astype(LOW)
    grads["filter"] = dot_inner(normed_low, grad_pre_filter)
    grad_normed = dot_outer(grad_pre_value, full["value"]) + dot_outer(grad_pre_filter, full["filter"])
    grad_rows, gain_grad, bias_grad = norm_pull(grad_normed)
    grad_tokens = (cot_rows.astype(F32) + grad_rows).astype(LOW).reshape(tokens.shape)

    grads = {m: a.reshape(n_seq, -1, a.shape[-1]) for m, a in grads.items()}
    if linked:
        grads = {m: a.astype(LOW) for m, a in grads.items()}
        order = ("out", "fore", "back", "kern", "value", "filter")
        grads["kern"] = grad_kern.reshape(n_seq, -1, LONG)
        sums = dict(zip(order, reduce_weights(order, [grads[m] for m in order])))
        sums = {m: a.astype(F32) for m, a in sums.items()}
    else:
        grads["kern"] = grad_kern.reshape(n_seq, -1, LONG)
        sums = {m: lax.psum_scatter(a.astype(F32), "seq", scatter_dimension=0, tiled=False) for m, a in grads.items()}
        sums = {m: lax.psum(a, "dp") for m, a in sums.items()}
    norm_grads = lax.psum(jnp.stack([gain_grad, bias_grad]), ("dp", "seq"))
    norm_grads = lax.dynamic_slice_in_dim(norm_grads, lax.axis_index("seq") * ln_gain.shape[0], ln_gain.shape[0], 1)
    modes_grad = jnp.stack(pull_kernels(sums["kern"], coef, rate, freq)).reshape(3, 2, some, modes)
    if linked:
        modes_grad = lax.all_gather(modes_grad, "dp", axis=2, tiled=True)
    return (
        mixed,
        grad_tokens,
        norm_grads[0],
        norm_grads[1],
        sums["value"],
        sums["filter"],
        sums["fore"],
        sums["back"],
        sums["out"],
        modes_grad[0],
        modes_grad[1],
        modes_grad[2],
    )


def solution(mesh):
    rows = P("seq", None)
    modes = P(None, "seq", None)
    tokens = P(None, ("dp", "seq"), None)
    return jax.shard_map(
        functools.partial(shards, mesh.shape["dp"], mesh.shape["seq"]),
        mesh=mesh,
        in_specs=(tokens, tokens, P(None, "dp", None), P("seq"), P("seq")) + (rows,) * 5 + (modes,) * 3,
        out_specs=(tokens, tokens, P("seq"), P("seq")) + (rows,) * 5 + (modes,) * 3,
        check_vma=False,
    )
```

```python
import functools

import numpy as np

import jax
import jax.numpy as jnp
from jax import lax
from jax.experimental import pallas as pl
from jax.experimental.pallas import tpu as pltpu
from jax.sharding import PartitionSpec as P

MESH = pl.DeviceIdType.MESH
LONG = 512
EPSILON = 1e-05
HIGHEST = lax.Precision.HIGHEST
LOW = jnp.bfloat16
F32 = jnp.float32


BLK = 128
REACH = 3


def wave_tables():
    k = np.arange(BLK)[:, None] + 0.5
    n = np.arange(-BLK, BLK)[None, :]
    angle = 2 * np.pi * k * n / (2 * BLK)
    return np.concatenate([np.cos(angle), -np.sin(angle)], 0).astype(np.float32)


def dot(a, b, ca, cb):
    return lax.dot_general(a, b, (((ca,), (cb,)), ((), ())), preferred_element_type=jnp.float32)


def kernel_spectra(wave_ref, kern_ref, spec_ref, tile):
    for side in range(2):
        rows = jnp.concatenate([kern_ref[a, b, side] for a in range(kern_ref.shape[0]) for b in range(kern_ref.shape[1])], 0)
        spec_ref[side, 0] = dot(wave_ref[:, BLK:], rows[:, :BLK], 1, 1)
        for d in range(1, REACH + 1):
            spec_ref[side, d] = dot(wave_ref[...], rows[:, (d - 1) * BLK:(d + 1) * BLK], 1, 1)


def block_of(parts, micro, at):
    for p in parts:
        n = p.shape[1] // BLK
        if at < n:
            return p[micro, at * BLK:(at + 1) * BLK]
        at -= n


def fore_kernel(mask_ref, wave_ref, kern_ref, *refs):
    parts = refs[:5]
    fore_ref, back_ref, spec_ref, x_ref, y_ref = refs[5:]
    tile = fore_ref.shape[-1]
    kernel_spectra(wave_ref, kern_ref, spec_ref, tile)
    fwd = wave_ref[:, BLK:]
    for micro in range(2):
        for b in range(8):
            x_ref[b] = dot(fwd, block_of(parts, micro, b), 1, 0)

        @pl.loop(0, BLK // 8)
        def _(r):
            re = pl.ds(pl.multiple_of(r * 8, 8), 8)
            im = pl.ds(pl.multiple_of(r * 8 + BLK, 8), 8)
            for lane in range(tile // 128):
                ln = slice(lane * 128, lane * 128 + 128)
                xr = [x_ref[b, re, ln] for b in range(8)]
                xi = [x_ref[b, im, ln] for b in range(8)]
                for side in range(2):
                    cr = [spec_ref[side, d, re, ln] for d in range(4)]
                    ci = [spec_ref[side, d, im, ln] for d in range(4)]
                    for own in range(2):
                        yr = yi = None
                        for d in range(4):
                            at = own + 3 + (d if side else -d)
                            pr = cr[d] * xr[at]
                            pi = cr[d] * xi[at]
                            qr = ci[d] * xi[at]
                            qi = ci[d] * xr[at]
                            if side:
                                tr, ti = pr + qr, pi - qi
                            else:
                                tr, ti = pr - qr, pi + qi
                            if d:
                                m = mask_ref[(micro * 2 + own) * 7 + 3 + (d if side else -d)]
                                tr, ti = tr * m, ti * m
                            yr = tr if yr is None else yr + tr
                            yi = ti if yi is None else yi + ti
                        y_ref[side, own, re, ln] = yr
                        y_ref[side, own, im, ln] = yi
        for own in range(2):
            for side, o in ((0, fore_ref), (1, back_ref)):
                y = dot(fwd, y_ref[side, own].astype(jnp.bfloat16), 0, 0)
                o[micro, own * BLK:(own + 1) * BLK] = (y * (1.0 / BLK)).astype(jnp.bfloat16)


def back_kernel(mask_ref, wave_ref, kern_ref, *refs):
    parts = refs[:-14]
    fparts = refs[-14:-11]
    bparts = refs[-11:-8]
    gfil_ref, gk_ref, spec_ref, x_ref, f_ref, b_ref, y_ref, r_ref = refs[-8:]
    tile = gfil_ref.shape[-1]
    kernel_spectra(wave_ref, kern_ref, spec_ref, tile)
    fwd = wave_ref[:, BLK:]
    for micro in range(2):
        for b in range(8):
            x_ref[b] = dot(fwd, block_of(parts, micro, b), 1, 0)
        for b in range(5):
            f_ref[b] = dot(fwd, block_of(fparts, micro, b), 1, 0)
            b_ref[b] = dot(fwd, block_of(bparts, micro, b), 1, 0)

        @pl.loop(0, BLK // 8)
        def _(r):
            re = pl.ds(pl.multiple_of(r * 8, 8), 8)
            im = pl.ds(pl.multiple_of(r * 8 + BLK, 8), 8)
            for lane in range(tile // 128):
                ln = slice(lane * 128, lane * 128 + 128)
                fr = [f_ref[b, re, ln] for b in range(5)]
                fi = [f_ref[b, im, ln] for b in range(5)]
                gr = [b_ref[b, re, ln] for b in range(5)]
                gi = [b_ref[b, im, ln] for b in range(5)]
                acc = [[None, None], [None, None]]
                for d in range(4):
                    for side in range(2):
                        cr = spec_ref[side, d, re, ln]
                        ci = spec_ref[side, d, im, ln]
                        for own in range(2):
                            if side == 0:
                                vr, vi = fr[own + d], fi[own + d]
                                tr, ti = cr * vr + ci * vi, cr * vi - ci * vr
                                e = d
                            else:
                                vr, vi = gr[own + 3 - d], gi[own + 3 - d]
                                tr, ti = cr * vr - ci * vi, cr * vi + ci * vr
                                e = -d
                            if d:
                                m = mask_ref[(micro * 2 + own) * 7 + 3 + e]
                                tr, ti = tr * m, ti * m
                            a = acc[own]
                            acc[own] = [tr if a[0] is None else a[0] + tr, ti if a[1] is None else a[1] + ti]
                for own in range(2):
                    y_ref[own, re, ln] = acc[own][0]
                    y_ref[own, im, ln] = acc[own][1]
                for side in range(2):
                    for d in range(4):
                        sr = si = None
                        for own in range(2):
                            e = d if side else -d
                            xr, xi = x_ref[own + 3 + e, re, ln], x_ref[own + 3 + e, im, ln]
                            if side == 0:
                                vr, vi = fr[own], fi[own]
                                tr, ti = vr * xr + vi * xi, vi * xr - vr * xi
                            else:
                                vr, vi = gr[own + 3], gi[own + 3]
                                tr, ti = vr * xr + vi * xi, vr * xi - vi * xr
                            if d:
                                m = mask_ref[(micro * 2 + own) * 7 + 3 + e]
                                tr, ti = tr * m, ti * m
                            sr = tr if sr is None else sr + tr
                            si = ti if si is None else si + ti
                        if micro:
                            sr = sr + r_ref[side, d, re, ln]
                            si = si + r_ref[side, d, im, ln]
                        r_ref[side, d, re, ln] = sr
                        r_ref[side, d, im, ln] = si
        for own in range(2):
            y = dot(fwd, y_ref[own].astype(jnp.bfloat16), 0, 0)
            gfil_ref[micro, own * BLK:(own + 1) * BLK] = (y * (1.0 / BLK)).astype(jnp.bfloat16)
    A, B = gk_ref.shape[:2]
    for side in range(2):
        rows = [dot(r_ref[side, d].astype(jnp.bfloat16), wave_ref[:, BLK:] if d == 0 else wave_ref[...], 0, 0) for d in range(4)]
        for d in range(4):
            seg = rows[d][:, -BLK:]
            if d < 3:
                seg = seg + rows[d + 1][:, :BLK]
            seg = (seg * (1.0 / BLK)).astype(jnp.bfloat16)
            w = tile // (A * B)
            for a in range(A):
                for b in range(B):
                    at = (a * B + b) * w
                    gk_ref[a, b, side, :, d * BLK:(d + 1) * BLK] = seg[at:at + w]


def _specs(parts, tile):
    return [pl.BlockSpec((2, p.shape[1], tile), lambda i: (0, 0, i)) for p in parts]


def conv_call(body, mask, wave, kern, parts, outs, scratch, step):
    channels = parts[0].shape[-1]
    steps = kern.shape[0] // step
    tile = channels // steps
    kspec = pl.BlockSpec((step,) + kern.shape[1:], lambda i: (i, 0, 0, 0, 0))
    out_specs = []
    for o in outs:
        if len(o.shape) == 3:
            out_specs.append(pl.BlockSpec((2, o.shape[1], tile), lambda i: (0, 0, i)))
        else:
            out_specs.append(kspec)
    return pl.pallas_call(
        body,
        grid=(steps,),
        out_shape=outs,
        in_specs=[pl.BlockSpec(memory_space=pltpu.SMEM), pl.BlockSpec(memory_space=pltpu.VMEM), kspec] + _specs(parts, tile),
        out_specs=out_specs,
        scratch_shapes=[pltpu.VMEM(sh + (tile,), jnp.float32) for sh in scratch],
        compiler_params=pltpu.CompilerParams(vmem_limit_bytes=56 * 2**20),
        cost_estimate=pl.CostEstimate(flops=10**10, bytes_accessed=3 * 10**7, transcendentals=0),
    )(mask, wave, kern, *parts)


def conv_forward(mask, wave, kern, parts, step):
    own = parts[2]
    sh = jax.ShapeDtypeStruct(own.shape, jnp.bfloat16)
    return conv_call(fore_kernel, mask, wave, kern, parts, [sh, sh], [(2, 4, 256), (8, 256), (2, 2, 256)], step)


def conv_backward(mask, wave, kern, parts, fparts, bparts, step):
    own = fparts[0]
    return conv_call(back_kernel, mask, wave, kern, list(parts) + list(fparts) + list(bparts),
                     [jax.ShapeDtypeStruct(own.shape, jnp.bfloat16), jax.ShapeDtypeStruct(kern.shape, jnp.bfloat16)],
                     [(2, 4, 256), (8, 256), (5, 256), (5, 256), (2, 256), (2, 4, 256)], step)


def place(n_z):
    dp = lax.axis_index("dp"); s = lax.axis_index("seq")
    return dp, s, s // 2, lax.rem(s, 2)

def cut(ref, geom, q, h=None):
    kind = geom
    if kind is None:
        return ref
    R, C = ref.shape[-2:]
    if kind == "col":
        cols = pl.ds(pl.multiple_of(q * (C // 4), 128), C // 4)
        rows = slice(None) if h is None else pl.ds(h * (R // 2), R // 2)
        return ref.at[rows, cols]
    if kind == "row":
        n = R // 4
        if h is None:
            return ref.at[pl.ds(pl.multiple_of(q * n, 16), n)]
        return ref.at[pl.ds(pl.multiple_of(q * n + h * (n // 2), 16), n // 2)]

GEOM = {"filter": "col", "kern": "row", "value": "col", "fore": "col", "back": "col", "out": "row", "norm": None}


FETCH = ("norm", "filter", "value", "out", "kern", "fore", "back")
GELU_C = 0.7978845608028654
GELU_D = 0.044715


def gelu_parts(x):
    sq = x * x
    t = jnp.tanh(GELU_C * x * (1.0 + GELU_D * sq))
    half = 0.5 * (1.0 + t)
    return x * half, half + 0.5 * x * (1.0 - t * t) * (GELU_C * (1.0 + 3.0 * GELU_D * sq))


def slab_forward(mask_ref, wave_ref, kr_ref, spec_ref, x_ref, y_ref, fb_ref, outs, chunk, slab):
    tile = 128
    rows = pl.ds(pl.multiple_of(slab * tile, tile), tile)
    lanes = pl.ds(pl.multiple_of(chunk * 384 + slab * tile, tile), tile)
    fwd = wave_ref[:, BLK:]
    for side in range(2):
        spec_ref[side, 0] = dot(fwd, kr_ref[side, rows, :BLK], 1, 1)
        for d in range(1, REACH + 1):
            spec_ref[side, d] = dot(wave_ref[...], kr_ref[side, rows, (d - 1) * BLK:(d + 1) * BLK], 1, 1)
    for micro in range(2):
        for b in range(8):
            x_ref[b] = dot(fwd, fb_ref[micro, b * BLK:(b + 1) * BLK, lanes], 1, 0)

        @pl.loop(0, BLK // 8)
        def _(r):
            re = pl.ds(pl.multiple_of(r * 8, 8), 8)
            im = pl.ds(pl.multiple_of(r * 8 + BLK, 8), 8)
            xr = [x_ref[b, re, :] for b in range(8)]
            xi = [x_ref[b, im, :] for b in range(8)]
            for side in range(2):
                cr = [spec_ref[side, d, re, :] for d in range(4)]
                ci = [spec_ref[side, d, im, :] for d in range(4)]
                for own in range(2):
                    yr = yi = None
                    for d in range(4):
                        at = own + 3 + (d if side else -d)
                        pr = cr[d] * xr[at]
                        pi = cr[d] * xi[at]
                        qr = ci[d] * xi[at]
                        qi = ci[d] * xr[at]
                        if side:
                            tr, ti = pr + qr, pi - qi
                        else:
                            tr, ti = pr - qr, pi + qi
                        if d:
                            m = mask_ref[(micro * 2 + own) * 7 + 3 + (d if side else -d)]
                            tr, ti = tr * m, ti * m
                        yr = tr if yr is None else yr + tr
                        yi = ti if yi is None else yi + ti
                    y_ref[side, own, re, :] = yr
                    y_ref[side, own, im, :] = yi

        for own in range(2):
            for side in range(2):
                y = dot(fwd, y_ref[side, own].astype(jnp.bfloat16), 0, 0)
                at = micro * 256 + own * BLK
                outs[side][at:at + BLK, lanes] = (y * (1.0 / BLK)).astype(jnp.bfloat16)


def forward_kernel(width, mask_ref, *refs):
    refs = list(refs)
    take = lambda n: [refs.pop(0) for _ in range(n)]
    names = FETCH
    n = len(names)
    wave_in, tok_in, cot_in = take(3)
    src = take(n)
    out = take(n)
    pre_out, fb_out, fore_out, back_out, hid_out, gpf_out, gpb_out, gpv_out, nrm_out = take(9)
    stage = take(n)
    wave_ref, tok, cot, nv, gb, nl, wa, wb, pf, pv, gh, fb, low_f, low_b, kv, kr, spec, xs_, ys_, ring = take(20)
    isem, lsem, zs, zr, xs, xr, ys, yr, fxs, fxr, fys, fyr, ss, sr, ss0, sr0, hs, hr, misc, rsem = refs
    dp, s, z, c = place(4)
    core = (dp, s + 1 - 2 * c)
    odd = (dp, lax.rem(s + 7 + 2 * c, 8))
    xn = (dp + 1 - 2 * lax.rem(dp, 2), s)
    yn = (lax.rem(dp + 2, 4), s)
    q = dp
    qx = xn[0]
    qy = yn[0]

    def zdev(k):
        return (dp, lax.rem(s + 2 * k, 8))

    first = {}
    for i, (a, b) in enumerate([(wave_in, wave_ref), (tok_in, tok), (cot_in, cot)]):
        first[i] = pltpu.make_async_copy(a, b, misc.at[i])
        first[i].start()
    lins = []
    for a in range(n):
        li = pltpu.make_async_copy(src[a], stage[a], isem.at[a])
        li.start()
        lins.append(li)
    halo_rows = 3 * BLK

    @pl.loop(0, halo_rows // 16)
    def _(r):
        lo = pl.ds(pl.multiple_of(r * 16, 16), 16)
        hi = pl.ds(pl.multiple_of(r * 16 + halo_rows + 256, 16), 16)
        zero = jnp.zeros((16, fb.shape[2]), jnp.bfloat16)
        for micro in range(2):
            fb[micro, lo, :] = zero
            fb[micro, hi, :] = zero

    bar = pltpu.get_barrier_semaphore()
    for d in [core, odd, xn, yn, zdev(1), zdev(3)]:
        pl.semaphore_signal(bar, inc=1, device_id=d, device_id_type=MESH)
    pl.semaphore_wait(bar, 6)

    def rc(a_ref, b_ref, s1, s2, dev):
        return pltpu.make_async_remote_copy(src_ref=a_ref, dst_ref=b_ref, send_sem=s1, recv_sem=s2, device_id=dev, device_id_type=MESH)

    g = [GEOM[m] for m in names]
    locs, own_sib, zsend = [], {}, {}
    for a in range(n):
        where = cut(out[a].at[s], g[a], q) if names[a] == "kern" else out[a].at[s]
        locs.append(pltpu.make_async_copy(stage[a], where, lsem.at[a]))

    def near(way, j):
        return lax.rem(s + (8 - 2 * j if way == 0 else 2 * j), 8)

    def here(u):
        a, way, j = u
        return True if j == 0 else (z >= j if way == 0 else z + j <= 3)

    def when(cond, f):
        if cond is True:
            f()
        else:
            pl.when(cond)(f)

    def onward(way):
        return z < 3 if way == 0 else z > 0

    def zgo(a):
        if a < n:
            for way in (0, 1):
                pl.when(onward(way))(zsend[a, way, 0].start)

    def sibgo(a):
        if a < n and names[a] != "kern":
            own_sib[a] = rc(src[a], out[a].at[s], ss0.at[a], sr0.at[a], core)
            own_sib[a].start()

    units = []
    for a in range(n):
        if names[a] == "kern":
            units.append((a, 0, 0))
        for j in (1, 2, 3):
            units += [(a, 0, j), (a, 1, j)]
    last_unit = {u[0]: i for i, u in enumerate(units)}
    xc, yc, fx, fy, sb = {}, {}, {}, {}, {}
    loc_done = set()

    def slot(u):
        return 6 if u[2] == 0 else u[1] * 3 + u[2] - 1

    def blk(u):
        return out[u[0]].at[s if u[2] == 0 else near(u[1], u[2])]

    for a in range(n):
        for way in (0, 1):
            for j in range(3):
                if j:
                    piece = cut(blk((a, way, j)), g[a], q)
                else:
                    piece = src[a] if names[a] == "kern" else cut(src[a], g[a], q)
                there = cut(out[a].at[near(way, j)], g[a], q)
                zsend[a, way, j] = rc(piece, there, zs.at[a, way * 3 + j], zr.at[a, way * 3 + j], zdev(1 if way == 0 else 3))
    zin = {}
    for u in units:
        a, i = u[0], slot(u)
        whole = blk(u)
        b = cut(whole, g[a], q)
        if u[2]:
            zin[u] = rc(b, b, zs.at[a, i], zr.at[a, i], zdev(1))
        if g[a] is not None:
            xc[u] = rc(b, b, xs.at[a, i], xr.at[a, i], xn)
            yc[u] = rc(b, b, ys.at[a, i], yr.at[a, i], yn)
            b = cut(whole, g[a], qx, 0)
            fy[u] = rc(b, b, fys.at[a, i], fyr.at[a, i], yn)
            b = cut(whole, g[a], qy, 1)
            fx[u] = rc(b, b, fxs.at[a, i], fxr.at[a, i], xn)
        sb[u] = rc(whole, whole, ss.at[a, i], sr.at[a, i], core)

    zgo(0)
    zgo(1)
    sibgo(0)
    sibgo(1)
    for a in range(n):
        lins[a].wait()
        locs[a].start()

    def st1(u):
        a, way, j = u
        if j == 0:
            locs[a].wait()
            loc_done.add(a)
        else:
            zin[u].wait_recv()
            if j < 3:
                pl.when(onward(way))(zsend[a, way, j].start)
        if u in xc:
            xc[u].start()
            yc[u].start()

    def st2(u):
        if u in xc:
            xc[u].wait_recv()
            fy[u].start()
            yc[u].wait_recv()
            fx[u].start()

    def st3(u):
        if u in xc:
            fx[u].wait_recv()
            fy[u].wait_recv()
        sb[u].start()

    state = {"t": 0}
    total = len(units) + L3

    def comm():
        t = state["t"]
        state["t"] += 1
        for lag, stage_of in ((0, st1), (L2, st2), (L3, st3)):
            if 0 <= t - lag < len(units):
                u = units[t - lag]
                when(here(u), functools.partial(stage_of, u))
        if t < len(units) and t == last_unit[units[t][0]]:
            zgo(units[t][0] + 2)
            sibgo(units[t][0] + 2)

    def complete(name):
        a = names.index(name)
        while state["t"] <= last_unit[a] + L3:
            comm()
        if a not in loc_done:
            locs[a].wait()
        if a in own_sib:
            own_sib[a].wait_recv()
        for u in units:
            if u[0] == a:
                when(here(u), sb[u].wait_recv)
        return a

    def fetch(pairs, sem0):
        cps = [pltpu.make_async_copy(x, y, misc.at[sem0 + i]) for i, (x, y) in enumerate(pairs)]
        for cp in cps:
            cp.start()
        for cp in cps:
            cp.wait()

    for i in range(3):
        first[i].wait()
    a = complete("norm")
    fetch([(out[a], nv)], 3)
    rows2 = jnp.zeros((16, width), jnp.float32)
    piece = width // 8
    for j in range(8):
        r_ = lax.broadcasted_iota(jnp.int32, (128, width), 0)
        c_ = lax.broadcasted_iota(jnp.int32, (128, width), 1)
        spread = jnp.where((c_ == r_ + j * piece) & (r_ < piece), 1.0, 0.0).astype(jnp.bfloat16)
        rows2 = rows2 + jnp.dot(nv[j], spread, preferred_element_type=jnp.float32)
    gb[...] = rows2

    @pl.loop(0, 512 // 64)
    def _(r):
        rows = pl.ds(pl.multiple_of(r * 64, 64), 64)
        x = tok[rows, :].astype(jnp.float32)
        x = x - jnp.mean(x, axis=-1, keepdims=True)
        var = jnp.mean(x * x, axis=-1, keepdims=True)
        nl[rows, :] = (x * lax.rsqrt(var + 1e-5) * gb[0:1, :] + gb[1:2, :]).astype(jnp.bfloat16)

    nout = pltpu.make_async_copy(nl, nrm_out, misc.at[4])
    nout.start()

    a = complete("filter")
    R = out[a].shape[1]
    fetch([(out[a].at[j], wa.at[pl.ds(768 + j * R, R), pl.ds(0, 1536)]) for j in range(8)], 5)

    @pl.loop(0, 4)
    def _(j):
        cols = pl.ds(pl.multiple_of(j * 384, 128), 384)
        t = jnp.dot(nl[...], wa[768:1536, cols], preferred_element_type=jnp.float32)
        pf[:, cols] = t
        act = gelu_parts(t)[0].astype(jnp.bfloat16)
        for micro in range(2):
            fb[micro, halo_rows:halo_rows + 256, cols] = act[micro * 256:(micro + 1) * 256]

    pre_cp = pltpu.make_async_copy(pf.at[:, pl.ds(0, 1536)], pre_out, misc.at[13])
    pre_cp.start()
    own_rows = pl.ds(halo_rows, 256)
    halos = [
        (1, own_rows, pl.ds(BLK, 256), s < 7, s > 0),
        (2, pl.ds(halo_rows + BLK, BLK), pl.ds(0, BLK), s < 6, s > 1),
        (-1, own_rows, pl.ds(halo_rows + 256, 256), s > 0, s < 7),
        (-2, pl.ds(halo_rows, BLK), pl.ds(halo_rows + 512, BLK), s > 1, s < 6),
    ]
    hcps = {}
    for chunk in range(4):
        cols = pl.ds(chunk * 384, 384)
        for i, (by, from_rows, to_rows, sends, recvs) in enumerate(halos):
            cp = rc(fb.at[:, from_rows, cols], fb.at[:, to_rows, cols], hs.at[chunk, i], hr.at[chunk, i], (dp, lax.rem(s + 8 + by, 8)))
            hcps[chunk, i] = (cp, sends, recvs)

    def halo_go(chunk):
        for i in range(4):
            cp, sends, _ = hcps[chunk, i]
            pl.when(sends)(cp.start)

    def halo_here(chunk):
        for i in range(4):
            cp, _, recvs = hcps[chunk, i]
            pl.when(recvs)(cp.wait_recv)

    halo_go(0)

    a = complete("value")
    R = out[a].shape[1]
    fetch([(out[a].at[j], wa.at[pl.ds(j * R, R)]) for j in range(8)], 5)
    for half in range(2):
        @pl.loop(half * 4, half * 4 + 4)
        def _(j):
            cols = pl.ds(pl.multiple_of(j * 384, 128), 384)
            pv[:, cols] = jnp.dot(nl[...], wa[:768, cols], preferred_element_type=jnp.float32)

        comm()

    halo_go(1)
    a = complete("out")
    halo_go(2)
    fetch([(out[a].at[j], wb.at[pl.ds((j % 2) * 384, 384), pl.ds((j // 2) * 768, 768)]) for j in range(8)], 5)
    for j in range(4):
        gh[:, j * 768:(j + 1) * 768] = dot(cot[...], wb[:768, j * 768:(j + 1) * 768], 1, 1)
        comm()


    def conv_chunk(chunk):
        halo_here(chunk)
        a = names.index("kern")
        fetch([(out[a].at[pl.ds(2 * chunk, 2)], kv)], 3)
        for side in range(2):
            for j in range(2):
                for p in range(4):
                    at = (j * 4 + p) * 48
                    kr[side, at:at + 48] = kv[j, (p * 2 + side) * 48:(p * 2 + side + 1) * 48]

        @pl.loop(0, 3)
        def _(slab):
            slab_forward(mask_ref, wave_ref, kr, spec, xs_, ys_, fb, (low_f, low_b), chunk, slab)

    complete("kern")
    halo_go(3)
    comm()
    comm()
    conv_chunk(0)
    comm()
    comm()
    conv_chunk(1)
    a = complete("fore")
    conv_chunk(2)
    comm()
    comm()
    conv_chunk(3)
    fb_cp = pltpu.make_async_copy(fb, fb_out, misc.at[14])
    fb_cp.start()
    low_cp = [pltpu.make_async_copy(low_f, fore_out, misc.at[15]), pltpu.make_async_copy(low_b, back_out, misc.at[16])]
    for cp in low_cp:
        cp.start()

    R = out[a].shape[1]
    pre_cp.wait()
    fetch([(out[a].at[j], wa.at[pl.ds(j * R, R)]) for j in range(8)], 5)
    for half in range(2):
        @pl.loop(half * 4, half * 4 + 4)
        def _(j):
            cols = pl.ds(pl.multiple_of(j * 384, 128), 384)
            pf[:, cols] = jnp.dot(low_f[...], wa[:, cols], preferred_element_type=jnp.float32)

        comm()
    a = complete("back")
    R = out[a].shape[1]
    fetch([(out[a].at[j], wb.at[pl.ds(j * R, R)]) for j in range(8)], 5)
    dests = (hid_out, gpf_out, gpb_out, gpv_out)

    def ring_cp(j, w):
        cols = pl.ds(pl.multiple_of(j * 256, 128), 256)
        return pltpu.make_async_copy(ring.at[lax.rem(j, 2), w], dests[w].at[:, cols], rsem.at[lax.rem(j, 2), w])

    @pl.loop(0, 12)
    def _(j):
        cols = pl.ds(pl.multiple_of(j * 256, 128), 256)
        slot = lax.rem(j, 2)

        @pl.when(j >= 2)
        def _():
            for w in range(4):
                ring_cp(j - 2, w).wait()

        pb = jnp.dot(low_b[...], wb[:, cols], preferred_element_type=jnp.float32)
        p = pf[:, cols]
        va, dva = gelu_parts(pv[:, cols])
        h = gh[:, cols]
        hv = h * va
        ring[slot, 0] = (p * pb * va).astype(jnp.bfloat16)
        ring[slot, 1] = (hv * pb).astype(jnp.bfloat16)
        ring[slot, 2] = (hv * p).astype(jnp.bfloat16)
        ring[slot, 3] = (h * p * pb * dva).astype(jnp.bfloat16)
        for w in range(4):
            ring_cp(j, w).start()

    for j in (10, 11):
        for w in range(4):
            ring_cp(j, w).wait()

    nout.wait()
    fb_cp.wait()
    for cp in low_cp:
        cp.wait()
    for cp, sends, recvs in hcps.values():
        pl.when(sends)(cp.wait_send)
    for u in units:
        def left():
            for d in (xc, yc, fx, fy, sb):
                if u in d:
                    d[u].wait_send()

        when(here(u), left)
    for (a, way, j), cp in zsend.items():
        gone = here((a, way, j))
        more = onward(way)
        when(more if gone is True else gone & more, cp.wait_send)
    for cp in own_sib.values():
        cp.wait_send()


def gather_forward(mask, tokens, cot, shards):
    rows, width = tokens.shape
    n = len(FETCH)
    D = pltpu.SemaphoreType.DMA
    V = lambda sh, t=jnp.bfloat16: pltpu.VMEM(sh, t)
    full = []
    for m in FETCH:
        R, C = shards[m].shape
        full.append(jax.ShapeDtypeStruct((8, R * (4 if m == "kern" else 1), C), jnp.bfloat16))
    FH, FFN = shards["filter"].shape[1], shards["value"].shape[1]
    f32 = jnp.float32
    S = lambda sh, t=jnp.bfloat16: jax.ShapeDtypeStruct(sh, t)
    extra = [S((rows, FH), f32), S((2, 1024, FH)), S((rows, FH)), S((rows, FH))] + [S((rows, FFN))] * 4 + [S((rows, width))]
    any_ = pl.BlockSpec(memory_space=pl.ANY)
    wave = jnp.asarray(wave_tables(), jnp.bfloat16)
    outs = pl.pallas_call(
        functools.partial(forward_kernel, width),
        out_shape=full + extra,
        in_specs=[pl.BlockSpec(memory_space=pltpu.SMEM)] + [any_] * (3 + n),
        out_specs=[any_] * (n + len(extra)),
        scratch_shapes=[V(shards[m].shape) for m in FETCH]
        + [V(wave.shape), V((rows, width)), V((rows, width)), V((8, 16, 128)), V((16, width), f32), V((rows, width))]
        + [V((FH, FFN)), V((FH, FFN)), V((rows, FFN), f32), V((rows, FFN), f32), V((rows, FFN), f32)]
        + [V((2, 1024, FH)), V((rows, FH)), V((rows, FH)), V((2, 384, 512)), V((2, 384, 512))]
        + [V((2, 4, 256, 128), f32), V((8, 256, 128), f32), V((2, 2, 256, 128), f32), V((2, 4, rows, 256))]
        + [D((n,)), D((n,)), D((n, 6)), D((n, 6))]
        + [D((n, 7))] * 10
        + [D((n,)), D((n,)), D((4, 4)), D((4, 4)), D((17,)), D((2, 4))],
        compiler_params=pltpu.CompilerParams(collective_id=0, has_side_effects=True, vmem_limit_bytes=int(63.5 * 2**20)),
        cost_estimate=pl.CostEstimate(flops=20 * 10**9, bytes_accessed=2 * 10**8, transcendentals=0),
    )(mask, wave, tokens, cot, *[shards[m] for m in FETCH])
    return dict(zip(FETCH, outs[:n])), outs[n:]


L2, L3 = 3, 6


ORDER = ("out", "fore", "back", "value", "kern", "filter")
DEPTH = 3


def add_into(dst, srcs):
    R = dst.shape[-2]

    @pl.loop(0, R // 16)
    def _(r):
        rows = pl.ds(pl.multiple_of(r * 16, 16), 16)
        t = dst[rows, :].astype(jnp.float32)
        for s_ in srcs:
            t = t + s_[rows, :].astype(jnp.float32)
        dst[rows, :] = t.astype(dst.dtype)


def grad_kernel(acts, rights, *refs):
    refs = list(refs)
    take = lambda n: [refs.pop(0) for _ in range(n)]
    act_in = dict(zip(acts, take(len(acts))))
    right_in = dict(zip(rights, take(len(rights))))
    kern_in, norm_in = take(2)
    out = dict(zip(ORDER, take(len(ORDER))))
    norm_out, = take(1)
    act = dict(zip(acts, take(len(acts))))
    right = dict(zip(rights, take(len(rights))))
    P = dict(zip(ORDER, take(len(ORDER))))
    bx = dict(zip(ORDER, take(len(ORDER))))
    by = dict(zip(ORDER, take(len(ORDER))))
    bc = dict(zip(ORDER, take(len(ORDER))))
    snd, stg, nbuf = take(3)
    isem, ksem, as_, ar, xs, xr, ys, yr, cs, cr, gxs, gxr, gys, gyr, hxs, hxr, hys, hyr, osem, ns, nr = refs
    dp, s, z, c = place(4)
    core = (dp, s + 1 - 2 * c)
    xn = (dp + 1 - 2 * lax.rem(dp, 2), s)
    yn = (lax.rem(dp + 2, 4), s)
    q = dp
    qx = xn[0]
    qy = yn[0]
    qd = lax.rem(qx + 2, 4)

    def zdev(k):
        return (dp, lax.rem(s + 2 * k, 8))

    loads = {}
    for i, m in enumerate(acts):
        loads["a", m] = pltpu.make_async_copy(act_in[m], act[m], isem.at[i])
    for i, m in enumerate(rights):
        loads["r", m] = pltpu.make_async_copy(right_in[m], right[m], isem.at[len(acts) + i])
    for m in ORDER:
        for kind, group in (("a", acts), ("r", rights)):
            if m in group:
                loads[kind, m].start()
    kload = pltpu.make_async_copy(kern_in, stg, ksem)
    kload.start()
    bar = pltpu.get_barrier_semaphore()
    for d in [core, xn, yn] + [zdev(k) for k in (1, 2, 3)]:
        pl.semaphore_signal(bar, inc=1, device_id=d, device_id_type=MESH)
    pl.semaphore_wait(bar, 6)

    def rc(a_ref, b_ref, s1, s2, dev):
        return pltpu.make_async_remote_copy(src_ref=a_ref, dst_ref=b_ref, send_sem=s1, recv_sem=s2, device_id=dev, device_id_type=MESH)

    g = GEOM
    units = [(m, k) for m in ORDER for k in (1, 2, 3, 0)]
    at = {m: j for j, m in enumerate(ORDER)}
    A, X, Y, C, waited = {}, {}, {}, {}, set()

    def ready(kind, m):
        if (kind, m) not in waited:
            waited.add((kind, m))
            loads[kind, m].wait()

    def so(k, other):
        base = lax.rem(s + 2 * k, 8)
        return base + 1 - 2 * c if other else base

    def product(m, shard, put):
        R, cols = P[m].shape[-2:]
        step = 768 if R <= 192 else 384
        left = act[m].at[shard]

        @pl.loop(0, cols // step)
        def _(j):
            at_cols = pl.ds(pl.multiple_of(j * step, 128), step)
            put(at_cols, jnp.dot(left[...], right[m][:, at_cols], preferred_element_type=jnp.float32))

    def stA(i):
        m, k = units[i]
        j = at[m]
        if m == "kern":
            if k == 1:
                kload.wait()
            A[i] = rc(stg.at[so(k, True)], P[m].at[k], as_.at[j, k], ar.at[j, k], core)
        else:
            ready("a", m)
            ready("r", m)
            back = [u for u in range(i) if units[u][0] != "kern"]
            if len(back) >= DEPTH:
                A[back[-DEPTH]].wait_send()
            slot = len(back) % DEPTH
            R, cols = P[m].shape[-2:]
            buf = snd.at[slot, pl.ds(0, R), pl.ds(0, cols)]

            def put(cs_, t):
                buf[:, cs_] = t.astype(jnp.bfloat16)

            product(m, so(k, True), put)
            A[i] = rc(buf, P[m].at[k], as_.at[j, k], ar.at[j, k], core)
        A[i].start()

    def stB(i):
        m, k = units[i]
        j = at[m]
        A[i].wait_recv()
        p = P[m].at[k]
        if m == "kern":
            add_into(p, [stg.at[so(k, False)]])
        else:
            def put(cs_, t):
                p[:, cs_] = (p[:, cs_].astype(jnp.float32) + t).astype(jnp.bfloat16)

            product(m, so(k, False), put)
        X[i, 1] = rc(cut(p, g[m], qd, 0), bx[m].at[k, 1], xs.at[j, k, 1], xr.at[j, k, 1], xn)
        X[i, 0] = rc(cut(p, g[m], qx, 0), bx[m].at[k, 0], xs.at[j, k, 0], xr.at[j, k, 0], xn)
        Y[i, 1] = rc(cut(p, g[m], qd, 1), by[m].at[k, 1], ys.at[j, k, 1], yr.at[j, k, 1], yn)
        Y[i, 0] = rc(cut(p, g[m], qy, 1), by[m].at[k, 0], ys.at[j, k, 0], yr.at[j, k, 0], yn)
        for w in (1, 0):
            X[i, w].start()
            Y[i, w].start()

    def stC(i):
        m, k = units[i]
        j = at[m]
        p = P[m].at[k]
        X[i, 1].wait_recv()
        add_into(cut(p, g[m], qy, 0), [bx[m].at[k, 1]])
        Y[i, 2] = rc(cut(p, g[m], qy, 0), by[m].at[k, 2], ys.at[j, k, 2], yr.at[j, k, 2], yn)
        Y[i, 2].start()
        Y[i, 1].wait_recv()
        add_into(cut(p, g[m], qx, 1), [by[m].at[k, 1]])
        X[i, 2] = rc(cut(p, g[m], qx, 1), bx[m].at[k, 2], xs.at[j, k, 2], xr.at[j, k, 2], xn)
        X[i, 2].start()

    def stD(i):
        m, k = units[i]
        j = at[m]
        p = P[m].at[k]
        X[i, 0].wait_recv()
        Y[i, 2].wait_recv()
        add_into(cut(p, g[m], q, 0), [bx[m].at[k, 0], by[m].at[k, 2]])
        Y[i, 0].wait_recv()
        X[i, 2].wait_recv()
        add_into(cut(p, g[m], q, 1), [by[m].at[k, 0], bx[m].at[k, 2]])
        if k:
            C[i] = rc(cut(p, g[m], q), bc[m].at[k - 1], cs.at[j, k - 1], cr.at[j, k - 1], zdev(k))
            C[i].start()

    ag = {}

    def stE(m):
        j = at[m]
        for k in (1, 2, 3):
            C[units.index((m, k))].wait_recv()
        p = cut(P[m].at[0], g[m], q)
        add_into(p, [bc[m].at[w] for w in range(3)])
        own = out[m] if m == "kern" else cut(out[m], g[m], q)
        ag[m, "o"] = pltpu.make_async_copy(p, own, osem.at[j])
        ag[m, "o"].start()
        if m != "kern":
            ag[m, "x"] = rc(p, own, gxs.at[j], gxr.at[j], xn)
            ag[m, "y"] = rc(p, own, gys.at[j], gyr.at[j], yn)
            ag[m, "x"].start()
            ag[m, "y"].start()

    def stF(m):
        if m == "kern":
            return
        j = at[m]
        ag[m, "x"].wait_recv()
        b = cut(out[m], g[m], qx, 0)
        ag[m, "fy"] = rc(b, b, hys.at[j], hyr.at[j], yn)
        ag[m, "fy"].start()
        ag[m, "y"].wait_recv()
        b = cut(out[m], g[m], qy, 1)
        ag[m, "fx"] = rc(b, b, hxs.at[j], hxr.at[j], xn)
        ag[m, "fx"].start()

    nload = pltpu.make_async_copy(norm_in, nbuf.at[0], ns.at[6])
    nload.start()
    N = {}

    def norm_step(w):
        if w == 0:
            nload.wait()
            N[0] = rc(nbuf.at[0], nbuf.at[1], ns.at[0], nr.at[0], core)
            N[0].start()
        elif w in (1, 2):
            N[w - 1].wait()
            nbuf[0] = nbuf[0] + nbuf[w]
            N[w] = rc(nbuf.at[0], nbuf.at[w + 1], ns.at[w], nr.at[w], xn if w == 1 else yn)
            N[w].start()
        elif w == 3:
            N[2].wait()
            nbuf[0] = nbuf[0] + nbuf[3]
            for k in (1, 2, 3):
                N[2 + k] = rc(nbuf.at[0, so(k, False)], nbuf.at[4, k], ns.at[2 + k], nr.at[2 + k], zdev(k))
                N[2 + k].start()
        elif w == 4:
            for k in (1, 2, 3):
                N[2 + k].wait()
            nbuf[4, 0] = nbuf[0, s] + nbuf[4, 1] + nbuf[4, 2] + nbuf[4, 3]
            N[6] = pltpu.make_async_copy(nbuf.at[4, 0], norm_out, ns.at[7])
            N[6].start()

    n = len(units)
    ahead = DEPTH - 1
    for i in range(ahead):
        stA(i)
    for t in range(n + LE + 4):
        if t < n:
            if t + ahead < n:
                stA(t + ahead)
            stB(t)
        if 0 <= t - LC < n:
            stC(t - LC)
        if 0 <= t - LD < n:
            stD(t - LD)
        j = t - LE
        if 0 <= j < n and j % 4 == 3:
            stE(units[j][0])
        j = t - LE - 2
        if 0 <= j < n and j % 4 == 3:
            stF(units[j][0])
        if t >= 4 and t % 2 == 0 and t // 2 - 2 < 5:
            norm_step(t // 2 - 2)
    for m in ORDER:
        if m != "kern":
            for w in ("fx", "fy"):
                ag[m, w].wait()
            for w in ("x", "y"):
                ag[m, w].wait_send()
        ag[m, "o"].wait()
    N[6].wait()
    plain = [u for u in range(n) if units[u][0] != "kern"][-DEPTH:]
    for i in A:
        if i in plain or units[i][0] == "kern":
            A[i].wait_send()
    for d in (X, Y, C):
        for v in d.values():
            v.wait_send()


LC, LD, LE = 1, 2, 3


def half_shape(m, R, C):
    return (R // 2, C // 4) if GEOM[m] == "col" else (R // 8, C)


def quarter_shape(m, R, C):
    return (R, C // 4) if GEOM[m] == "col" else (R // 4, C)


def reduce_gradients(act, right, kern, norm):
    D = pltpu.SemaphoreType.DMA
    V = lambda sh: pltpu.VMEM(sh, jnp.bfloat16)
    shp = {m: kern.shape[1:] if m == "kern" else (act[m].shape[1], right[m].shape[1]) for m in ORDER}
    n = len(ORDER)
    acts, rights = tuple(act), tuple(right)
    any_ = pl.BlockSpec(memory_space=pl.ANY)
    snd = max(shp[m][0] for m in acts), max(shp[m][1] for m in acts)
    outs = pl.pallas_call(
        functools.partial(grad_kernel, acts, rights),
        out_shape=[jax.ShapeDtypeStruct(quarter_shape(m, *shp[m]) if m == "kern" else shp[m], jnp.bfloat16) for m in ORDER]
        + [jax.ShapeDtypeStruct(norm.shape[1:], jnp.float32)],
        in_specs=[any_] * (len(acts) + len(rights) + 2),
        out_specs=[any_] * (n + 1),
        scratch_shapes=[V(act[m].shape) for m in acts]
        + [V(right[m].shape) for m in rights]
        + [V((4,) + shp[m]) for m in ORDER]
        + [V((4, 3) + half_shape(m, *shp[m])) for m in ORDER] * 2
        + [V((3,) + quarter_shape(m, *shp[m])) for m in ORDER]
        + [V((DEPTH,) + snd), V(kern.shape), pltpu.VMEM((5,) + norm.shape, jnp.float32)]
        + [D((len(acts) + len(rights),)), D(()), D((n, 4)), D((n, 4))]
        + [D((n, 4, 3))] * 4
        + [D((n, 3))] * 2
        + [D((n,))] * 9
        + [D((8,))] * 2,
        compiler_params=pltpu.CompilerParams(collective_id=1, has_side_effects=True, vmem_limit_bytes=63 * 2**20),
        cost_estimate=pl.CostEstimate(flops=16 * 10**9, bytes_accessed=10**8, transcendentals=0),
    )(*[act[m] for m in acts], *[right[m] for m in rights], kern, norm)
    return dict(zip(ORDER, outs[:-1])), outs[-1]


STEP_A = 32


def mode_powers(rate, freq):
    coarse = (jnp.arange(LONG // STEP_A) * STEP_A).astype(F32)
    fine = jnp.arange(STEP_A).astype(F32)

    def powers(lags):
        size = jnp.exp(-rate[:, None, :] * lags[None, :, None])
        turn = freq[:, None, :] * lags[None, :, None]
        return size * jnp.cos(turn), size * jnp.sin(turn)

    return powers(coarse), powers(fine)


def make_kernels(coef, rate, freq):
    (ar, ai), (br, bi) = mode_powers(rate, freq)
    weight = (coef * jnp.sqrt(rate))[:, None, :]
    left = jnp.concatenate([weight * ar, -weight * ai], -1)
    right = jnp.concatenate([br, bi], -1)
    rows = jnp.einsum("ran,rbn->rab", left, right, precision=HIGHEST, preferred_element_type=F32)
    return rows.reshape(rows.shape[0], LONG)


def pull_kernels(grad, coef, rate, freq):
    (ar, ai), (br, bi) = mode_powers(rate, freq)
    rows = grad.reshape(grad.shape[0], LONG // STEP_A, STEP_A)
    lags = jnp.arange(LONG).astype(F32).reshape(LONG // STEP_A, STEP_A)
    both = jnp.concatenate([rows, rows * lags[None]], 1)
    fine = jnp.concatenate([br, bi], -1)
    inner = jnp.einsum("rab,rbn->ran", both, fine, precision=HIGHEST, preferred_element_type=F32)
    n = rate.shape[-1]
    a = LONG // STEP_A
    zero_r, zero_i = inner[:, :a, :n], inner[:, :a, n:]
    one_r, one_i = inner[:, a:, :n], inner[:, a:, n:]
    plain = jnp.sum(ar * zero_r - ai * zero_i, 1)
    lag_r = jnp.sum(ar * one_r - ai * one_i, 1)
    lag_i = jnp.sum(ar * one_i + ai * one_r, 1)
    root = jnp.sqrt(rate)
    return root * plain, coef * (plain / (2 * root) - root * lag_r), -coef * root * lag_i


def dot_plain(left_side, right_side):
    return jnp.dot(left_side, right_side, preferred_element_type=F32)


def dot_inner(left_side, right_side):
    return lax.dot_general(left_side, right_side, (((0,), (0,)), ((), ())), preferred_element_type=F32)


def dot_outer(left_side, right_side):
    return lax.dot_general(left_side, right_side, (((1,), (1,)), ((), ())), preferred_element_type=F32)


def layer_norm(rows, gain, bias):
    centre = jnp.mean(rows, axis=-1, keepdims=True)
    shifted = rows - centre
    spread = jnp.mean(shifted * shifted, axis=-1, keepdims=True)
    return shifted * lax.rsqrt(spread + EPSILON) * gain + bias


def shift(array, by, count):
    pairs = [(i, i + by) for i in range(count) if 0 <= i + by < count]
    return lax.ppermute(array, "seq", pairs)


def from_left(array, count):
    return [shift(array[:, BLK:], 2, count), shift(array, 1, count)]


def from_right(array, count):
    return [shift(array, -1, count), shift(array[:, :BLK], -2, count)]


def same_item(lengths, own_blocks, count):
    starts = jnp.cumsum(lengths, axis=1) - lengths
    total = own_blocks * count
    places = jnp.arange(total) * BLK
    present = (starts[:, None, :] <= places[None, :, None]) & (lengths[:, None, :] > 0)
    owner = jnp.sum(present.astype(jnp.int32), -1)
    first = lax.axis_index("seq") * own_blocks
    padded = jnp.pad(owner, ((0, 0), (REACH, REACH)), constant_values=-1)
    near = lax.dynamic_slice_in_dim(padded, first, own_blocks + 2 * REACH, 1)
    return jnp.stack(
        [
            jnp.stack([(near[:, o + REACH] == near[:, o + REACH + e]) for e in range(-REACH, REACH + 1)], -1)
            for o in range(own_blocks)
        ],
        1,
    ).astype(F32)


def shards(
    n_dp,
    n_seq,
    tokens,
    cotangent,
    lengths,
    ln_gain,
    ln_bias,
    w_value,
    w_filter,
    w_fore,
    w_back,
    w_out,
    ssm_coef,
    ssm_rate,
    ssm_freq,
):
    linked = n_dp == 4 and n_seq == 8
    micros, rows_each, width = tokens.shape
    rows = micros * rows_each
    channels = ssm_coef.shape[1]
    modes = ssm_coef.shape[2]
    parts = 4 if linked else 1
    some = channels // parts
    first = lax.axis_index("dp") * some if linked else 0

    def mine(array):
        return lax.dynamic_slice_in_dim(array, first, some, 1).reshape(2 * some, modes)

    coef, rate, freq = mine(ssm_coef), mine(ssm_rate), mine(ssm_freq)
    kernels = make_kernels(coef, rate, freq).astype(LOW)
    mask = same_item(lengths[:, 0], rows_each // BLK, n_seq).reshape(-1)
    wave = jnp.asarray(wave_tables(), LOW)
    tile_step = max(1, 384 // channels)
    cot_rows = cotangent.reshape(rows, width)
    token_rows = tokens.reshape(rows, width).astype(F32)
    if linked:
        pack = jnp.pad(jnp.stack([ln_gain, ln_bias]), ((0, 14), (0, 128 - ln_gain.shape[0])))
        own = {"norm": pack, "filter": w_filter, "kern": kernels, "value": w_value, "fore": w_fore, "back": w_back, "out": w_out}
        gathered, made = gather_forward(mask, tokens.reshape(rows, width), cot_rows, own)
        pre_filter, filter_near, fore_low, back_low, hidden_low, grad_proj_fore, grad_proj_back, grad_pre_value, normed_low = made
        kern = gathered.pop("kern").reshape(n_seq, parts, 2, some, LONG)
        norm = gathered.pop("norm")[:, :2, : ln_gain.shape[0]].astype(F32)
        gain, bias = norm[:, 0].reshape(-1), norm[:, 1].reshape(-1)
        full = {m: a.reshape(-1, a.shape[-1]) for m, a in gathered.items()}
        around = [filter_near]
    else:
        own = {"filter": w_filter, "value": w_value, "fore": w_fore, "back": w_back, "out": w_out}
        full = {m: lax.all_gather(a, "seq", axis=0, tiled=True) for m, a in own.items()}
        kern = lax.all_gather(kernels.reshape(1, 2, some, LONG), "seq", axis=0)
        gain = lax.all_gather(ln_gain, "seq", axis=0, tiled=True).astype(F32)
        bias = lax.all_gather(ln_bias, "seq", axis=0, tiled=True).astype(F32)
        normed_low = layer_norm(token_rows, gain, bias).astype(LOW)
        pre_filter = dot_plain(normed_low, full["filter"])
        filter_low = jax.nn.gelu(pre_filter).astype(LOW).reshape(micros, rows_each, -1)
        around = from_left(filter_low, n_seq) + [filter_low] + from_right(filter_low, n_seq)
        pre_value = dot_plain(normed_low, full["value"])
        value_act, value_pull = jax.vjp(jax.nn.gelu, pre_value)
        fore_low, back_low = [a.reshape(rows, -1) for a in conv_forward(mask, wave, kern, around, tile_step)]
        proj_fore = dot_plain(fore_low, full["fore"])
        proj_back = dot_plain(back_low, full["back"])
        hidden_low = (proj_fore * proj_back * value_act).astype(LOW)
        grad_hidden = dot_outer(cot_rows, full["out"])
        grad_proj_fore = (grad_hidden * proj_back * value_act).astype(LOW)
        grad_proj_back = (grad_hidden * proj_fore * value_act).astype(LOW)
        grad_pre_value = value_pull(grad_hidden * proj_fore * proj_back)[0].astype(LOW)
    filter_pull = jax.vjp(jax.nn.gelu, pre_filter)[1]
    norm_pull = jax.vjp(layer_norm, token_rows, gain, bias)[1]
    mixed = (token_rows + dot_plain(hidden_low, full["out"])).astype(LOW).reshape(tokens.shape)

    grad_fore_low = dot_outer(grad_proj_fore, full["fore"]).astype(LOW).reshape(micros, rows_each, -1)
    grad_back_low = dot_outer(grad_proj_back, full["back"]).astype(LOW).reshape(micros, rows_each, -1)
    fore_around = [grad_fore_low] + from_right(grad_fore_low, n_seq)
    back_around = from_left(grad_back_low, n_seq) + [grad_back_low]
    grad_filter_low, grad_kern = conv_backward(mask, wave, kern, around, fore_around, back_around, tile_step)
    grad_pre_filter = filter_pull(grad_filter_low.reshape(rows, -1).astype(F32))[0].astype(LOW)
    grad_normed = dot_outer(grad_pre_value, full["value"]) + dot_outer(grad_pre_filter, full["filter"])
    grad_rows, gain_grad, bias_grad = norm_pull(grad_normed)
    grad_tokens = (cot_rows.astype(F32) + grad_rows).astype(LOW).reshape(tokens.shape)

    left = {"out": hidden_low, "fore": fore_low, "back": back_low, "value": normed_low, "filter": normed_low}
    right = {"out": cot_rows, "fore": grad_proj_fore, "back": grad_proj_back, "value": grad_pre_value, "filter": grad_pre_filter}
    grad_kern = grad_kern.reshape(n_seq, -1, LONG)
    norm_grads = jnp.stack([gain_grad, bias_grad]).reshape(2, n_seq, -1)
    if linked:
        pack = jnp.pad(jnp.swapaxes(norm_grads, 0, 1), ((0, 0), (0, 6), (0, 128 - norm_grads.shape[2])))
        left = {m: jnp.transpose(a).reshape(n_seq, -1, rows) for m, a in left.items()}
        sums, norm_grads = reduce_gradients(left, right, grad_kern, pack)
        sums = {m: a.astype(F32) for m, a in sums.items()}
        norm_grads = norm_grads[:2, : ln_gain.shape[0]]
    else:
        grads = {m: dot_inner(left[m], right[m]).reshape(n_seq, -1, right[m].shape[1]) for m in left}
        grads["kern"] = grad_kern.astype(F32)
        sums = {m: lax.psum_scatter(a, "seq", scatter_dimension=0, tiled=False) for m, a in grads.items()}
        sums = {m: lax.psum(a, "dp") for m, a in sums.items()}
        norm_grads = lax.psum_scatter(norm_grads, "seq", scatter_dimension=1, tiled=False)
        norm_grads = lax.psum(norm_grads, "dp")
    modes_grad = jnp.stack(pull_kernels(sums["kern"], coef, rate, freq)).reshape(3, 2, some, modes)
    if linked:
        modes_grad = lax.all_gather(modes_grad, "dp", axis=2, tiled=True)
    return (
        mixed,
        grad_tokens,
        norm_grads[0],
        norm_grads[1],
        sums["value"],
        sums["filter"],
        sums["fore"],
        sums["back"],
        sums["out"],
        modes_grad[0],
        modes_grad[1],
        modes_grad[2],
    )


def solution(mesh):
    rows = P("seq", None)
    modes = P(None, "seq", None)
    tokens = P(None, ("dp", "seq"), None)
    return jax.shard_map(
        functools.partial(shards, mesh.shape["dp"], mesh.shape["seq"]),
        mesh=mesh,
        in_specs=(tokens, tokens, P(None, "dp", None), P("seq"), P("seq")) + (rows,) * 5 + (modes,) * 3,
        out_specs=(tokens, tokens, P("seq"), P("seq")) + (rows,) * 5 + (modes,) * 3,
        check_vma=False,
    )
```

```python
import functools

import numpy as np

import jax
import jax.numpy as jnp
from jax import lax
from jax.experimental import pallas as pl
from jax.experimental.pallas import tpu as pltpu
from jax.sharding import PartitionSpec as P

MESH = pl.DeviceIdType.MESH
LONG = 512
EPSILON = 1e-05
HIGHEST = lax.Precision.HIGHEST
LOW = jnp.bfloat16
F32 = jnp.float32


BLK = 128
REACH = 3


def wave_tables():
    k = np.arange(BLK)[:, None] + 0.5
    n = np.arange(-BLK, BLK)[None, :]
    angle = 2 * np.pi * k * n / (2 * BLK)
    return np.concatenate([np.cos(angle), -np.sin(angle)], 0).astype(np.float32)


def dot(a, b, ca, cb):
    return lax.dot_general(a, b, (((ca,), (cb,)), ((), ())), preferred_element_type=jnp.float32)


def kernel_spectra(wave_ref, kern_ref, spec_ref, tile):
    for side in range(2):
        rows = jnp.concatenate([kern_ref[a, b, side] for a in range(kern_ref.shape[0]) for b in range(kern_ref.shape[1])], 0)
        spec_ref[side, 0] = dot(wave_ref[:, BLK:], rows[:, :BLK], 1, 1)
        for d in range(1, REACH + 1):
            spec_ref[side, d] = dot(wave_ref[...], rows[:, (d - 1) * BLK:(d + 1) * BLK], 1, 1)


def block_of(parts, micro, at):
    for p in parts:
        n = p.shape[1] // BLK
        if at < n:
            return p[micro, at * BLK:(at + 1) * BLK]
        at -= n


def fore_kernel(mask_ref, wave_ref, kern_ref, *refs):
    parts = refs[:5]
    fore_ref, back_ref, spec_ref, x_ref, y_ref = refs[5:]
    tile = fore_ref.shape[-1]
    kernel_spectra(wave_ref, kern_ref, spec_ref, tile)
    fwd = wave_ref[:, BLK:]
    for micro in range(2):
        for b in range(8):
            x_ref[b] = dot(fwd, block_of(parts, micro, b), 1, 0)

        @pl.loop(0, BLK // 8)
        def _(r):
            re = pl.ds(pl.multiple_of(r * 8, 8), 8)
            im = pl.ds(pl.multiple_of(r * 8 + BLK, 8), 8)
            for lane in range(tile // 128):
                ln = slice(lane * 128, lane * 128 + 128)
                xr = [x_ref[b, re, ln] for b in range(8)]
                xi = [x_ref[b, im, ln] for b in range(8)]
                for side in range(2):
                    cr = [spec_ref[side, d, re, ln] for d in range(4)]
                    ci = [spec_ref[side, d, im, ln] for d in range(4)]
                    for own in range(2):
                        yr = yi = None
                        for d in range(4):
                            at = own + 3 + (d if side else -d)
                            pr = cr[d] * xr[at]
                            pi = cr[d] * xi[at]
                            qr = ci[d] * xi[at]
                            qi = ci[d] * xr[at]
                            if side:
                                tr, ti = pr + qr, pi - qi
                            else:
                                tr, ti = pr - qr, pi + qi
                            if d:
                                m = mask_ref[(micro * 2 + own) * 7 + 3 + (d if side else -d)]
                                tr, ti = tr * m, ti * m
                            yr = tr if yr is None else yr + tr
                            yi = ti if yi is None else yi + ti
                        y_ref[side, own, re, ln] = yr
                        y_ref[side, own, im, ln] = yi
        for own in range(2):
            for side, o in ((0, fore_ref), (1, back_ref)):
                y = dot(fwd, y_ref[side, own].astype(jnp.bfloat16), 0, 0)
                o[micro, own * BLK:(own + 1) * BLK] = (y * (1.0 / BLK)).astype(jnp.bfloat16)


def back_kernel(mask_ref, wave_ref, kern_ref, *refs):
    parts = refs[:-14]
    fparts = refs[-14:-11]
    bparts = refs[-11:-8]
    gfil_ref, gk_ref, spec_ref, x_ref, f_ref, b_ref, y_ref, r_ref = refs[-8:]
    tile = gfil_ref.shape[-1]
    kernel_spectra(wave_ref, kern_ref, spec_ref, tile)
    fwd = wave_ref[:, BLK:]
    for micro in range(2):
        for b in range(8):
            x_ref[b] = dot(fwd, block_of(parts, micro, b), 1, 0)
        for b in range(5):
            f_ref[b] = dot(fwd, block_of(fparts, micro, b), 1, 0)
            b_ref[b] = dot(fwd, block_of(bparts, micro, b), 1, 0)

        @pl.loop(0, BLK // 8)
        def _(r):
            re = pl.ds(pl.multiple_of(r * 8, 8), 8)
            im = pl.ds(pl.multiple_of(r * 8 + BLK, 8), 8)
            for lane in range(tile // 128):
                ln = slice(lane * 128, lane * 128 + 128)
                fr = [f_ref[b, re, ln] for b in range(5)]
                fi = [f_ref[b, im, ln] for b in range(5)]
                gr = [b_ref[b, re, ln] for b in range(5)]
                gi = [b_ref[b, im, ln] for b in range(5)]
                acc = [[None, None], [None, None]]
                for d in range(4):
                    for side in range(2):
                        cr = spec_ref[side, d, re, ln]
                        ci = spec_ref[side, d, im, ln]
                        for own in range(2):
                            if side == 0:
                                vr, vi = fr[own + d], fi[own + d]
                                tr, ti = cr * vr + ci * vi, cr * vi - ci * vr
                                e = d
                            else:
                                vr, vi = gr[own + 3 - d], gi[own + 3 - d]
                                tr, ti = cr * vr - ci * vi, cr * vi + ci * vr
                                e = -d
                            if d:
                                m = mask_ref[(micro * 2 + own) * 7 + 3 + e]
                                tr, ti = tr * m, ti * m
                            a = acc[own]
                            acc[own] = [tr if a[0] is None else a[0] + tr, ti if a[1] is None else a[1] + ti]
                for own in range(2):
                    y_ref[own, re, ln] = acc[own][0]
                    y_ref[own, im, ln] = acc[own][1]
                for side in range(2):
                    for d in range(4):
                        sr = si = None
                        for own in range(2):
                            e = d if side else -d
                            xr, xi = x_ref[own + 3 + e, re, ln], x_ref[own + 3 + e, im, ln]
                            if side == 0:
                                vr, vi = fr[own], fi[own]
                                tr, ti = vr * xr + vi * xi, vi * xr - vr * xi
                            else:
                                vr, vi = gr[own + 3], gi[own + 3]
                                tr, ti = vr * xr + vi * xi, vr * xi - vi * xr
                            if d:
                                m = mask_ref[(micro * 2 + own) * 7 + 3 + e]
                                tr, ti = tr * m, ti * m
                            sr = tr if sr is None else sr + tr
                            si = ti if si is None else si + ti
                        if micro:
                            sr = sr + r_ref[side, d, re, ln]
                            si = si + r_ref[side, d, im, ln]
                        r_ref[side, d, re, ln] = sr
                        r_ref[side, d, im, ln] = si
        for own in range(2):
            y = dot(fwd, y_ref[own].astype(jnp.bfloat16), 0, 0)
            gfil_ref[micro, own * BLK:(own + 1) * BLK] = (y * (1.0 / BLK)).astype(jnp.bfloat16)
    A, B = gk_ref.shape[:2]
    for side in range(2):
        rows = [dot(r_ref[side, d].astype(jnp.bfloat16), wave_ref[:, BLK:] if d == 0 else wave_ref[...], 0, 0) for d in range(4)]
        for d in range(4):
            seg = rows[d][:, -BLK:]
            if d < 3:
                seg = seg + rows[d + 1][:, :BLK]
            seg = (seg * (1.0 / BLK)).astype(jnp.bfloat16)
            w = tile // (A * B)
            for a in range(A):
                for b in range(B):
                    at = (a * B + b) * w
                    gk_ref[a, b, side, :, d * BLK:(d + 1) * BLK] = seg[at:at + w]


def _specs(parts, tile):
    return [pl.BlockSpec((2, p.shape[1], tile), lambda i: (0, 0, i)) for p in parts]


def conv_call(body, mask, wave, kern, parts, outs, scratch, step):
    channels = parts[0].shape[-1]
    steps = kern.shape[0] // step
    tile = channels // steps
    kspec = pl.BlockSpec((step,) + kern.shape[1:], lambda i: (i, 0, 0, 0, 0))
    out_specs = []
    for o in outs:
        if len(o.shape) == 3:
            out_specs.append(pl.BlockSpec((2, o.shape[1], tile), lambda i: (0, 0, i)))
        else:
            out_specs.append(kspec)
    return pl.pallas_call(
        body,
        grid=(steps,),
        out_shape=outs,
        in_specs=[pl.BlockSpec(memory_space=pltpu.SMEM), pl.BlockSpec(memory_space=pltpu.VMEM), kspec] + _specs(parts, tile),
        out_specs=out_specs,
        scratch_shapes=[pltpu.VMEM(sh + (tile,), jnp.float32) for sh in scratch],
        compiler_params=pltpu.CompilerParams(vmem_limit_bytes=56 * 2**20),
        cost_estimate=pl.CostEstimate(flops=10**10, bytes_accessed=3 * 10**7, transcendentals=0),
    )(mask, wave, kern, *parts)


def conv_forward(mask, wave, kern, parts, step):
    own = parts[2]
    sh = jax.ShapeDtypeStruct(own.shape, jnp.bfloat16)
    return conv_call(fore_kernel, mask, wave, kern, parts, [sh, sh], [(2, 4, 256), (8, 256), (2, 2, 256)], step)


def conv_backward(mask, wave, kern, parts, fparts, bparts, step):
    own = fparts[0]
    return conv_call(back_kernel, mask, wave, kern, list(parts) + list(fparts) + list(bparts),
                     [jax.ShapeDtypeStruct(own.shape, jnp.bfloat16), jax.ShapeDtypeStruct(kern.shape, jnp.bfloat16)],
                     [(2, 4, 256), (8, 256), (5, 256), (5, 256), (2, 256), (2, 4, 256)], step)


def place(n_z):
    dp = lax.axis_index("dp"); s = lax.axis_index("seq")
    return dp, s, s // 2, lax.rem(s, 2)

def cut(ref, geom, q, h=None):
    kind = geom
    if kind is None:
        return ref
    R, C = ref.shape[-2:]
    if kind == "col":
        cols = pl.ds(pl.multiple_of(q * (C // 4), 128), C // 4)
        rows = slice(None) if h is None else pl.ds(h * (R // 2), R // 2)
        return ref.at[rows, cols]
    if kind == "row":
        n = R // 4
        if h is None:
            return ref.at[pl.ds(pl.multiple_of(q * n, 16), n)]
        return ref.at[pl.ds(pl.multiple_of(q * n + h * (n // 2), 16), n // 2)]

GEOM = {"filter": "col", "kern": "row", "value": "col", "fore": "col", "back": "col", "out": "row", "norm": None}


FETCH = ("norm", "filter", "kern", "fore", "back", "value", "out")
SMALL = ("norm", "kern")
GELU_C = 0.7978845608028654
GELU_D = 0.044715


def gelu_parts(x):
    sq = x * x
    t = jnp.tanh(GELU_C * x * (1.0 + GELU_D * sq))
    half = 0.5 * (1.0 + t)
    return x * half, half + 0.5 * x * (1.0 - t * t) * (GELU_C * (1.0 + 3.0 * GELU_D * sq))


def slab_forward(mask_ref, wave_ref, kr_ref, spec_ref, x_ref, y_ref, fb_ref, outs, chunk):
    rows = slice(None)
    lanes = slice(chunk * 384, chunk * 384 + 384)
    fwd = wave_ref[:, BLK:]
    for side in range(2):
        spec_ref[side, 0] = dot(fwd, kr_ref[side, rows, :BLK], 1, 1)
        for d in range(1, REACH + 1):
            spec_ref[side, d] = dot(wave_ref[...], kr_ref[side, rows, (d - 1) * BLK:(d + 1) * BLK], 1, 1)
    for micro in range(2):
        for b in range(8):
            x_ref[b] = dot(fwd, fb_ref[micro, b * BLK:(b + 1) * BLK, lanes], 1, 0)

        @pl.loop(0, BLK // 16)
        def _(r):
            re = pl.ds(pl.multiple_of(r * 16, 16), 16)
            im = pl.ds(pl.multiple_of(r * 16 + BLK, 16), 16)
            for lane in range(3):
                ln = slice(lane * 128, lane * 128 + 128)
                xr = [x_ref[b, re, ln] for b in range(8)]
                xi = [x_ref[b, im, ln] for b in range(8)]
                for side in range(2):
                    cr = [spec_ref[side, d, re, ln] for d in range(4)]
                    ci = [spec_ref[side, d, im, ln] for d in range(4)]
                    for own in range(2):
                        yr = yi = None
                        for d in range(4):
                            at = own + 3 + (d if side else -d)
                            pr = cr[d] * xr[at]
                            pi = cr[d] * xi[at]
                            qr = ci[d] * xi[at]
                            qi = ci[d] * xr[at]
                            if side:
                                tr, ti = pr + qr, pi - qi
                            else:
                                tr, ti = pr - qr, pi + qi
                            if d:
                                m = mask_ref[(micro * 2 + own) * 7 + 3 + (d if side else -d)]
                                tr, ti = tr * m, ti * m
                            yr = tr if yr is None else yr + tr
                            yi = ti if yi is None else yi + ti
                        y_ref[side, own, re, ln] = yr.astype(jnp.bfloat16)
                        y_ref[side, own, im, ln] = yi.astype(jnp.bfloat16)

        for own in range(2):
            for side in range(2):
                y = dot(fwd, y_ref[side, own], 0, 0)
                at = micro * 256 + own * BLK
                outs[side][at:at + BLK, lanes] = (y * (1.0 / BLK)).astype(jnp.bfloat16)


def forward_kernel(width, mask_ref, *refs):
    refs = list(refs)
    take = lambda n: [refs.pop(0) for _ in range(n)]
    names = FETCH
    n = len(names)
    wave_in, tok_in, cot_in = take(3)
    src = take(n)
    out = take(n)
    pre_out, fb_out, fore_out, back_out, hid_out, gpf_out, gpb_out, gpv_out, nrm_out = take(9)
    stage = dict(zip(SMALL, take(len(SMALL))))
    wave_ref, tok, cot, nv, gb, nl, wa, wb, pf, pv, pk, fb, low_f, low_b, kv, kr, spec, xs_, ys_, ring = take(20)
    isem, lsem, fsem, zs, zr, xs, xr, ys, yr, fxs, fxr, fys, fyr, ss, sr, ss0, sr0, hs, hr, misc, rsem = refs
    dp, s, z, c = place(4)
    core = (dp, s + 1 - 2 * c)
    odd = (dp, lax.rem(s + 7 + 2 * c, 8))
    xn = (dp + 1 - 2 * lax.rem(dp, 2), s)
    yn = (lax.rem(dp + 2, 4), s)
    q = dp
    qx = xn[0]
    qy = yn[0]

    def zdev(k):
        return (dp, lax.rem(s + 2 * k, 8))

    first = {}
    for i, (a, b) in enumerate([(wave_in, wave_ref), (tok_in, tok), (cot_in, cot)]):
        first[i] = pltpu.make_async_copy(a, b, misc.at[i])
        first[i].start()
    lins = {}
    for m in SMALL:
        a = names.index(m)
        lins[a] = pltpu.make_async_copy(src[a], stage[m], isem.at[a])
        lins[a].start()
    halo_rows = 3 * BLK

    @pl.loop(0, halo_rows // 16)
    def _(r):
        lo = pl.ds(pl.multiple_of(r * 16, 16), 16)
        hi = pl.ds(pl.multiple_of(r * 16 + halo_rows + 256, 16), 16)
        zero = jnp.zeros((16, fb.shape[2]), jnp.bfloat16)
        for micro in range(2):
            fb[micro, lo, :] = zero
            fb[micro, hi, :] = zero

    bar = pltpu.get_barrier_semaphore()
    for d in [core, odd, xn, yn, zdev(1), zdev(3)]:
        pl.semaphore_signal(bar, inc=1, device_id=d, device_id_type=MESH)
    pl.semaphore_wait(bar, 6)

    def rc(a_ref, b_ref, s1, s2, dev):
        return pltpu.make_async_remote_copy(src_ref=a_ref, dst_ref=b_ref, send_sem=s1, recv_sem=s2, device_id=dev, device_id_type=MESH)

    g = [GEOM[m] for m in names]
    def place_of(m, shard):
        R = out[names.index(m)].shape[1]
        if m == "filter":
            return wa.at[pl.ds(pl.multiple_of(768 + shard * R, 16), R), pl.ds(0, 1536)]
        if m == "out":
            return wa.at[pl.ds(pl.multiple_of(768 + lax.rem(shard, 2) * R, 16), R), pl.ds(pl.multiple_of(lax.div(shard, 2) * 768, 128), 768)]
        return (wb if m == "back" else wa).at[pl.ds(pl.multiple_of(shard * R, 16), R)]

    locs, own_sib, zsend = [], {}, {}
    for a in range(n):
        where = cut(out[a].at[s], g[a], q) if names[a] == "kern" else out[a].at[s]
        held = stage[names[a]] if names[a] in SMALL else place_of(names[a], s)
        locs.append(pltpu.make_async_copy(held, where, lsem.at[a]))

    def near(way, j):
        return lax.rem(s + (8 - 2 * j if way == 0 else 2 * j), 8)

    def here(u):
        a, way, j = u
        return True if j == 0 else (z >= j if way == 0 else z + j <= 3)

    def when(cond, f):
        if cond is True:
            f()
        else:
            pl.when(cond)(f)

    def onward(way):
        return z < 3 if way == 0 else z > 0

    def zgo(a):
        if a < n:
            for way in (0, 1):
                pl.when(onward(way))(zsend[a, way, 0].start)

    def sibgo(a):
        if a < n and names[a] != "kern":
            own_sib[a] = rc(src[a], out[a].at[s], ss0.at[a], sr0.at[a], core)
            own_sib[a].start()

    units = []
    for a in range(n):
        if names[a] == "kern":
            units.append((a, 0, 0))
        for j in (1, 2, 3):
            units += [(a, 0, j), (a, 1, j)]
    last_unit = {u[0]: i for i, u in enumerate(units)}
    xc, yc, fx, fy, sb = {}, {}, {}, {}, {}
    loc_done = set()

    def slot(u):
        return 6 if u[2] == 0 else u[1] * 3 + u[2] - 1

    def blk(u):
        return out[u[0]].at[s if u[2] == 0 else near(u[1], u[2])]

    for a in range(n):
        for way in (0, 1):
            for j in range(3):
                if j:
                    piece = cut(blk((a, way, j)), g[a], q)
                else:
                    piece = src[a] if names[a] == "kern" else cut(src[a], g[a], q)
                there = cut(out[a].at[near(way, j)], g[a], q)
                zsend[a, way, j] = rc(piece, there, zs.at[a, way * 3 + j], zr.at[a, way * 3 + j], zdev(1 if way == 0 else 3))
    zin = {}
    for u in units:
        a, i = u[0], slot(u)
        whole = blk(u)
        b = cut(whole, g[a], q)
        if u[2]:
            zin[u] = rc(b, b, zs.at[a, i], zr.at[a, i], zdev(1))
        if g[a] is not None:
            xc[u] = rc(b, b, xs.at[a, i], xr.at[a, i], xn)
            yc[u] = rc(b, b, ys.at[a, i], yr.at[a, i], yn)
            b = cut(whole, g[a], qx, 0)
            fy[u] = rc(b, b, fys.at[a, i], fyr.at[a, i], yn)
            b = cut(whole, g[a], qy, 1)
            fx[u] = rc(b, b, fxs.at[a, i], fxr.at[a, i], xn)
        sb[u] = rc(whole, whole, ss.at[a, i], sr.at[a, i], core)

    zgo(0)
    zgo(1)
    sibgo(0)
    sibgo(1)
    for a in lins:
        lins[a].wait()
        locs[a].start()

    def st0(u):
        a, way, j = u
        if j == 0:
            locs[a].wait()
            loc_done.add(a)
        else:
            zin[u].wait_recv()
            if j < 3:
                pl.when(onward(way))(zsend[a, way, j].start)

    def st1(u):
        if u in xc:
            xc[u].start()
            yc[u].start()

    def st2(u):
        if u in xc:
            xc[u].wait_recv()
            fy[u].start()
            yc[u].wait_recv()
            fx[u].start()

    def st3(u):
        if u in xc:
            fx[u].wait_recv()
            fy[u].wait_recv()
        sb[u].start()

    loaded = {}
    for u in units:
        a = u[0]
        if names[a] in ("filter", "value", "out", "fore", "back"):
            shard = near(u[1], u[2])
            other = shard + 1 - 2 * c
            for w, sh in ((0, shard), (1, other)):
                loaded[u, w] = pltpu.make_async_copy(out[a].at[sh], place_of(names[a], sh), fsem.at[a, slot(u), w])
    for a in range(n):
        if names[a] in ("filter", "value", "out", "fore", "back"):
            for w, sh in ((0, s), (1, s + 1 - 2 * c)):
                origin = src[a] if w == 0 else out[a].at[sh]
                loaded[(a, 0, 0), w] = pltpu.make_async_copy(origin, place_of(names[a], sh), fsem.at[a, 6, w])

    def st4(u):
        sb[u].wait_recv()
        for w in (0, 1):
            if (u, w) in loaded:
                assert names[u[0]] not in ("value", "out") or state["free"]
                loaded[u, w].start()

    state = {"t": 0, "free": False}

    def comm():
        t = state["t"]
        state["t"] += 1
        for lag, stage_of in ((0, st0), (L1, st1), (L2, st2), (L3, st3), (L4, st4)):
            if 0 <= t - lag < len(units):
                u = units[t - lag]
                when(here(u), functools.partial(stage_of, u))
        if t < len(units) and t == last_unit[units[t][0]]:
            zgo(units[t][0] + 2)
            sibgo(units[t][0] + 2)

    def complete(name):
        a = names.index(name)
        while state["t"] <= last_unit[a] + L4:
            comm()
        if a not in loc_done and name in SMALL:
            locs[a].wait()
        if a in own_sib:
            own_sib[a].wait_recv()
        own = (a, 0, 0)
        for w in (0, 1):
            if (own, w) in loaded:
                loaded[own, w].start()
        for u in [own] + [u for u in units if u[0] == a]:
            for w in (0, 1):
                if (u, w) in loaded:
                    when(here(u), loaded[u, w].wait)
        if name not in SMALL:
            locs[a].start()
            locs[a].wait()
        return a

    def fetch(pairs, sem0):
        cps = [pltpu.make_async_copy(x, y, misc.at[sem0 + i]) for i, (x, y) in enumerate(pairs)]
        for cp in cps:
            cp.start()
        for cp in cps:
            cp.wait()

    for i in range(3):
        first[i].wait()
    a = complete("norm")
    fetch([(out[a], nv)], 3)
    rows2 = jnp.zeros((16, width), jnp.float32)
    piece = width // 8
    for j in range(8):
        r_ = lax.broadcasted_iota(jnp.int32, (128, width), 0)
        c_ = lax.broadcasted_iota(jnp.int32, (128, width), 1)
        spread = jnp.where((c_ == r_ + j * piece) & (r_ < piece), 1.0, 0.0).astype(jnp.bfloat16)
        rows2 = rows2 + jnp.dot(nv[j], spread, preferred_element_type=jnp.float32)
    gb[...] = rows2

    @pl.loop(0, 512 // 64)
    def _(r):
        rows = pl.ds(pl.multiple_of(r * 64, 64), 64)
        x = tok[rows, :].astype(jnp.float32)
        x = x - jnp.mean(x, axis=-1, keepdims=True)
        var = jnp.mean(x * x, axis=-1, keepdims=True)
        nl[rows, :] = (x * lax.rsqrt(var + 1e-5) * gb[0:1, :] + gb[1:2, :]).astype(jnp.bfloat16)

    nout = pltpu.make_async_copy(nl, nrm_out, misc.at[4])
    nout.start()

    a = complete("filter")

    @pl.loop(0, 3)
    def _(j):
        cols = pl.ds(pl.multiple_of(j * 512, 128), 512)
        t = jnp.dot(nl[...], wa[768:1536, cols], preferred_element_type=jnp.float32)
        pf[:, cols] = t
        act = gelu_parts(t)[0].astype(jnp.bfloat16)
        for micro in range(2):
            fb[micro, halo_rows:halo_rows + 256, cols] = act[micro * 256:(micro + 1) * 256]

    pre_cp = pltpu.make_async_copy(pf.at[:, pl.ds(0, 1536)], pre_out, misc.at[13])
    pre_cp.start()
    own_rows = pl.ds(halo_rows, 256)
    halos = [
        (1, own_rows, pl.ds(BLK, 256), s < 7, s > 0),
        (2, pl.ds(halo_rows + BLK, BLK), pl.ds(0, BLK), s < 6, s > 1),
        (-1, own_rows, pl.ds(halo_rows + 256, 256), s > 0, s < 7),
        (-2, pl.ds(halo_rows, BLK), pl.ds(halo_rows + 512, BLK), s > 1, s < 6),
    ]
    hcps = {}
    for chunk in range(4):
        cols = pl.ds(chunk * 384, 384)
        for i, (by, from_rows, to_rows, sends, recvs) in enumerate(halos):
            cp = rc(fb.at[:, from_rows, cols], fb.at[:, to_rows, cols], hs.at[chunk, i], hr.at[chunk, i], (dp, lax.rem(s + 8 + by, 8)))
            hcps[chunk, i] = (cp, sends, recvs)

    def halo_go(chunk):
        for i in range(4):
            cp, sends, _ = hcps[chunk, i]
            pl.when(sends)(cp.start)

    def halo_here(chunk):
        for i in range(4):
            cp, _, recvs = hcps[chunk, i]
            pl.when(recvs)(cp.wait_recv)

    halo_go(0)


    def conv_chunk(chunk):
        halo_here(chunk)
        a = names.index("kern")
        fetch([(out[a].at[pl.ds(2 * chunk, 2)], kv)], 3)
        for side in range(2):
            for j in range(2):
                for p in range(4):
                    at = (j * 4 + p) * 48
                    kr[side, at:at + 48] = kv[j, (p * 2 + side) * 48:(p * 2 + side + 1) * 48]

        slab_forward(mask_ref, wave_ref, kr, spec, xs_, ys_, fb, (low_f, low_b), chunk)

    complete("kern")
    halo_go(1)
    comm()
    halo_go(2)
    conv_chunk(0)
    comm()
    comm()
    halo_go(3)
    conv_chunk(1)
    comm()
    comm()
    conv_chunk(2)
    comm()
    comm()
    conv_chunk(3)
    complete("fore")
    fb_cp = pltpu.make_async_copy(fb, fb_out, misc.at[14])
    fb_cp.start()
    low_cp = [pltpu.make_async_copy(low_f, fore_out, misc.at[15]), pltpu.make_async_copy(low_b, back_out, misc.at[16])]
    for cp in low_cp:
        cp.start()

    R = out[a].shape[1]
    pre_cp.wait()
    for half in range(2):
        @pl.loop(half * 3, half * 3 + 3)
        def _(j):
            cols = pl.ds(pl.multiple_of(j * 512, 128), 512)
            pf[:, cols] = jnp.dot(low_f[...], wa[:, cols], preferred_element_type=jnp.float32)

        comm()
    state["free"] = True
    complete("back")
    for half in range(2):
        @pl.loop(half * 3, half * 3 + 3)
        def _(j):
            cols = pl.ds(pl.multiple_of(j * 512, 128), 512)
            pk[:, cols] = jnp.dot(low_b[...], wb[:, cols], preferred_element_type=jnp.float32)

        comm()
    a = complete("value")
    for half in range(2):
        @pl.loop(half * 3, half * 3 + 3)
        def _(j):
            cols = pl.ds(pl.multiple_of(j * 512, 128), 512)
            pv[:, cols] = jnp.dot(nl[...], wa[:768, cols], preferred_element_type=jnp.float32)

        comm()

    complete("out")
    dests = (hid_out, gpf_out, gpb_out, gpv_out)

    def ring_cp(j, w):
        cols = pl.ds(pl.multiple_of(j * 256, 128), 256)
        return pltpu.make_async_copy(ring.at[lax.rem(j, 2), w], dests[w].at[:, cols], rsem.at[lax.rem(j, 2), w])

    @pl.loop(0, 12)
    def _(j):
        cols = pl.ds(pl.multiple_of(j * 256, 128), 256)
        slot = lax.rem(j, 2)

        @pl.when(j >= 2)
        def _():
            for w in range(4):
                ring_cp(j - 2, w).wait()

        out_rows = pl.ds(pl.multiple_of(768 + lax.rem(j, 3) * 256, 16), 256)
        out_cols = pl.ds(pl.multiple_of(lax.div(j, 3) * 768, 128), 768)
        h = dot(cot[...], wa[out_rows, out_cols], 1, 1)
        pb = pk[:, cols]
        p = pf[:, cols]
        va, dva = gelu_parts(pv[:, cols])
        hv = h * va
        ring[slot, 0] = (p * pb * va).astype(jnp.bfloat16)
        ring[slot, 1] = (hv * pb).astype(jnp.bfloat16)
        ring[slot, 2] = (hv * p).astype(jnp.bfloat16)
        ring[slot, 3] = (h * p * pb * dva).astype(jnp.bfloat16)
        for w in range(4):
            ring_cp(j, w).start()

    for j in (10, 11):
        for w in range(4):
            ring_cp(j, w).wait()

    nout.wait()
    fb_cp.wait()
    for cp in low_cp:
        cp.wait()
    for cp, sends, recvs in hcps.values():
        pl.when(sends)(cp.wait_send)
    for u in units:
        def left():
            for d in (xc, yc, fx, fy, sb):
                if u in d:
                    d[u].wait_send()

        when(here(u), left)
    for (a, way, j), cp in zsend.items():
        gone = here((a, way, j))
        more = onward(way)
        when(more if gone is True else gone & more, cp.wait_send)
    for cp in own_sib.values():
        cp.wait_send()


def gather_forward(mask, tokens, cot, shards):
    rows, width = tokens.shape
    n = len(FETCH)
    D = pltpu.SemaphoreType.DMA
    V = lambda sh, t=jnp.bfloat16: pltpu.VMEM(sh, t)
    full = []
    for m in FETCH:
        R, C = shards[m].shape
        full.append(jax.ShapeDtypeStruct((8, R * (4 if m == "kern" else 1), C), jnp.bfloat16))
    FH, FFN = shards["filter"].shape[1], shards["value"].shape[1]
    f32 = jnp.float32
    S = lambda sh, t=jnp.bfloat16: jax.ShapeDtypeStruct(sh, t)
    extra = [S((rows, FH), f32), S((2, 1024, FH)), S((rows, FH)), S((rows, FH))] + [S((rows, FFN))] * 4 + [S((rows, width))]
    any_ = pl.BlockSpec(memory_space=pl.ANY)
    wave = jnp.asarray(wave_tables(), jnp.bfloat16)
    outs = pl.pallas_call(
        functools.partial(forward_kernel, width),
        out_shape=full + extra,
        in_specs=[pl.BlockSpec(memory_space=pltpu.SMEM)] + [any_] * (3 + n),
        out_specs=[any_] * (n + len(extra)),
        scratch_shapes=[V(shards[m].shape) for m in SMALL]
        + [V(wave.shape), V((rows, width)), V((rows, width)), V((8, 16, 128)), V((16, width), f32), V((rows, width))]
        + [V((FH, FFN)), V((FH, FFN)), V((rows, FFN), f32), V((rows, FFN), f32), V((rows, FFN), f32)]
        + [V((2, 1024, FH)), V((rows, FH)), V((rows, FH)), V((2, 384, 512)), V((2, 384, 512))]
        + [V((2, 4, 256, 384), f32), V((8, 256, 384), f32), V((2, 2, 256, 384)), V((2, 4, rows, 256))]
        + [D((n,)), D((n,)), D((n, 7, 2)), D((n, 6)), D((n, 6))]
        + [D((n, 7))] * 10
        + [D((n,)), D((n,)), D((4, 4)), D((4, 4)), D((17,)), D((2, 4))],
        compiler_params=pltpu.CompilerParams(collective_id=0, has_side_effects=True, vmem_limit_bytes=int(63.5 * 2**20)),
        cost_estimate=pl.CostEstimate(flops=20 * 10**9, bytes_accessed=2 * 10**8, transcendentals=0),
    )(mask, wave, tokens, cot, *[shards[m] for m in FETCH])
    return dict(zip(FETCH, outs[:n])), outs[n:]


L1, L2, L3, L4 = 0, 2, 5, 7


FIRST_Z = ()
ORDER = ("out", "fore", "back", "value", "kern", "filter")
DEPTH = 3


def add_into(dst, srcs):
    R = dst.shape[-2]

    @pl.loop(0, R // 16)
    def _(r):
        rows = pl.ds(pl.multiple_of(r * 16, 16), 16)
        t = dst[rows, :].astype(jnp.float32)
        for s_ in srcs:
            t = t + s_[rows, :].astype(jnp.float32)
        dst[rows, :] = t.astype(dst.dtype)


def grad_kernel(acts, rights, *refs):
    refs = list(refs)
    take = lambda n: [refs.pop(0) for _ in range(n)]
    act_in = dict(zip(acts, take(len(acts))))
    right_in = dict(zip(rights, take(len(rights))))
    kern_in, norm_in = take(2)
    out = dict(zip(ORDER, take(len(ORDER))))
    norm_out, = take(1)
    act = dict(zip(acts, take(len(acts))))
    right = dict(zip(rights, take(len(rights))))
    P = dict(zip(ORDER, take(len(ORDER))))
    bx = dict(zip(ORDER, take(len(ORDER))))
    by = dict(zip(ORDER, take(len(ORDER))))
    bc = dict(zip(ORDER, take(len(ORDER))))
    snd, snd2, stg, nbuf = take(4)
    isem, ksem, as_, ar, xs, xr, ys, yr, cs, cr, gxs, gxr, gys, gyr, hxs, hxr, hys, hyr, osem, ns, nr = refs
    dp, s, z, c = place(4)
    core = (dp, s + 1 - 2 * c)
    xn = (dp + 1 - 2 * lax.rem(dp, 2), s)
    yn = (lax.rem(dp + 2, 4), s)
    q = dp
    qx = xn[0]
    qy = yn[0]
    qd = lax.rem(qx + 2, 4)

    def zdev(k):
        return (dp, lax.rem(s + 2 * k, 8))

    loads = {}
    for i, m in enumerate(acts):
        loads["a", m] = pltpu.make_async_copy(act_in[m], act[m], isem.at[i])
    for i, m in enumerate(rights):
        loads["r", m] = pltpu.make_async_copy(right_in[m], right[m], isem.at[len(acts) + i])
    for m in ORDER:
        for kind, group in (("a", acts), ("r", rights)):
            if m in group:
                loads[kind, m].start()
    kload = pltpu.make_async_copy(kern_in, stg, ksem)
    kload.start()
    bar = pltpu.get_barrier_semaphore()
    for d in [core, xn, yn] + [zdev(k) for k in (1, 2, 3)]:
        pl.semaphore_signal(bar, inc=1, device_id=d, device_id_type=MESH)
    pl.semaphore_wait(bar, 6)

    def rc(a_ref, b_ref, s1, s2, dev):
        return pltpu.make_async_remote_copy(src_ref=a_ref, dst_ref=b_ref, send_sem=s1, recv_sem=s2, device_id=dev, device_id_type=MESH)

    g = GEOM
    units = [(m, k) for m in FIRST_Z for k in (1, 2, 3)]
    for m in ORDER:
        if m == ORDER[-2]:
            units += [(w, 0) for w in FIRST_Z]
        if m not in FIRST_Z:
            units += [(m, k) for k in (1, 2, 3, 0)]
    at = {m: j for j, m in enumerate(ORDER)}
    A, X, Y, C, waited, left_behind = {}, {}, {}, {}, set(), set()

    def ready(kind, m):
        if (kind, m) not in waited:
            waited.add((kind, m))
            loads[kind, m].wait()

    def so(k, other):
        base = lax.rem(s + 2 * k, 8)
        return base + 1 - 2 * c if other else base

    def product(m, shard, put):
        R, cols = P[m].shape[-2:]
        step = 768 if R <= 192 else 384
        left = act[m].at[shard]

        @pl.loop(0, cols // step)
        def _(j):
            at_cols = pl.ds(pl.multiple_of(j * step, 128), step)
            put(at_cols, jnp.dot(left[...], right[m][:, at_cols], preferred_element_type=jnp.float32))

    def stA(i):
        m, k = units[i]
        j = at[m]
        if m == "kern":
            if k == 1:
                kload.wait()
            A[i] = rc(stg.at[so(k, True)], P[m].at[k], as_.at[j, k], ar.at[j, k], core)
        else:
            ready("a", m)
            ready("r", m)
            back = [u for u in range(i) if units[u][0] != "kern" and (units[u][0] in FIRST_Z) == (m in FIRST_Z)]
            if len(back) >= DEPTH:
                A[back[-DEPTH]].wait_send()
                left_behind.discard(back[-DEPTH])
            slot = len(back) % DEPTH
            R, cols = P[m].shape[-2:]
            buf = (snd2 if m in FIRST_Z else snd).at[slot, pl.ds(0, R), pl.ds(0, cols)]

            def put(cs_, t):
                buf[:, cs_] = t.astype(jnp.bfloat16)

            product(m, so(k, True), put)
            A[i] = rc(buf, P[m].at[k], as_.at[j, k], ar.at[j, k], core)
        left_behind.add(i)
        A[i].start()

    def stB(i):
        m, k = units[i]
        j = at[m]
        A[i].wait_recv()
        p = P[m].at[k]
        if m == "kern":
            add_into(p, [stg.at[so(k, False)]])
        else:
            def put(cs_, t):
                p[:, cs_] = (p[:, cs_].astype(jnp.float32) + t).astype(jnp.bfloat16)

            product(m, so(k, False), put)
        if m in FIRST_Z:
            if k:
                C[i] = rc(p, bc[m].at[k - 1], cs.at[j, k - 1], cr.at[j, k - 1], zdev(k))
                C[i].start()
                return
            for w in (1, 2, 3):
                C[units.index((m, w))].wait_recv()
            add_into(p, [bc[m].at[w] for w in range(3)])
        X[i, 1] = rc(cut(p, g[m], qd, 0), bx[m].at[k, 1], xs.at[j, k, 1], xr.at[j, k, 1], xn)
        X[i, 0] = rc(cut(p, g[m], qx, 0), bx[m].at[k, 0], xs.at[j, k, 0], xr.at[j, k, 0], xn)
        Y[i, 1] = rc(cut(p, g[m], qd, 1), by[m].at[k, 1], ys.at[j, k, 1], yr.at[j, k, 1], yn)
        Y[i, 0] = rc(cut(p, g[m], qy, 1), by[m].at[k, 0], ys.at[j, k, 0], yr.at[j, k, 0], yn)
        for w in (1, 0):
            X[i, w].start()
            Y[i, w].start()

    def stC(i):
        m, k = units[i]
        if m in FIRST_Z and k:
            return
        j = at[m]
        p = P[m].at[k]
        X[i, 1].wait_recv()
        add_into(cut(p, g[m], qy, 0), [bx[m].at[k, 1]])
        Y[i, 2] = rc(cut(p, g[m], qy, 0), by[m].at[k, 2], ys.at[j, k, 2], yr.at[j, k, 2], yn)
        Y[i, 2].start()
        Y[i, 1].wait_recv()
        add_into(cut(p, g[m], qx, 1), [by[m].at[k, 1]])
        X[i, 2] = rc(cut(p, g[m], qx, 1), bx[m].at[k, 2], xs.at[j, k, 2], xr.at[j, k, 2], xn)
        X[i, 2].start()

    def stD(i):
        m, k = units[i]
        if m in FIRST_Z and k:
            return
        j = at[m]
        p = P[m].at[k]
        X[i, 0].wait_recv()
        Y[i, 2].wait_recv()
        add_into(cut(p, g[m], q, 0), [bx[m].at[k, 0], by[m].at[k, 2]])
        Y[i, 0].wait_recv()
        X[i, 2].wait_recv()
        add_into(cut(p, g[m], q, 1), [by[m].at[k, 0], bx[m].at[k, 2]])
        if k:
            C[i] = rc(cut(p, g[m], q), bc[m].at[k - 1], cs.at[j, k - 1], cr.at[j, k - 1], zdev(k))
            C[i].start()

    ag = {}

    def stE(m):
        j = at[m]
        p = cut(P[m].at[0], g[m], q)
        if m not in FIRST_Z:
            for k in (1, 2, 3):
                C[units.index((m, k))].wait_recv()
            add_into(p, [bc[m].at[w] for w in range(3)])
        own = out[m] if m == "kern" else cut(out[m], g[m], q)
        ag[m, "o"] = pltpu.make_async_copy(p, own, osem.at[j])
        ag[m, "o"].start()
        if m != "kern":
            ag[m, "x"] = rc(p, own, gxs.at[j], gxr.at[j], xn)
            ag[m, "y"] = rc(p, own, gys.at[j], gyr.at[j], yn)
            ag[m, "x"].start()
            ag[m, "y"].start()

    def stF(m):
        if m == "kern":
            return
        j = at[m]
        ag[m, "x"].wait_recv()
        b = cut(out[m], g[m], qx, 0)
        ag[m, "fy"] = rc(b, b, hys.at[j], hyr.at[j], yn)
        ag[m, "fy"].start()
        ag[m, "y"].wait_recv()
        b = cut(out[m], g[m], qy, 1)
        ag[m, "fx"] = rc(b, b, hxs.at[j], hxr.at[j], xn)
        ag[m, "fx"].start()

    nload = pltpu.make_async_copy(norm_in, nbuf.at[0], ns.at[6])
    nload.start()
    N = {}

    def norm_step(w):
        if w == 0:
            nload.wait()
            N[0] = rc(nbuf.at[0], nbuf.at[1], ns.at[0], nr.at[0], core)
            N[0].start()
        elif w in (1, 2):
            N[w - 1].wait()
            nbuf[0] = nbuf[0] + nbuf[w]
            N[w] = rc(nbuf.at[0], nbuf.at[w + 1], ns.at[w], nr.at[w], xn if w == 1 else yn)
            N[w].start()
        elif w == 3:
            N[2].wait()
            nbuf[0] = nbuf[0] + nbuf[3]
            for k in (1, 2, 3):
                N[2 + k] = rc(nbuf.at[0, so(k, False)], nbuf.at[4, k], ns.at[2 + k], nr.at[2 + k], zdev(k))
                N[2 + k].start()
        elif w == 4:
            for k in (1, 2, 3):
                N[2 + k].wait()
            nbuf[4, 0] = nbuf[0, s] + nbuf[4, 1] + nbuf[4, 2] + nbuf[4, 3]
            N[6] = pltpu.make_async_copy(nbuf.at[4, 0], norm_out, ns.at[7])
            N[6].start()

    n = len(units)
    ahead = DEPTH - 1
    for i in range(ahead):
        stA(i)
    for t in range(n + LE + 6):
        if t < n:
            if t + ahead < n:
                stA(t + ahead)
            stB(t)
        if 0 <= t - LC < n:
            stC(t - LC)
        if 0 <= t - LD < n:
            stD(t - LD)
        for j in range(n):
            m, k = units[j]
            wait = LATE if m in ORDER[1:-2] and m not in FIRST_Z else LE
            if k == 0 and t == j + wait:
                stE(m)
            if k == 0 and t == j + wait + 2:
                stF(m)
        if t >= 4 and t % 2 == 0 and t // 2 - 2 < 5:
            norm_step(t // 2 - 2)
    for m in ORDER:
        if m != "kern":
            for w in ("fx", "fy"):
                ag[m, w].wait()
            for w in ("x", "y"):
                ag[m, w].wait_send()
        ag[m, "o"].wait()
    N[6].wait()
    for i in sorted(left_behind):
        A[i].wait_send()
    for d in (X, Y, C):
        for v in d.values():
            v.wait_send()


LC, LD, LE, LATE = 1, 2, 3, 6


def half_shape(m, R, C):
    return (R // 2, C // 4) if GEOM[m] == "col" else (R // 8, C)


def quarter_shape(m, R, C):
    return (R, C // 4) if GEOM[m] == "col" else (R // 4, C)


def reduce_gradients(act, right, kern, norm):
    D = pltpu.SemaphoreType.DMA
    V = lambda sh: pltpu.VMEM(sh, jnp.bfloat16)
    shp = {m: kern.shape[1:] if m == "kern" else (act[m].shape[1], right[m].shape[1]) for m in ORDER}
    n = len(ORDER)
    acts, rights = tuple(act), tuple(right)
    any_ = pl.BlockSpec(memory_space=pl.ANY)
    snd = max(shp[m][0] for m in acts if m not in FIRST_Z), max(shp[m][1] for m in acts if m not in FIRST_Z)
    snd2 = (16, 128)
    outs = pl.pallas_call(
        functools.partial(grad_kernel, acts, rights),
        out_shape=[jax.ShapeDtypeStruct(quarter_shape(m, *shp[m]) if m == "kern" else shp[m], jnp.bfloat16) for m in ORDER]
        + [jax.ShapeDtypeStruct(norm.shape[1:], jnp.float32)],
        in_specs=[any_] * (len(acts) + len(rights) + 2),
        out_specs=[any_] * (n + 1),
        scratch_shapes=[V(act[m].shape) for m in acts]
        + [V(right[m].shape) for m in rights]
        + [V((4,) + shp[m]) for m in ORDER]
        + [V((1 if m in FIRST_Z else 4, 3) + half_shape(m, *shp[m])) for m in ORDER] * 2
        + [V((3,) + (shp[m] if m in FIRST_Z else quarter_shape(m, *shp[m]))) for m in ORDER]
        + [V((DEPTH,) + snd), V((DEPTH,) + snd2), V(kern.shape), pltpu.VMEM((5,) + norm.shape, jnp.float32)]
        + [D((len(acts) + len(rights),)), D(()), D((n, 4)), D((n, 4))]
        + [D((n, 4, 3))] * 4
        + [D((n, 3))] * 2
        + [D((n,))] * 9
        + [D((8,))] * 2,
        compiler_params=pltpu.CompilerParams(collective_id=1, has_side_effects=True, vmem_limit_bytes=63 * 2**20),
        cost_estimate=pl.CostEstimate(flops=16 * 10**9, bytes_accessed=10**8, transcendentals=0),
    )(*[act[m] for m in acts], *[right[m] for m in rights], kern, norm)
    return dict(zip(ORDER, outs[:-1])), outs[-1]


STEP_A = 32


def mode_powers(rate, freq):
    coarse = (jnp.arange(LONG // STEP_A) * STEP_A).astype(F32)
    fine = jnp.arange(STEP_A).astype(F32)

    def powers(lags):
        size = jnp.exp(-rate[:, None, :] * lags[None, :, None])
        turn = freq[:, None, :] * lags[None, :, None]
        return size * jnp.cos(turn), size * jnp.sin(turn)

    return powers(coarse), powers(fine)


def make_kernels(coef, rate, freq):
    (ar, ai), (br, bi) = mode_powers(rate, freq)
    weight = (coef * jnp.sqrt(rate))[:, None, :]
    left = jnp.concatenate([weight * ar, -weight * ai], -1)
    right = jnp.concatenate([br, bi], -1)
    rows = jnp.einsum("ran,rbn->rab", left, right, precision=HIGHEST, preferred_element_type=F32)
    return rows.reshape(rows.shape[0], LONG)


def pull_kernels(grad, coef, rate, freq):
    (ar, ai), (br, bi) = mode_powers(rate, freq)
    rows = grad.reshape(grad.shape[0], LONG // STEP_A, STEP_A)
    lags = jnp.arange(LONG).astype(F32).reshape(LONG // STEP_A, STEP_A)
    both = jnp.concatenate([rows, rows * lags[None]], 1)
    fine = jnp.concatenate([br, bi], -1)
    inner = jnp.einsum("rab,rbn->ran", both, fine, precision=HIGHEST, preferred_element_type=F32)
    n = rate.shape[-1]
    a = LONG // STEP_A
    zero_r, zero_i = inner[:, :a, :n], inner[:, :a, n:]
    one_r, one_i = inner[:, a:, :n], inner[:, a:, n:]
    plain = jnp.sum(ar * zero_r - ai * zero_i, 1)
    lag_r = jnp.sum(ar * one_r - ai * one_i, 1)
    lag_i = jnp.sum(ar * one_i + ai * one_r, 1)
    root = jnp.sqrt(rate)
    return root * plain, coef * (plain / (2 * root) - root * lag_r), -coef * root * lag_i


def dot_plain(left_side, right_side):
    return jnp.dot(left_side, right_side, preferred_element_type=F32)


def dot_inner(left_side, right_side):
    return lax.dot_general(left_side, right_side, (((0,), (0,)), ((), ())), preferred_element_type=F32)


def dot_outer(left_side, right_side):
    return lax.dot_general(left_side, right_side, (((1,), (1,)), ((), ())), preferred_element_type=F32)


def layer_norm(rows, gain, bias):
    centre = jnp.mean(rows, axis=-1, keepdims=True)
    shifted = rows - centre
    spread = jnp.mean(shifted * shifted, axis=-1, keepdims=True)
    return shifted * lax.rsqrt(spread + EPSILON) * gain + bias


def shift(array, by, count):
    pairs = [(i, i + by) for i in range(count) if 0 <= i + by < count]
    return lax.ppermute(array, "seq", pairs)


def from_left(array, count):
    return [shift(array[:, BLK:], 2, count), shift(array, 1, count)]


def from_right(array, count):
    return [shift(array, -1, count), shift(array[:, :BLK], -2, count)]


def same_item(lengths, own_blocks, count):
    starts = jnp.cumsum(lengths, axis=1) - lengths
    total = own_blocks * count
    places = jnp.arange(total) * BLK
    present = (starts[:, None, :] <= places[None, :, None]) & (lengths[:, None, :] > 0)
    owner = jnp.sum(present.astype(jnp.int32), -1)
    first = lax.axis_index("seq") * own_blocks
    padded = jnp.pad(owner, ((0, 0), (REACH, REACH)), constant_values=-1)
    near = lax.dynamic_slice_in_dim(padded, first, own_blocks + 2 * REACH, 1)
    return jnp.stack(
        [
            jnp.stack([(near[:, o + REACH] == near[:, o + REACH + e]) for e in range(-REACH, REACH + 1)], -1)
            for o in range(own_blocks)
        ],
        1,
    ).astype(F32)


def shards(
    n_dp,
    n_seq,
    tokens,
    cotangent,
    lengths,
    ln_gain,
    ln_bias,
    w_value,
    w_filter,
    w_fore,
    w_back,
    w_out,
    ssm_coef,
    ssm_rate,
    ssm_freq,
):
    linked = n_dp == 4 and n_seq == 8
    micros, rows_each, width = tokens.shape
    rows = micros * rows_each
    channels = ssm_coef.shape[1]
    modes = ssm_coef.shape[2]
    parts = 4 if linked else 1
    some = channels // parts
    first = lax.axis_index("dp") * some if linked else 0

    def mine(array):
        return lax.dynamic_slice_in_dim(array, first, some, 1).reshape(2 * some, modes)

    coef, rate, freq = mine(ssm_coef), mine(ssm_rate), mine(ssm_freq)
    kernels = make_kernels(coef, rate, freq).astype(LOW)
    mask = same_item(lengths[:, 0], rows_each // BLK, n_seq).reshape(-1)
    wave = jnp.asarray(wave_tables(), LOW)
    tile_step = max(1, 384 // channels)
    cot_rows = cotangent.reshape(rows, width)
    token_rows = tokens.reshape(rows, width).astype(F32)
    if linked:
        pack = jnp.pad(jnp.stack([ln_gain, ln_bias]), ((0, 14), (0, 128 - ln_gain.shape[0])))
        own = {"norm": pack, "filter": w_filter, "kern": kernels, "value": w_value, "fore": w_fore, "back": w_back, "out": w_out}
        gathered, made = gather_forward(mask, tokens.reshape(rows, width), cot_rows, own)
        pre_filter, filter_near, fore_low, back_low, hidden_low, grad_proj_fore, grad_proj_back, grad_pre_value, normed_low = made
        kern = gathered.pop("kern").reshape(n_seq, parts, 2, some, LONG)
        norm = gathered.pop("norm")[:, :2, : ln_gain.shape[0]].astype(F32)
        gain, bias = norm[:, 0].reshape(-1), norm[:, 1].reshape(-1)
        full = {m: a.reshape(-1, a.shape[-1]) for m, a in gathered.items()}
        around = [filter_near]
    else:
        own = {"filter": w_filter, "value": w_value, "fore": w_fore, "back": w_back, "out": w_out}
        full = {m: lax.all_gather(a, "seq", axis=0, tiled=True) for m, a in own.items()}
        kern = lax.all_gather(kernels.reshape(1, 2, some, LONG), "seq", axis=0)
        gain = lax.all_gather(ln_gain, "seq", axis=0, tiled=True).astype(F32)
        bias = lax.all_gather(ln_bias, "seq", axis=0, tiled=True).astype(F32)
        normed_low = layer_norm(token_rows, gain, bias).astype(LOW)
        pre_filter = dot_plain(normed_low, full["filter"])
        filter_low = jax.nn.gelu(pre_filter).astype(LOW).reshape(micros, rows_each, -1)
        around = from_left(filter_low, n_seq) + [filter_low] + from_right(filter_low, n_seq)
        pre_value = dot_plain(normed_low, full["value"])
        value_act, value_pull = jax.vjp(jax.nn.gelu, pre_value)
        fore_low, back_low = [a.reshape(rows, -1) for a in conv_forward(mask, wave, kern, around, tile_step)]
        proj_fore = dot_plain(fore_low, full["fore"])
        proj_back = dot_plain(back_low, full["back"])
        hidden_low = (proj_fore * proj_back * value_act).astype(LOW)
        grad_hidden = dot_outer(cot_rows, full["out"])
        grad_proj_fore = (grad_hidden * proj_back * value_act).astype(LOW)
        grad_proj_back = (grad_hidden * proj_fore * value_act).astype(LOW)
        grad_pre_value = value_pull(grad_hidden * proj_fore * proj_back)[0].astype(LOW)
    filter_pull = jax.vjp(jax.nn.gelu, pre_filter)[1]
    norm_pull = jax.vjp(layer_norm, token_rows, gain, bias)[1]
    mixed = (token_rows + dot_plain(hidden_low, full["out"])).astype(LOW).reshape(tokens.shape)

    grad_fore_low = dot_outer(grad_proj_fore, full["fore"]).astype(LOW).reshape(micros, rows_each, -1)
    grad_back_low = dot_outer(grad_proj_back, full["back"]).astype(LOW).reshape(micros, rows_each, -1)
    fore_around = [grad_fore_low] + from_right(grad_fore_low, n_seq)
    back_around = from_left(grad_back_low, n_seq) + [grad_back_low]
    grad_filter_low, grad_kern = conv_backward(mask, wave, kern, around, fore_around, back_around, tile_step)
    grad_pre_filter = filter_pull(grad_filter_low.reshape(rows, -1).astype(F32))[0].astype(LOW)
    grad_normed = dot_outer(grad_pre_value, full["value"]) + dot_outer(grad_pre_filter, full["filter"])
    grad_rows, gain_grad, bias_grad = norm_pull(grad_normed)
    grad_tokens = (cot_rows.astype(F32) + grad_rows).astype(LOW).reshape(tokens.shape)

    left = {"out": hidden_low, "fore": fore_low, "back": back_low, "value": normed_low, "filter": normed_low}
    right = {"out": cot_rows, "fore": grad_proj_fore, "back": grad_proj_back, "value": grad_pre_value, "filter": grad_pre_filter}
    grad_kern = grad_kern.reshape(n_seq, -1, LONG)
    norm_grads = jnp.stack([gain_grad, bias_grad]).reshape(2, n_seq, -1)
    if linked:
        pack = jnp.pad(jnp.swapaxes(norm_grads, 0, 1), ((0, 0), (0, 6), (0, 128 - norm_grads.shape[2])))
        left = {m: jnp.transpose(a).reshape(n_seq, -1, rows) for m, a in left.items()}
        sums, norm_grads = reduce_gradients(left, right, grad_kern, pack)
        norm_grads = norm_grads[:2, : ln_gain.shape[0]]
    else:
        grads = {m: dot_inner(left[m], right[m]).reshape(n_seq, -1, right[m].shape[1]) for m in left}
        grads["kern"] = grad_kern.astype(F32)
        sums = {m: lax.psum_scatter(a, "seq", scatter_dimension=0, tiled=False) for m, a in grads.items()}
        sums = {m: lax.psum(a, "dp") for m, a in sums.items()}
        norm_grads = lax.psum_scatter(norm_grads, "seq", scatter_dimension=1, tiled=False)
        norm_grads = lax.psum(norm_grads, "dp")
    modes_grad = jnp.stack(pull_kernels(sums["kern"].astype(F32), coef, rate, freq)).reshape(3, 2, some, modes)
    if linked:
        modes_grad, sums = lax.optimization_barrier((modes_grad, sums))
        sums = {m: a.astype(F32) for m, a in sums.items()}
        column = lax.axis_index("dp")
        hand = [modes_grad] + [lax.ppermute(modes_grad, "dp", [(i, i ^ w) for i in range(n_dp)]) for w in (1, 2, 3)]
        odd, high = column % 2 == 1, column >= 2
        hand = [jnp.where(odd, hand[w ^ 1], hand[w]) for w in range(4)]
        hand = [jnp.where(high, hand[w ^ 2], hand[w]) for w in range(4)]
        modes_grad = jnp.concatenate(hand, 2)
    return (
        mixed,
        grad_tokens,
        norm_grads[0],
        norm_grads[1],
        sums["value"],
        sums["filter"],
        sums["fore"],
        sums["back"],
        sums["out"],
        modes_grad[0],
        modes_grad[1],
        modes_grad[2],
    )


def solution(mesh):
    rows = P("seq", None)
    modes = P(None, "seq", None)
    tokens = P(None, ("dp", "seq"), None)
    return jax.shard_map(
        functools.partial(shards, mesh.shape["dp"], mesh.shape["seq"]),
        mesh=mesh,
        in_specs=(tokens, tokens, P(None, "dp", None), P("seq"), P("seq")) + (rows,) * 5 + (modes,) * 3,
        out_specs=(tokens, tokens, P("seq"), P("seq")) + (rows,) * 5 + (modes,) * 3,
        check_vma=False,
    )
```

```python
import functools

import numpy as np

import jax
import jax.numpy as jnp
from jax import lax
from jax.experimental import pallas as pl
from jax.experimental.pallas import tpu as pltpu
from jax.sharding import PartitionSpec as P

MESH = pl.DeviceIdType.MESH
LONG = 512
EPSILON = 1e-05
HIGHEST = lax.Precision.HIGHEST
LOW = jnp.bfloat16
F32 = jnp.float32


BLK = 128
REACH = 3


def wave_tables():
    k = np.arange(BLK)[:, None] + 0.5
    n = np.arange(-BLK, BLK)[None, :]
    angle = 2 * np.pi * k * n / (2 * BLK)
    return np.concatenate([np.cos(angle), -np.sin(angle)], 0).astype(np.float32)


def dot(a, b, ca, cb):
    return lax.dot_general(a, b, (((ca,), (cb,)), ((), ())), preferred_element_type=jnp.float32)


def kernel_spectra(wave_ref, kern_ref, spec_ref, tile):
    for side in range(2):
        rows = jnp.concatenate([kern_ref[a, b, side] for a in range(kern_ref.shape[0]) for b in range(kern_ref.shape[1])], 0)
        spec_ref[side, 0] = dot(wave_ref[:, BLK:], rows[:, :BLK], 1, 1)
        for d in range(1, REACH + 1):
            spec_ref[side, d] = dot(wave_ref[...], rows[:, (d - 1) * BLK:(d + 1) * BLK], 1, 1)


def block_of(parts, micro, at):
    for p in parts:
        n = p.shape[1] // BLK
        if at < n:
            return p[micro, at * BLK:(at + 1) * BLK]
        at -= n


def fore_kernel(mask_ref, wave_ref, kern_ref, *refs):
    parts = refs[:5]
    fore_ref, back_ref, spec_ref, x_ref, y_ref = refs[5:]
    tile = fore_ref.shape[-1]
    kernel_spectra(wave_ref, kern_ref, spec_ref, tile)
    fwd = wave_ref[:, BLK:]
    for micro in range(2):
        for b in range(8):
            x_ref[b] = dot(fwd, block_of(parts, micro, b), 1, 0)

        @pl.loop(0, BLK // 8)
        def _(r):
            re = pl.ds(pl.multiple_of(r * 8, 8), 8)
            im = pl.ds(pl.multiple_of(r * 8 + BLK, 8), 8)
            for lane in range(tile // 128):
                ln = slice(lane * 128, lane * 128 + 128)
                xr = [x_ref[b, re, ln] for b in range(8)]
                xi = [x_ref[b, im, ln] for b in range(8)]
                for side in range(2):
                    cr = [spec_ref[side, d, re, ln] for d in range(4)]
                    ci = [spec_ref[side, d, im, ln] for d in range(4)]
                    for own in range(2):
                        yr = yi = None
                        for d in range(4):
                            at = own + 3 + (d if side else -d)
                            pr = cr[d] * xr[at]
                            pi = cr[d] * xi[at]
                            qr = ci[d] * xi[at]
                            qi = ci[d] * xr[at]
                            if side:
                                tr, ti = pr + qr, pi - qi
                            else:
                                tr, ti = pr - qr, pi + qi
                            if d:
                                m = mask_ref[(micro * 2 + own) * 7 + 3 + (d if side else -d)]
                                tr, ti = tr * m, ti * m
                            yr = tr if yr is None else yr + tr
                            yi = ti if yi is None else yi + ti
                        y_ref[side, own, re, ln] = yr
                        y_ref[side, own, im, ln] = yi
        for own in range(2):
            for side, o in ((0, fore_ref), (1, back_ref)):
                y = dot(fwd, y_ref[side, own].astype(jnp.bfloat16), 0, 0)
                o[micro, own * BLK:(own + 1) * BLK] = (y * (1.0 / BLK)).astype(jnp.bfloat16)


def back_kernel(mask_ref, wave_ref, kern_ref, *refs):
    parts = refs[:-14]
    fparts = refs[-14:-11]
    bparts = refs[-11:-8]
    gfil_ref, gk_ref, spec_ref, x_ref, f_ref, b_ref, y_ref, r_ref = refs[-8:]
    tile = gfil_ref.shape[-1]
    kernel_spectra(wave_ref, kern_ref, spec_ref, tile)
    fwd = wave_ref[:, BLK:]
    for micro in range(2):
        for b in range(8):
            x_ref[b] = dot(fwd, block_of(parts, micro, b), 1, 0)
        for b in range(5):
            f_ref[b] = dot(fwd, block_of(fparts, micro, b), 1, 0)
            b_ref[b] = dot(fwd, block_of(bparts, micro, b), 1, 0)

        @pl.loop(0, BLK // 8)
        def _(r):
            re = pl.ds(pl.multiple_of(r * 8, 8), 8)
            im = pl.ds(pl.multiple_of(r * 8 + BLK, 8), 8)
            for lane in range(tile // 128):
                ln = slice(lane * 128, lane * 128 + 128)
                fr = [f_ref[b, re, ln] for b in range(5)]
                fi = [f_ref[b, im, ln] for b in range(5)]
                gr = [b_ref[b, re, ln] for b in range(5)]
                gi = [b_ref[b, im, ln] for b in range(5)]
                acc = [[None, None], [None, None]]
                for d in range(4):
                    for side in range(2):
                        cr = spec_ref[side, d, re, ln]
                        ci = spec_ref[side, d, im, ln]
                        for own in range(2):
                            if side == 0:
                                vr, vi = fr[own + d], fi[own + d]
                                tr, ti = cr * vr + ci * vi, cr * vi - ci * vr
                                e = d
                            else:
                                vr, vi = gr[own + 3 - d], gi[own + 3 - d]
                                tr, ti = cr * vr - ci * vi, cr * vi + ci * vr
                                e = -d
                            if d:
                                m = mask_ref[(micro * 2 + own) * 7 + 3 + e]
                                tr, ti = tr * m, ti * m
                            a = acc[own]
                            acc[own] = [tr if a[0] is None else a[0] + tr, ti if a[1] is None else a[1] + ti]
                for own in range(2):
                    y_ref[own, re, ln] = acc[own][0]
                    y_ref[own, im, ln] = acc[own][1]
                for side in range(2):
                    for d in range(4):
                        sr = si = None
                        for own in range(2):
                            e = d if side else -d
                            xr, xi = x_ref[own + 3 + e, re, ln], x_ref[own + 3 + e, im, ln]
                            if side == 0:
                                vr, vi = fr[own], fi[own]
                                tr, ti = vr * xr + vi * xi, vi * xr - vr * xi
                            else:
                                vr, vi = gr[own + 3], gi[own + 3]
                                tr, ti = vr * xr + vi * xi, vr * xi - vi * xr
                            if d:
                                m = mask_ref[(micro * 2 + own) * 7 + 3 + e]
                                tr, ti = tr * m, ti * m
                            sr = tr if sr is None else sr + tr
                            si = ti if si is None else si + ti
                        if micro:
                            sr = sr + r_ref[side, d, re, ln]
                            si = si + r_ref[side, d, im, ln]
                        r_ref[side, d, re, ln] = sr
                        r_ref[side, d, im, ln] = si
        for own in range(2):
            y = dot(fwd, y_ref[own].astype(jnp.bfloat16), 0, 0)
            gfil_ref[micro, own * BLK:(own + 1) * BLK] = (y * (1.0 / BLK)).astype(jnp.bfloat16)
    A, B = gk_ref.shape[:2]
    for side in range(2):
        rows = [dot(r_ref[side, d].astype(jnp.bfloat16), wave_ref[:, BLK:] if d == 0 else wave_ref[...], 0, 0) for d in range(4)]
        for d in range(4):
            seg = rows[d][:, -BLK:]
            if d < 3:
                seg = seg + rows[d + 1][:, :BLK]
            seg = (seg * (1.0 / BLK)).astype(jnp.bfloat16)
            w = tile // (A * B)
            for a in range(A):
                for b in range(B):
                    at = (a * B + b) * w
                    gk_ref[a, b, side, :, d * BLK:(d + 1) * BLK] = seg[at:at + w]


def _specs(parts, tile):
    return [pl.BlockSpec((2, p.shape[1], tile), lambda i: (0, 0, i)) for p in parts]


def conv_call(body, mask, wave, kern, parts, outs, scratch, step):
    channels = parts[0].shape[-1]
    steps = kern.shape[0] // step
    tile = channels // steps
    kspec = pl.BlockSpec((step,) + kern.shape[1:], lambda i: (i, 0, 0, 0, 0))
    out_specs = []
    for o in outs:
        if len(o.shape) == 3:
            out_specs.append(pl.BlockSpec((2, o.shape[1], tile), lambda i: (0, 0, i)))
        else:
            out_specs.append(kspec)
    return pl.pallas_call(
        body,
        grid=(steps,),
        out_shape=outs,
        in_specs=[pl.BlockSpec(memory_space=pltpu.SMEM), pl.BlockSpec(memory_space=pltpu.VMEM), kspec] + _specs(parts, tile),
        out_specs=out_specs,
        scratch_shapes=[pltpu.VMEM(sh + (tile,), jnp.float32) for sh in scratch],
        compiler_params=pltpu.CompilerParams(vmem_limit_bytes=56 * 2**20),
        cost_estimate=pl.CostEstimate(flops=10**10, bytes_accessed=3 * 10**7, transcendentals=0),
    )(mask, wave, kern, *parts)


def conv_forward(mask, wave, kern, parts, step):
    own = parts[2]
    sh = jax.ShapeDtypeStruct(own.shape, jnp.bfloat16)
    return conv_call(fore_kernel, mask, wave, kern, parts, [sh, sh], [(2, 4, 256), (8, 256), (2, 2, 256)], step)


def conv_backward(mask, wave, kern, parts, fparts, bparts, step):
    own = fparts[0]
    return conv_call(back_kernel, mask, wave, kern, list(parts) + list(fparts) + list(bparts),
                     [jax.ShapeDtypeStruct(own.shape, jnp.bfloat16), jax.ShapeDtypeStruct(kern.shape, jnp.bfloat16)],
                     [(2, 4, 256), (8, 256), (5, 256), (5, 256), (2, 256), (2, 4, 256)], step)


def place(n_z):
    dp = lax.axis_index("dp"); s = lax.axis_index("seq")
    return dp, s, s // 2, lax.rem(s, 2)

def cut(ref, geom, q, h=None):
    kind = geom
    if kind is None:
        return ref
    R, C = ref.shape[-2:]
    if kind == "col":
        cols = pl.ds(pl.multiple_of(q * (C // 4), 128), C // 4)
        rows = slice(None) if h is None else pl.ds(h * (R // 2), R // 2)
        return ref.at[rows, cols]
    if kind == "row":
        n = R // 4
        if h is None:
            return ref.at[pl.ds(pl.multiple_of(q * n, 16), n)]
        return ref.at[pl.ds(pl.multiple_of(q * n + h * (n // 2), 16), n // 2)]

GEOM = {"filter": "col", "kern": "row", "value": "col", "fore": "col", "back": "col", "out": "row", "norm": None}


FETCH = ("norm", "filter", "kern", "fore", "back", "value", "out")
SMALL = ("norm", "kern")
GELU_C = 0.7978845608028654
GELU_D = 0.044715


def gelu_parts(x):
    sq = x * x
    t = jnp.tanh(GELU_C * x * (1.0 + GELU_D * sq))
    half = 0.5 * (1.0 + t)
    return x * half, half + 0.5 * x * (1.0 - t * t) * (GELU_C * (1.0 + 3.0 * GELU_D * sq))


def slab_forward(mask_ref, wave_ref, kr_ref, spec_ref, x_ref, y_ref, fb_ref, outs, chunk):
    rows = slice(None)
    lanes = slice(chunk * 384, chunk * 384 + 384)
    fwd = wave_ref[:, BLK:]
    for side in range(2):
        spec_ref[side, 0] = dot(fwd, kr_ref[side, rows, :BLK], 1, 1)
        for d in range(1, REACH + 1):
            spec_ref[side, d] = dot(wave_ref[...], kr_ref[side, rows, (d - 1) * BLK:(d + 1) * BLK], 1, 1)
    for micro in range(2):
        for b in range(8):
            x_ref[b] = dot(fwd, fb_ref[micro, b * BLK:(b + 1) * BLK, lanes], 1, 0)

        @pl.loop(0, BLK // 16)
        def _(r):
            re = pl.ds(pl.multiple_of(r * 16, 16), 16)
            im = pl.ds(pl.multiple_of(r * 16 + BLK, 16), 16)
            for lane in range(3):
                ln = slice(lane * 128, lane * 128 + 128)
                xr = [x_ref[b, re, ln] for b in range(8)]
                xi = [x_ref[b, im, ln] for b in range(8)]
                for side in range(2):
                    cr = [spec_ref[side, d, re, ln] for d in range(4)]
                    ci = [spec_ref[side, d, im, ln] for d in range(4)]
                    for own in range(2):
                        yr = yi = None
                        for d in range(4):
                            at = own + 3 + (d if side else -d)
                            pr = cr[d] * xr[at]
                            pi = cr[d] * xi[at]
                            qr = ci[d] * xi[at]
                            qi = ci[d] * xr[at]
                            if side:
                                tr, ti = pr + qr, pi - qi
                            else:
                                tr, ti = pr - qr, pi + qi
                            if d:
                                m = mask_ref[(micro * 2 + own) * 7 + 3 + (d if side else -d)]
                                tr, ti = tr * m, ti * m
                            yr = tr if yr is None else yr + tr
                            yi = ti if yi is None else yi + ti
                        y_ref[side, own, re, ln] = yr.astype(jnp.bfloat16)
                        y_ref[side, own, im, ln] = yi.astype(jnp.bfloat16)

        for own in range(2):
            for side in range(2):
                y = dot(fwd, y_ref[side, own], 0, 0)
                at = micro * 256 + own * BLK
                outs[side][at:at + BLK, lanes] = (y * (1.0 / BLK)).astype(jnp.bfloat16)


def forward_kernel(width, mask_ref, *refs):
    refs = list(refs)
    take = lambda n: [refs.pop(0) for _ in range(n)]
    names = FETCH
    n = len(names)
    wave_in, tok_in, cot_in = take(3)
    src = take(n)
    out = take(n)
    pre_out, fb_out, fore_out, back_out, hid_out, gpf_out, gpb_out, gpv_out, nrm_out = take(9)
    stage = dict(zip(SMALL, take(len(SMALL))))
    wave_ref, tok, cot, nv, gb, nl, wa, wb, pf, pv, pk, fb, low_f, low_b, kv, kr, spec, xs_, ys_, ring = take(20)
    isem, lsem, fsem, zs, zr, xs, xr, ys, yr, fxs, fxr, fys, fyr, ss, sr, ss0, sr0, hs, hr, misc, rsem = refs
    dp, s, z, c = place(4)
    core = (dp, s + 1 - 2 * c)
    odd = (dp, lax.rem(s + 7 + 2 * c, 8))
    xn = (dp + 1 - 2 * lax.rem(dp, 2), s)
    yn = (lax.rem(dp + 2, 4), s)
    q = dp
    qx = xn[0]
    qy = yn[0]

    def zdev(k):
        return (dp, lax.rem(s + 2 * k, 8))

    first = {}
    for i, (a, b) in enumerate([(wave_in, wave_ref), (tok_in, tok), (cot_in, cot)]):
        first[i] = pltpu.make_async_copy(a, b, misc.at[i])
        first[i].start()
    lins = {}
    for m in SMALL:
        a = names.index(m)
        lins[a] = pltpu.make_async_copy(src[a], stage[m], isem.at[a])
        lins[a].start()
    halo_rows = 3 * BLK

    @pl.loop(0, halo_rows // 16)
    def _(r):
        lo = pl.ds(pl.multiple_of(r * 16, 16), 16)
        hi = pl.ds(pl.multiple_of(r * 16 + halo_rows + 256, 16), 16)
        zero = jnp.zeros((16, fb.shape[2]), jnp.bfloat16)
        for micro in range(2):
            fb[micro, lo, :] = zero
            fb[micro, hi, :] = zero

    bar = pltpu.get_barrier_semaphore()
    for d in [core, odd, xn, yn, zdev(1), zdev(3)]:
        pl.semaphore_signal(bar, inc=1, device_id=d, device_id_type=MESH)
    pl.semaphore_wait(bar, 6)

    def rc(a_ref, b_ref, s1, s2, dev):
        return pltpu.make_async_remote_copy(src_ref=a_ref, dst_ref=b_ref, send_sem=s1, recv_sem=s2, device_id=dev, device_id_type=MESH)

    g = [GEOM[m] for m in names]
    def place_of(m, shard):
        R = out[names.index(m)].shape[1]
        if m == "filter":
            return wa.at[pl.ds(pl.multiple_of(768 + shard * R, 16), R), pl.ds(0, 1536)]
        if m == "out":
            return wa.at[pl.ds(pl.multiple_of(768 + lax.rem(shard, 2) * R, 16), R), pl.ds(pl.multiple_of(lax.div(shard, 2) * 768, 128), 768)]
        return (wb if m == "back" else wa).at[pl.ds(pl.multiple_of(shard * R, 16), R)]

    locs, own_sib, zsend = [], {}, {}
    for a in range(n):
        where = cut(out[a].at[s], g[a], q) if names[a] == "kern" else out[a].at[s]
        held = stage[names[a]] if names[a] in SMALL else place_of(names[a], s)
        locs.append(pltpu.make_async_copy(held, where, lsem.at[a]))

    def near(way, j):
        return lax.rem(s + (8 - 2 * j if way == 0 else 2 * j), 8)

    def here(u):
        a, way, j = u
        return True if j == 0 else (z >= j if way == 0 else z + j <= 3)

    def when(cond, f):
        if cond is True:
            f()
        else:
            pl.when(cond)(f)

    def onward(way):
        return z < 3 if way == 0 else z > 0

    def zgo(a):
        if a < n:
            for way in (0, 1):
                pl.when(onward(way))(zsend[a, way, 0].start)

    def sibgo(a):
        if a < n and names[a] != "kern":
            own_sib[a] = rc(src[a], out[a].at[s], ss0.at[a], sr0.at[a], core)
            own_sib[a].start()

    units = []
    for a in range(n):
        if names[a] == "kern":
            units.append((a, 0, 0))
        for j in (1, 2, 3):
            units += [(a, 0, j), (a, 1, j)]
    last_unit = {u[0]: i for i, u in enumerate(units)}
    xc, yc, fx, fy, sb = {}, {}, {}, {}, {}
    loc_done = set()

    def slot(u):
        return 6 if u[2] == 0 else u[1] * 3 + u[2] - 1

    def blk(u):
        return out[u[0]].at[s if u[2] == 0 else near(u[1], u[2])]

    for a in range(n):
        for way in (0, 1):
            for j in range(3):
                if j:
                    piece = cut(blk((a, way, j)), g[a], q)
                else:
                    piece = src[a] if names[a] == "kern" else cut(src[a], g[a], q)
                there = cut(out[a].at[near(way, j)], g[a], q)
                zsend[a, way, j] = rc(piece, there, zs.at[a, way * 3 + j], zr.at[a, way * 3 + j], zdev(1 if way == 0 else 3))
    zin = {}
    for u in units:
        a, i = u[0], slot(u)
        whole = blk(u)
        b = cut(whole, g[a], q)
        if u[2]:
            zin[u] = rc(b, b, zs.at[a, i], zr.at[a, i], zdev(1))
        if g[a] is not None:
            xc[u] = rc(b, b, xs.at[a, i], xr.at[a, i], xn)
            yc[u] = rc(b, b, ys.at[a, i], yr.at[a, i], yn)
            b = cut(whole, g[a], qx, 0)
            fy[u] = rc(b, b, fys.at[a, i], fyr.at[a, i], yn)
            b = cut(whole, g[a], qy, 1)
            fx[u] = rc(b, b, fxs.at[a, i], fxr.at[a, i], xn)
        sb[u] = rc(whole, whole, ss.at[a, i], sr.at[a, i], core)

    zgo(0)
    zgo(1)
    sibgo(0)
    sibgo(1)
    for a in lins:
        lins[a].wait()
        locs[a].start()

    def st0(u):
        a, way, j = u
        if j == 0:
            locs[a].wait()
            loc_done.add(a)
        else:
            zin[u].wait_recv()
            if j < 3:
                pl.when(onward(way))(zsend[a, way, j].start)

    def st1(u):
        if u in xc:
            xc[u].start()
            yc[u].start()

    def st2(u):
        if u in xc:
            xc[u].wait_recv()
            fy[u].start()
            yc[u].wait_recv()
            fx[u].start()

    def st3(u):
        if u in xc:
            fx[u].wait_recv()
            fy[u].wait_recv()
        sb[u].start()

    loaded = {}
    for u in units:
        a = u[0]
        if names[a] in ("filter", "value", "out", "fore", "back"):
            shard = near(u[1], u[2])
            other = shard + 1 - 2 * c
            for w, sh in ((0, shard), (1, other)):
                loaded[u, w] = pltpu.make_async_copy(out[a].at[sh], place_of(names[a], sh), fsem.at[a, slot(u), w])
    for a in range(n):
        if names[a] in ("filter", "value", "out", "fore", "back"):
            for w, sh in ((0, s), (1, s + 1 - 2 * c)):
                origin = src[a] if w == 0 else out[a].at[sh]
                loaded[(a, 0, 0), w] = pltpu.make_async_copy(origin, place_of(names[a], sh), fsem.at[a, 6, w])

    def st4(u):
        sb[u].wait_recv()
        for w in (0, 1):
            if (u, w) in loaded:
                assert names[u[0]] not in ("value", "out") or state["free"]
                loaded[u, w].start()

    state = {"t": 0, "free": False}

    def comm():
        t = state["t"]
        state["t"] += 1
        for lag, stage_of in ((0, st0), (L1, st1), (L2, st2), (L3, st3), (L4, st4)):
            if 0 <= t - lag < len(units):
                u = units[t - lag]
                when(here(u), functools.partial(stage_of, u))
        if t < len(units) and t == last_unit[units[t][0]]:
            zgo(units[t][0] + 2)
            sibgo(units[t][0] + 2)

    def complete(name):
        a = names.index(name)
        while state["t"] <= last_unit[a] + L4:
            comm()
        if a not in loc_done and name in SMALL:
            locs[a].wait()
        if a in own_sib:
            own_sib[a].wait_recv()
        own = (a, 0, 0)
        for w in (0, 1):
            if (own, w) in loaded:
                loaded[own, w].start()
        for u in [own] + [u for u in units if u[0] == a]:
            for w in (0, 1):
                if (u, w) in loaded:
                    when(here(u), loaded[u, w].wait)
        if name not in SMALL:
            locs[a].start()
            locs[a].wait()
        return a

    def fetch(pairs, sem0):
        cps = [pltpu.make_async_copy(x, y, misc.at[sem0 + i]) for i, (x, y) in enumerate(pairs)]
        for cp in cps:
            cp.start()
        for cp in cps:
            cp.wait()

    for i in range(3):
        first[i].wait()
    a = complete("norm")
    fetch([(out[a], nv)], 3)
    rows2 = jnp.zeros((16, width), jnp.float32)
    piece = width // 8
    for j in range(8):
        r_ = lax.broadcasted_iota(jnp.int32, (128, width), 0)
        c_ = lax.broadcasted_iota(jnp.int32, (128, width), 1)
        spread = jnp.where((c_ == r_ + j * piece) & (r_ < piece), 1.0, 0.0).astype(jnp.bfloat16)
        rows2 = rows2 + jnp.dot(nv[j], spread, preferred_element_type=jnp.float32)
    gb[...] = rows2

    @pl.loop(0, 512 // 64)
    def _(r):
        rows = pl.ds(pl.multiple_of(r * 64, 64), 64)
        x = tok[rows, :].astype(jnp.float32)
        x = x - jnp.mean(x, axis=-1, keepdims=True)
        var = jnp.mean(x * x, axis=-1, keepdims=True)
        nl[rows, :] = (x * lax.rsqrt(var + 1e-5) * gb[0:1, :] + gb[1:2, :]).astype(jnp.bfloat16)

    nout = pltpu.make_async_copy(nl, nrm_out, misc.at[4])
    nout.start()

    a = complete("filter")

    @pl.loop(0, 3)
    def _(j):
        cols = pl.ds(pl.multiple_of(j * 512, 128), 512)
        t = jnp.dot(nl[...], wa[768:1536, cols], preferred_element_type=jnp.float32)
        pf[:, cols] = t
        act = gelu_parts(t)[0].astype(jnp.bfloat16)
        for micro in range(2):
            fb[micro, halo_rows:halo_rows + 256, cols] = act[micro * 256:(micro + 1) * 256]

    pre_cp = pltpu.make_async_copy(pf.at[:, pl.ds(0, 1536)], pre_out, misc.at[13])
    pre_cp.start()
    own_rows = pl.ds(halo_rows, 256)
    halos = [
        (1, own_rows, pl.ds(BLK, 256), s < 7, s > 0),
        (2, pl.ds(halo_rows + BLK, BLK), pl.ds(0, BLK), s < 6, s > 1),
        (-1, own_rows, pl.ds(halo_rows + 256, 256), s > 0, s < 7),
        (-2, pl.ds(halo_rows, BLK), pl.ds(halo_rows + 512, BLK), s > 1, s < 6),
    ]
    hcps = {}
    for chunk in range(4):
        cols = pl.ds(chunk * 384, 384)
        for i, (by, from_rows, to_rows, sends, recvs) in enumerate(halos):
            cp = rc(fb.at[:, from_rows, cols], fb.at[:, to_rows, cols], hs.at[chunk, i], hr.at[chunk, i], (dp, lax.rem(s + 8 + by, 8)))
            hcps[chunk, i] = (cp, sends, recvs)

    def halo_go(chunk):
        for i in range(4):
            cp, sends, _ = hcps[chunk, i]
            pl.when(sends)(cp.start)

    def halo_here(chunk):
        for i in range(4):
            cp, _, recvs = hcps[chunk, i]
            pl.when(recvs)(cp.wait_recv)

    halo_go(0)


    def conv_chunk(chunk):
        halo_here(chunk)
        a = names.index("kern")
        fetch([(out[a].at[pl.ds(2 * chunk, 2)], kv)], 3)
        for side in range(2):
            for j in range(2):
                for p in range(4):
                    at = (j * 4 + p) * 48
                    kr[side, at:at + 48] = kv[j, (p * 2 + side) * 48:(p * 2 + side + 1) * 48]

        slab_forward(mask_ref, wave_ref, kr, spec, xs_, ys_, fb, (low_f, low_b), chunk)

    complete("kern")
    halo_go(1)
    comm()
    halo_go(2)
    conv_chunk(0)
    comm()
    comm()
    halo_go(3)
    conv_chunk(1)
    comm()
    comm()
    conv_chunk(2)
    comm()
    comm()
    conv_chunk(3)
    complete("fore")
    fb_cp = pltpu.make_async_copy(fb, fb_out, misc.at[14])
    fb_cp.start()
    low_cp = [pltpu.make_async_copy(low_f, fore_out, misc.at[15]), pltpu.make_async_copy(low_b, back_out, misc.at[16])]
    for cp in low_cp:
        cp.start()

    R = out[a].shape[1]
    pre_cp.wait()
    for half in range(2):
        @pl.loop(half * 3, half * 3 + 3)
        def _(j):
            cols = pl.ds(pl.multiple_of(j * 512, 128), 512)
            pf[:, cols] = jnp.dot(low_f[...], wa[:, cols], preferred_element_type=jnp.float32)

        comm()
    state["free"] = True
    complete("back")
    for half in range(2):
        @pl.loop(half * 3, half * 3 + 3)
        def _(j):
            cols = pl.ds(pl.multiple_of(j * 512, 128), 512)
            pk[:, cols] = jnp.dot(low_b[...], wb[:, cols], preferred_element_type=jnp.float32)

        comm()
    a = complete("value")
    for half in range(2):
        @pl.loop(half * 3, half * 3 + 3)
        def _(j):
            cols = pl.ds(pl.multiple_of(j * 512, 128), 512)
            pv[:, cols] = jnp.dot(nl[...], wa[:768, cols], preferred_element_type=jnp.float32)

        comm()

    complete("out")
    dests = (hid_out, gpf_out, gpb_out, gpv_out)

    def ring_cp(j, w):
        cols = pl.ds(pl.multiple_of(j * 256, 128), 256)
        return pltpu.make_async_copy(ring.at[lax.rem(j, 2), w], dests[w].at[:, cols], rsem.at[lax.rem(j, 2), w])

    @pl.loop(0, 12)
    def _(j):
        cols = pl.ds(pl.multiple_of(j * 256, 128), 256)
        slot = lax.rem(j, 2)

        @pl.when(j >= 2)
        def _():
            for w in range(4):
                ring_cp(j - 2, w).wait()

        out_rows = pl.ds(pl.multiple_of(768 + lax.rem(j, 3) * 256, 16), 256)
        out_cols = pl.ds(pl.multiple_of(lax.div(j, 3) * 768, 128), 768)
        h = dot(cot[...], wa[out_rows, out_cols], 1, 1)
        pb = pk[:, cols]
        p = pf[:, cols]
        va, dva = gelu_parts(pv[:, cols])
        hv = h * va
        ring[slot, 0] = (p * pb * va).astype(jnp.bfloat16)
        ring[slot, 1] = (hv * pb).astype(jnp.bfloat16)
        ring[slot, 2] = (hv * p).astype(jnp.bfloat16)
        ring[slot, 3] = (h * p * pb * dva).astype(jnp.bfloat16)
        for w in range(4):
            ring_cp(j, w).start()

    for j in (10, 11):
        for w in range(4):
            ring_cp(j, w).wait()

    nout.wait()
    fb_cp.wait()
    for cp in low_cp:
        cp.wait()
    for cp, sends, recvs in hcps.values():
        pl.when(sends)(cp.wait_send)
    for u in units:
        def left():
            for d in (xc, yc, fx, fy, sb):
                if u in d:
                    d[u].wait_send()

        when(here(u), left)
    for (a, way, j), cp in zsend.items():
        gone = here((a, way, j))
        more = onward(way)
        when(more if gone is True else gone & more, cp.wait_send)
    for cp in own_sib.values():
        cp.wait_send()


def gather_forward(mask, tokens, cot, shards):
    rows, width = tokens.shape
    n = len(FETCH)
    D = pltpu.SemaphoreType.DMA
    V = lambda sh, t=jnp.bfloat16: pltpu.VMEM(sh, t)
    full = []
    for m in FETCH:
        R, C = shards[m].shape
        full.append(jax.ShapeDtypeStruct((8, R * (4 if m == "kern" else 1), C), jnp.bfloat16))
    FH, FFN = shards["filter"].shape[1], shards["value"].shape[1]
    f32 = jnp.float32
    S = lambda sh, t=jnp.bfloat16: jax.ShapeDtypeStruct(sh, t)
    extra = [S((rows, FH), f32), S((2, 1024, FH)), S((rows, FH)), S((rows, FH))] + [S((rows, FFN))] * 4 + [S((rows, width))]
    any_ = pl.BlockSpec(memory_space=pl.ANY)
    wave = jnp.asarray(wave_tables(), jnp.bfloat16)
    outs = pl.pallas_call(
        functools.partial(forward_kernel, width),
        out_shape=full + extra,
        in_specs=[pl.BlockSpec(memory_space=pltpu.SMEM)] + [any_] * (3 + n),
        out_specs=[any_] * (n + len(extra)),
        scratch_shapes=[V(shards[m].shape) for m in SMALL]
        + [V(wave.shape), V((rows, width)), V((rows, width)), V((8, 16, 128)), V((16, width), f32), V((rows, width))]
        + [V((FH, FFN)), V((FH, FFN)), V((rows, FFN), f32), V((rows, FFN), f32), V((rows, FFN), f32)]
        + [V((2, 1024, FH)), V((rows, FH)), V((rows, FH)), V((2, 384, 512)), V((2, 384, 512))]
        + [V((2, 4, 256, 384), f32), V((8, 256, 384), f32), V((2, 2, 256, 384)), V((2, 4, rows, 256))]
        + [D((n,)), D((n,)), D((n, 7, 2)), D((n, 6)), D((n, 6))]
        + [D((n, 7))] * 10
        + [D((n,)), D((n,)), D((4, 4)), D((4, 4)), D((17,)), D((2, 4))],
        compiler_params=pltpu.CompilerParams(collective_id=0, has_side_effects=True, vmem_limit_bytes=int(63.5 * 2**20)),
        cost_estimate=pl.CostEstimate(flops=20 * 10**9, bytes_accessed=2 * 10**8, transcendentals=0),
    )(mask, wave, tokens, cot, *[shards[m] for m in FETCH])
    return dict(zip(FETCH, outs[:n])), outs[n:]


L1, L2, L3, L4 = 0, 2, 5, 7


FIRST_Z = ()
ORDER = ("out", "fore", "back", "value", "kern", "filter")
DEPTH = 3


def add_into(dst, srcs):
    R = dst.shape[-2]

    @pl.loop(0, R // 16)
    def _(r):
        rows = pl.ds(pl.multiple_of(r * 16, 16), 16)
        t = dst[rows, :].astype(jnp.float32)
        for s_ in srcs:
            t = t + s_[rows, :].astype(jnp.float32)
        dst[rows, :] = t.astype(dst.dtype)


def grad_kernel(acts, rights, *refs):
    refs = list(refs)
    take = lambda n: [refs.pop(0) for _ in range(n)]
    act_in = dict(zip(acts, take(len(acts))))
    right_in = dict(zip(rights, take(len(rights))))
    kern_in, norm_in = take(2)
    out = dict(zip(ORDER, take(len(ORDER))))
    norm_out, = take(1)
    act = dict(zip(acts, take(len(acts))))
    right = dict(zip(rights, take(len(rights))))
    P = dict(zip(ORDER, take(len(ORDER))))
    bx = dict(zip(ORDER, take(len(ORDER))))
    by = dict(zip(ORDER, take(len(ORDER))))
    bc = dict(zip(ORDER, take(len(ORDER))))
    snd, snd2, stg, nbuf = take(4)
    isem, ksem, as_, ar, xs, xr, ys, yr, cs, cr, gxs, gxr, gys, gyr, hxs, hxr, hys, hyr, osem, ns, nr = refs
    dp, s, z, c = place(4)
    core = (dp, s + 1 - 2 * c)
    xn = (dp + 1 - 2 * lax.rem(dp, 2), s)
    yn = (lax.rem(dp + 2, 4), s)
    q = dp
    qx = xn[0]
    qy = yn[0]
    qd = lax.rem(qx + 2, 4)

    def zdev(k):
        return (dp, lax.rem(s + 2 * k, 8))

    loads = {}
    for i, m in enumerate(acts):
        loads["a", m] = pltpu.make_async_copy(act_in[m], act[m], isem.at[i])
    for i, m in enumerate(rights):
        loads["r", m] = pltpu.make_async_copy(right_in[m], right[m], isem.at[len(acts) + i])
    for m in ORDER:
        for kind, group in (("a", acts), ("r", rights)):
            if m in group:
                loads[kind, m].start()
    kload = pltpu.make_async_copy(kern_in, stg, ksem)
    kload.start()
    bar = pltpu.get_barrier_semaphore()
    for d in [core, xn, yn] + [zdev(k) for k in (1, 2, 3)]:
        pl.semaphore_signal(bar, inc=1, device_id=d, device_id_type=MESH)
    pl.semaphore_wait(bar, 6)

    def rc(a_ref, b_ref, s1, s2, dev):
        return pltpu.make_async_remote_copy(src_ref=a_ref, dst_ref=b_ref, send_sem=s1, recv_sem=s2, device_id=dev, device_id_type=MESH)

    g = GEOM
    units = [(m, k) for m in FIRST_Z for k in (1, 2, 3)]
    for m in ORDER:
        if m == ORDER[-2]:
            units += [(w, 0) for w in FIRST_Z]
        if m not in FIRST_Z:
            units += [(m, k) for k in (1, 2, 3, 0)]
    at = {m: j for j, m in enumerate(ORDER)}
    A, X, Y, C, waited, left_behind = {}, {}, {}, {}, set(), set()

    def ready(kind, m):
        if (kind, m) not in waited:
            waited.add((kind, m))
            loads[kind, m].wait()

    def so(k, other):
        base = lax.rem(s + 2 * k, 8)
        return base + 1 - 2 * c if other else base

    def product(m, shard, put):
        R, cols = P[m].shape[-2:]
        step = 768 if R <= 192 else 384
        left = act[m].at[shard]

        @pl.loop(0, cols // step)
        def _(j):
            at_cols = pl.ds(pl.multiple_of(j * step, 128), step)
            put(at_cols, jnp.dot(left[...], right[m][:, at_cols], preferred_element_type=jnp.float32))

    def stA(i):
        m, k = units[i]
        j = at[m]
        if m == "kern":
            if k == 1:
                kload.wait()
            A[i] = rc(stg.at[so(k, True)], P[m].at[k], as_.at[j, k], ar.at[j, k], core)
        else:
            ready("a", m)
            ready("r", m)
            back = [u for u in range(i) if units[u][0] != "kern" and (units[u][0] in FIRST_Z) == (m in FIRST_Z)]
            if len(back) >= DEPTH:
                A[back[-DEPTH]].wait_send()
                left_behind.discard(back[-DEPTH])
            slot = len(back) % DEPTH
            R, cols = P[m].shape[-2:]
            buf = (snd2 if m in FIRST_Z else snd).at[slot, pl.ds(0, R), pl.ds(0, cols)]

            def put(cs_, t):
                buf[:, cs_] = t.astype(jnp.bfloat16)

            product(m, so(k, True), put)
            A[i] = rc(buf, P[m].at[k], as_.at[j, k], ar.at[j, k], core)
        left_behind.add(i)
        A[i].start()

    def stB(i):
        m, k = units[i]
        j = at[m]
        A[i].wait_recv()
        p = P[m].at[k]
        if m == "kern":
            add_into(p, [stg.at[so(k, False)]])
        else:
            def put(cs_, t):
                p[:, cs_] = (p[:, cs_].astype(jnp.float32) + t).astype(jnp.bfloat16)

            product(m, so(k, False), put)
        if m in FIRST_Z:
            if k:
                C[i] = rc(p, bc[m].at[k - 1], cs.at[j, k - 1], cr.at[j, k - 1], zdev(k))
                C[i].start()
                return
            for w in (1, 2, 3):
                C[units.index((m, w))].wait_recv()
            add_into(p, [bc[m].at[w] for w in range(3)])
        X[i, 1] = rc(cut(p, g[m], qd, 0), bx[m].at[k, 1], xs.at[j, k, 1], xr.at[j, k, 1], xn)
        X[i, 0] = rc(cut(p, g[m], qx, 0), bx[m].at[k, 0], xs.at[j, k, 0], xr.at[j, k, 0], xn)
        Y[i, 1] = rc(cut(p, g[m], qd, 1), by[m].at[k, 1], ys.at[j, k, 1], yr.at[j, k, 1], yn)
        Y[i, 0] = rc(cut(p, g[m], qy, 1), by[m].at[k, 0], ys.at[j, k, 0], yr.at[j, k, 0], yn)
        for w in (1, 0):
            X[i, w].start()
            Y[i, w].start()

    def stC(i):
        m, k = units[i]
        if m in FIRST_Z and k:
            return
        j = at[m]
        p = P[m].at[k]
        X[i, 1].wait_recv()
        add_into(cut(p, g[m], qy, 0), [bx[m].at[k, 1]])
        Y[i, 2] = rc(cut(p, g[m], qy, 0), by[m].at[k, 2], ys.at[j, k, 2], yr.at[j, k, 2], yn)
        Y[i, 2].start()
        Y[i, 1].wait_recv()
        add_into(cut(p, g[m], qx, 1), [by[m].at[k, 1]])
        X[i, 2] = rc(cut(p, g[m], qx, 1), bx[m].at[k, 2], xs.at[j, k, 2], xr.at[j, k, 2], xn)
        X[i, 2].start()

    def stD(i):
        m, k = units[i]
        if m in FIRST_Z and k:
            return
        j = at[m]
        p = P[m].at[k]
        X[i, 0].wait_recv()
        Y[i, 2].wait_recv()
        add_into(cut(p, g[m], q, 0), [bx[m].at[k, 0], by[m].at[k, 2]])
        Y[i, 0].wait_recv()
        X[i, 2].wait_recv()
        add_into(cut(p, g[m], q, 1), [by[m].at[k, 0], bx[m].at[k, 2]])
        if k:
            C[i] = rc(cut(p, g[m], q), bc[m].at[k - 1], cs.at[j, k - 1], cr.at[j, k - 1], zdev(k))
            C[i].start()

    ag = {}

    def stE(m):
        j = at[m]
        p = cut(P[m].at[0], g[m], q)
        if m not in FIRST_Z:
            for k in (1, 2, 3):
                C[units.index((m, k))].wait_recv()
            add_into(p, [bc[m].at[w] for w in range(3)])
        own = out[m] if m == "kern" else cut(out[m], g[m], q)
        ag[m, "o"] = pltpu.make_async_copy(p, own, osem.at[j])
        ag[m, "o"].start()
        if m != "kern":
            ag[m, "x"] = rc(p, own, gxs.at[j], gxr.at[j], xn)
            ag[m, "y"] = rc(p, own, gys.at[j], gyr.at[j], yn)
            ag[m, "x"].start()
            ag[m, "y"].start()

    def stF(m):
        if m == "kern":
            return
        j = at[m]
        ag[m, "x"].wait_recv()
        b = cut(out[m], g[m], qx, 0)
        ag[m, "fy"] = rc(b, b, hys.at[j], hyr.at[j], yn)
        ag[m, "fy"].start()
        ag[m, "y"].wait_recv()
        b = cut(out[m], g[m], qy, 1)
        ag[m, "fx"] = rc(b, b, hxs.at[j], hxr.at[j], xn)
        ag[m, "fx"].start()

    nload = pltpu.make_async_copy(norm_in, nbuf.at[0], ns.at[6])
    nload.start()
    N = {}

    def norm_step(w):
        if w == 0:
            nload.wait()
            N[0] = rc(nbuf.at[0], nbuf.at[1], ns.at[0], nr.at[0], core)
            N[0].start()
        elif w in (1, 2):
            N[w - 1].wait()
            nbuf[0] = nbuf[0] + nbuf[w]
            N[w] = rc(nbuf.at[0], nbuf.at[w + 1], ns.at[w], nr.at[w], xn if w == 1 else yn)
            N[w].start()
        elif w == 3:
            N[2].wait()
            nbuf[0] = nbuf[0] + nbuf[3]
            for k in (1, 2, 3):
                N[2 + k] = rc(nbuf.at[0, so(k, False)], nbuf.at[4, k], ns.at[2 + k], nr.at[2 + k], zdev(k))
                N[2 + k].start()
        elif w == 4:
            for k in (1, 2, 3):
                N[2 + k].wait()
            nbuf[4, 0] = nbuf[0, s] + nbuf[4, 1] + nbuf[4, 2] + nbuf[4, 3]
            N[6] = pltpu.make_async_copy(nbuf.at[4, 0], norm_out, ns.at[7])
            N[6].start()

    n = len(units)
    ahead = DEPTH - 1
    for i in range(ahead):
        stA(i)
    for t in range(n + LE + 6):
        if t < n:
            if t + ahead < n:
                stA(t + ahead)
            stB(t)
        if 0 <= t - LC < n:
            stC(t - LC)
        if 0 <= t - LD < n:
            stD(t - LD)
        for j in range(n):
            m, k = units[j]
            wait = LATE if m in ORDER[1:-2] and m not in FIRST_Z else LE
            if k == 0 and t == j + wait:
                stE(m)
            if k == 0 and t == j + wait + 2:
                stF(m)
        if t >= 4 and t % 2 == 0 and t // 2 - 2 < 5:
            norm_step(t // 2 - 2)
    for m in ORDER:
        if m != "kern":
            for w in ("fx", "fy"):
                ag[m, w].wait()
            for w in ("x", "y"):
                ag[m, w].wait_send()
        ag[m, "o"].wait()
    N[6].wait()
    for i in sorted(left_behind):
        A[i].wait_send()
    for d in (X, Y, C):
        for v in d.values():
            v.wait_send()


LC, LD, LE, LATE = 1, 2, 3, 6


def half_shape(m, R, C):
    return (R // 2, C // 4) if GEOM[m] == "col" else (R // 8, C)


def quarter_shape(m, R, C):
    return (R, C // 4) if GEOM[m] == "col" else (R // 4, C)


def reduce_gradients(act, right, kern, norm):
    D = pltpu.SemaphoreType.DMA
    V = lambda sh: pltpu.VMEM(sh, jnp.bfloat16)
    shp = {m: kern.shape[1:] if m == "kern" else (act[m].shape[1], right[m].shape[1]) for m in ORDER}
    n = len(ORDER)
    acts, rights = tuple(act), tuple(right)
    any_ = pl.BlockSpec(memory_space=pl.ANY)
    snd = max(shp[m][0] for m in acts if m not in FIRST_Z), max(shp[m][1] for m in acts if m not in FIRST_Z)
    snd2 = (16, 128)
    outs = pl.pallas_call(
        functools.partial(grad_kernel, acts, rights),
        out_shape=[jax.ShapeDtypeStruct(quarter_shape(m, *shp[m]) if m == "kern" else shp[m], jnp.bfloat16) for m in ORDER]
        + [jax.ShapeDtypeStruct(norm.shape[1:], jnp.float32)],
        in_specs=[any_] * (len(acts) + len(rights) + 2),
        out_specs=[any_] * (n + 1),
        scratch_shapes=[V(act[m].shape) for m in acts]
        + [V(right[m].shape) for m in rights]
        + [V((4,) + shp[m]) for m in ORDER]
        + [V((1 if m in FIRST_Z else 4, 3) + half_shape(m, *shp[m])) for m in ORDER] * 2
        + [V((3,) + (shp[m] if m in FIRST_Z else quarter_shape(m, *shp[m]))) for m in ORDER]
        + [V((DEPTH,) + snd), V((DEPTH,) + snd2), V(kern.shape), pltpu.VMEM((5,) + norm.shape, jnp.float32)]
        + [D((len(acts) + len(rights),)), D(()), D((n, 4)), D((n, 4))]
        + [D((n, 4, 3))] * 4
        + [D((n, 3))] * 2
        + [D((n,))] * 9
        + [D((8,))] * 2,
        compiler_params=pltpu.CompilerParams(collective_id=1, has_side_effects=True, vmem_limit_bytes=63 * 2**20),
        cost_estimate=pl.CostEstimate(flops=16 * 10**9, bytes_accessed=10**8, transcendentals=0),
    )(*[act[m] for m in acts], *[right[m] for m in rights], kern, norm)
    return dict(zip(ORDER, outs[:-1])), outs[-1]


STEP_A = 32


def mode_powers(rate, freq):
    coarse = (jnp.arange(LONG // STEP_A) * STEP_A).astype(F32)
    fine = jnp.arange(STEP_A).astype(F32)

    def powers(lags):
        size = jnp.exp(-rate[:, None, :] * lags[None, :, None])
        turn = freq[:, None, :] * lags[None, :, None]
        return size * jnp.cos(turn), size * jnp.sin(turn)

    return powers(coarse), powers(fine)


def make_kernels(coef, rate, powers):
    (ar, ai), (br, bi) = powers
    weight = (coef * jnp.sqrt(rate))[:, None, :]
    left = jnp.concatenate([weight * ar, -weight * ai], -1)
    right = jnp.concatenate([br, bi], -1)
    rows = jnp.einsum("ran,rbn->rab", left, right, precision=HIGHEST, preferred_element_type=F32)
    return rows.reshape(rows.shape[0], LONG)


def pull_kernels(grad, coef, rate, powers):
    (ar, ai), (br, bi) = powers
    rows = grad.reshape(grad.shape[0], LONG // STEP_A, STEP_A)
    lags = jnp.arange(LONG).astype(F32).reshape(LONG // STEP_A, STEP_A)
    both = jnp.concatenate([rows, rows * lags[None]], 1)
    fine = jnp.concatenate([br, bi], -1)
    inner = jnp.einsum("rab,rbn->ran", both, fine, precision=HIGHEST, preferred_element_type=F32)
    n = rate.shape[-1]
    a = LONG // STEP_A
    zero_r, zero_i = inner[:, :a, :n], inner[:, :a, n:]
    one_r, one_i = inner[:, a:, :n], inner[:, a:, n:]
    plain = jnp.sum(ar * zero_r - ai * zero_i, 1)
    lag_r = jnp.sum(ar * one_r - ai * one_i, 1)
    lag_i = jnp.sum(ar * one_i + ai * one_r, 1)
    root = jnp.sqrt(rate)
    return root * plain, coef * (plain / (2 * root) - root * lag_r), -coef * root * lag_i


def dot_plain(left_side, right_side):
    return jnp.dot(left_side, right_side, preferred_element_type=F32)


def dot_inner(left_side, right_side):
    return lax.dot_general(left_side, right_side, (((0,), (0,)), ((), ())), preferred_element_type=F32)


def dot_outer(left_side, right_side):
    return lax.dot_general(left_side, right_side, (((1,), (1,)), ((), ())), preferred_element_type=F32)


def layer_norm(rows, gain, bias):
    centre = jnp.mean(rows, axis=-1, keepdims=True)
    shifted = rows - centre
    spread = jnp.mean(shifted * shifted, axis=-1, keepdims=True)
    return shifted * lax.rsqrt(spread + EPSILON) * gain + bias


def shift(array, by, count):
    pairs = [(i, i + by) for i in range(count) if 0 <= i + by < count]
    return lax.ppermute(array, "seq", pairs)


def from_left(array, count):
    return [shift(array[:, BLK:], 2, count), shift(array, 1, count)]


def from_right(array, count):
    return [shift(array, -1, count), shift(array[:, :BLK], -2, count)]


def same_item(lengths, own_blocks, count):
    slots = jnp.arange(lengths.shape[1])
    starts = jnp.sum(jnp.where(slots[None, :] < slots[:, None], lengths[:, None, :], 0), -1)
    total = own_blocks * count
    places = jnp.arange(total) * BLK
    present = (starts[:, None, :] <= places[None, :, None]) & (lengths[:, None, :] > 0)
    owner = jnp.sum(present.astype(jnp.int32), -1)
    first = lax.axis_index("seq") * own_blocks
    padded = jnp.pad(owner, ((0, 0), (REACH, REACH)), constant_values=-1)
    near = lax.dynamic_slice_in_dim(padded, first, own_blocks + 2 * REACH, 1)
    return jnp.stack(
        [
            jnp.stack([(near[:, o + REACH] == near[:, o + REACH + e]) for e in range(-REACH, REACH + 1)], -1)
            for o in range(own_blocks)
        ],
        1,
    ).astype(F32)


def shards(
    n_dp,
    n_seq,
    tokens,
    cotangent,
    lengths,
    ln_gain,
    ln_bias,
    w_value,
    w_filter,
    w_fore,
    w_back,
    w_out,
    ssm_coef,
    ssm_rate,
    ssm_freq,
):
    linked = n_dp == 4 and n_seq == 8
    micros, rows_each, width = tokens.shape
    rows = micros * rows_each
    channels = ssm_coef.shape[1]
    modes = ssm_coef.shape[2]
    parts = 4 if linked else 1
    some = channels // parts
    first = lax.axis_index("dp") * some if linked else 0

    def mine(array):
        return lax.dynamic_slice_in_dim(array, first, some, 1).reshape(2 * some, modes)

    coef, rate, freq = mine(ssm_coef), mine(ssm_rate), mine(ssm_freq)
    powers = lax.optimization_barrier(mode_powers(rate, freq))
    kernels = make_kernels(coef, rate, powers).astype(LOW)
    mask = same_item(lengths[:, 0], rows_each // BLK, n_seq).reshape(-1)
    wave = jnp.asarray(wave_tables(), LOW)
    tile_step = max(1, 384 // channels)
    cot_rows = cotangent.reshape(rows, width)
    token_rows = tokens.reshape(rows, width).astype(F32)
    if linked:
        pack = jnp.pad(jnp.stack([ln_gain, ln_bias]), ((0, 14), (0, 128 - ln_gain.shape[0])))
        own = {"norm": pack, "filter": w_filter, "kern": kernels, "value": w_value, "fore": w_fore, "back": w_back, "out": w_out}
        gathered, made = gather_forward(mask, tokens.reshape(rows, width), cot_rows, own)
        pre_filter, filter_near, fore_low, back_low, hidden_low, grad_proj_fore, grad_proj_back, grad_pre_value, normed_low = made
        kern = gathered.pop("kern").reshape(n_seq, parts, 2, some, LONG)
        norm = gathered.pop("norm")[:, :2, : ln_gain.shape[0]].astype(F32)
        gain, bias = norm[:, 0].reshape(-1), norm[:, 1].reshape(-1)
        full = {m: a.reshape(-1, a.shape[-1]) for m, a in gathered.items()}
        around = [filter_near]
    else:
        own = {"filter": w_filter, "value": w_value, "fore": w_fore, "back": w_back, "out": w_out}
        full = {m: lax.all_gather(a, "seq", axis=0, tiled=True) for m, a in own.items()}
        kern = lax.all_gather(kernels.reshape(1, 2, some, LONG), "seq", axis=0)
        gain = lax.all_gather(ln_gain, "seq", axis=0, tiled=True).astype(F32)
        bias = lax.all_gather(ln_bias, "seq", axis=0, tiled=True).astype(F32)
        normed_low = layer_norm(token_rows, gain, bias).astype(LOW)
        pre_filter = dot_plain(normed_low, full["filter"])
        filter_low = jax.nn.gelu(pre_filter).astype(LOW).reshape(micros, rows_each, -1)
        around = from_left(filter_low, n_seq) + [filter_low] + from_right(filter_low, n_seq)
        pre_value = dot_plain(normed_low, full["value"])
        value_act, value_pull = jax.vjp(jax.nn.gelu, pre_value)
        fore_low, back_low = [a.reshape(rows, -1) for a in conv_forward(mask, wave, kern, around, tile_step)]
        proj_fore = dot_plain(fore_low, full["fore"])
        proj_back = dot_plain(back_low, full["back"])
        hidden_low = (proj_fore * proj_back * value_act).astype(LOW)
        grad_hidden = dot_outer(cot_rows, full["out"])
        grad_proj_fore = (grad_hidden * proj_back * value_act).astype(LOW)
        grad_proj_back = (grad_hidden * proj_fore * value_act).astype(LOW)
        grad_pre_value = value_pull(grad_hidden * proj_fore * proj_back)[0].astype(LOW)
    filter_pull = jax.vjp(jax.nn.gelu, pre_filter)[1]
    norm_pull = jax.vjp(layer_norm, token_rows, gain, bias)[1]
    mixed = (token_rows + dot_plain(hidden_low, full["out"])).astype(LOW).reshape(tokens.shape)

    grad_fore_low = dot_outer(grad_proj_fore, full["fore"]).astype(LOW).reshape(micros, rows_each, -1)
    grad_back_low = dot_outer(grad_proj_back, full["back"]).astype(LOW).reshape(micros, rows_each, -1)
    fore_around = [grad_fore_low] + from_right(grad_fore_low, n_seq)
    back_around = from_left(grad_back_low, n_seq) + [grad_back_low]
    grad_filter_low, grad_kern = conv_backward(mask, wave, kern, around, fore_around, back_around, tile_step)
    grad_pre_filter = filter_pull(grad_filter_low.reshape(rows, -1).astype(F32))[0].astype(LOW)
    grad_normed = dot_outer(grad_pre_value, full["value"]) + dot_outer(grad_pre_filter, full["filter"])
    grad_rows, gain_grad, bias_grad = norm_pull(grad_normed)
    grad_tokens = (cot_rows.astype(F32) + grad_rows).astype(LOW).reshape(tokens.shape)

    left = {"out": hidden_low, "fore": fore_low, "back": back_low, "value": normed_low, "filter": normed_low}
    right = {"out": cot_rows, "fore": grad_proj_fore, "back": grad_proj_back, "value": grad_pre_value, "filter": grad_pre_filter}
    grad_kern = grad_kern.reshape(n_seq, -1, LONG)
    norm_grads = jnp.stack([gain_grad, bias_grad]).reshape(2, n_seq, -1)
    if linked:
        pack = jnp.pad(jnp.swapaxes(norm_grads, 0, 1), ((0, 0), (0, 6), (0, 128 - norm_grads.shape[2])))
        left = {m: jnp.transpose(a).reshape(n_seq, -1, rows) for m, a in left.items()}
        sums, norm_grads = reduce_gradients(left, right, grad_kern, pack)
        norm_grads = norm_grads[:2, : ln_gain.shape[0]]
    else:
        grads = {m: dot_inner(left[m], right[m]).reshape(n_seq, -1, right[m].shape[1]) for m in left}
        grads["kern"] = grad_kern.astype(F32)
        sums = {m: lax.psum_scatter(a, "seq", scatter_dimension=0, tiled=False) for m, a in grads.items()}
        sums = {m: lax.psum(a, "dp") for m, a in sums.items()}
        norm_grads = lax.psum_scatter(norm_grads, "seq", scatter_dimension=1, tiled=False)
        norm_grads = lax.psum(norm_grads, "dp")
    modes_grad = jnp.stack(pull_kernels(sums["kern"].astype(F32), coef, rate, powers)).reshape(3, 2, some, modes)
    if linked:
        modes_grad, sums = lax.optimization_barrier((modes_grad, sums))
        sums = {m: a.astype(F32) for m, a in sums.items()}
        column = lax.axis_index("dp")
        hand = [modes_grad] + [lax.ppermute(modes_grad, "dp", [(i, i ^ w) for i in range(n_dp)]) for w in (1, 2, 3)]
        odd, high = column % 2 == 1, column >= 2
        hand = [jnp.where(odd, hand[w ^ 1], hand[w]) for w in range(4)]
        hand = [jnp.where(high, hand[w ^ 2], hand[w]) for w in range(4)]
        modes_grad = jnp.concatenate(hand, 2)
    return (
        mixed,
        grad_tokens,
        norm_grads[0],
        norm_grads[1],
        sums["value"],
        sums["filter"],
        sums["fore"],
        sums["back"],
        sums["out"],
        modes_grad[0],
        modes_grad[1],
        modes_grad[2],
    )


def solution(mesh):
    rows = P("seq", None)
    modes = P(None, "seq", None)
    tokens = P(None, ("dp", "seq"), None)
    return jax.shard_map(
        functools.partial(shards, mesh.shape["dp"], mesh.shape["seq"]),
        mesh=mesh,
        in_specs=(tokens, tokens, P(None, "dp", None), P("seq"), P("seq")) + (rows,) * 5 + (modes,) * 3,
        out_specs=(tokens, tokens, P("seq"), P("seq")) + (rows,) * 5 + (modes,) * 3,
        check_vma=False,
    )
```
